32 devices in a mesh: hier: 8 (over z, x), row: 4 (over y, core).
Axes of the slice: x: 2, y: 2, z: 4, core: 2. Of those that a mesh axis runs over, the one named last changes fastest.
Arguments:
- state: bfloat16 [24, 2, 1024, 1024], P('hier', None, 'row'), may hold values from -6 to 6
- prev_slope: float32 [24, 2, 1024, 1024], P('hier', None, 'row'), may hold values from -6 to 6
- accumulated: float32 [24, 2, 1024, 1024], P('hier', None, 'row'), may hold values from -6 to 6
- hamiltonian: bfloat16 [2, 1024, 1024], P(None, 'row'), as said below
- couple_v: float32 [6, 1024], replicated, may hold values from -4 to 4
- coupling: float32 [2, 6], replicated, may hold values from 0.2 to 1
- damping: float32 [6], replicated, may hold values from 0.2 to 2
- occupation: int32 [24, 6], P('hier'), may hold values from 0 to 2, as said below
- parents: int32 [24, 6], P('hier'), may hold values from -1 to 23, as said below
- children: int32 [24, 6], P('hier'), may hold values from -1 to 22, as said below
Outputs:
- slope: float32 [24, 2, 1024, 1024], P('hier', None, 'row')
- accumulated_out: float32 [24, 2, 1024, 1024], P('hier', None, 'row')
The draws below stay inside these ranges and needn't reach their ends.
Inputs may be any that keep to these rules, and one draw needn't show every extreme that they name: `occupation`: row s is the index of the operator in slot s. The rows are the 24 indices of smallest total among all indices of 6 entries with total at most 4, taken by total and then lexicographically; the all-zero index stands in the last slot, the others in a slot order drawn from the seed; the set is closed under lowering one entry. `parents`: entry (s, k) is the slot whose index equals slot s's index with entry k lowered by one, or -1 where entry k of slot s is 0. `children`: entry (s, k) is the slot whose index equals slot s's index with entry k raised by one, or -1 where that index is not among the 24. `hamiltonian`: Hermitian: the real part is symmetric, the imaginary part antisymmetric.
All inputs are finite; a program needn't handle non-finite values.
Results may differ from the reference program's by a relative error of at most 0.0029.
Values may be sent and summed in bfloat16 or wider, within the bound.
No kernel may reach another device: no remote copies, remote signals or barrier semaphores. Data moves between devices by JAX's collectives and lax.ppermute only.
A program may use at most 320 MiB of HBM per device.

```python
import math
import jax
import jax.numpy as jnp
import numpy as np
from jax import lax

N = 1024
MODES = 6
ADOS = 24


def window_table():
    entries = [()]
    for mode in range(MODES):
        entries = [entry + (level,) for entry in entries for level in range(5)]
    chosen = [entry for entry in entries if sum(entry) <= 4]
    chosen = sorted(chosen, key=lambda entry: (sum(entry), entry))[:ADOS]
    lookup = {entry: place for place, entry in enumerate(chosen)}
    upward = np.full((ADOS, MODES), -1, np.int32)
    downward = np.full((ADOS, MODES), -1, np.int32)
    for place, entry in enumerate(chosen):
        for mode in range(MODES):
            raised = list(entry)
            raised[mode] = raised[mode] + 1
            upward[place, mode] = lookup.get(tuple(raised), -1)
            if entry[mode] > 0:
                lowered = list(entry)
                lowered[mode] = lowered[mode] - 1
                downward[place, mode] = lookup[tuple(lowered)]
    return (np.array(chosen, np.int32), upward, downward)


def hierarchy_draw(key):
    table, upward, downward = window_table()
    others = jax.random.permutation(jax.random.fold_in(key, 11), ADOS - 1).astype(jnp.int32)
    order = jnp.concatenate([jnp.array([ADOS - 1], jnp.int32), others])
    inverse = jnp.argsort(order)
    up_slots = jnp.where(upward >= 0, order[np.maximum(upward, 0)], -1).astype(jnp.int32)
    down_slots = jnp.where(downward >= 0, order[np.maximum(downward, 0)], -1).astype(jnp.int32)
    return (jnp.asarray(table)[inverse], down_slots[inverse], up_slots[inverse])


def draw_occupation(key, part):
    return hierarchy_draw(key)[0]


def draw_parents(key, part):
    return hierarchy_draw(key)[1]


def draw_children(key, part):
    return hierarchy_draw(key)[2]


def draw_hamiltonian(key, part):
    first_key, second_key = jax.random.split(jax.random.fold_in(key, 5))
    first = jax.random.normal(first_key, (N, N), jnp.float32)
    second = jax.random.normal(second_key, (N, N), jnp.float32)
    factor = (2.0 * N) ** (-0.5)
    real_part = (first + first.T) * factor
    imag_part = (second - second.T) * factor
    return jnp.stack([real_part, imag_part]).astype(jnp.bfloat16)


def block_levels(key, extent, shards, least, high):
    gain, own = 1.0, jax.random.fold_in(key, 6)
    for position, shards_of in shards:
        draws = jnp.exp(jax.random.uniform(jax.random.fold_in(own, position), (shards_of,), jnp.float32, least / len(shards), high / len(shards)))
        gain = gain * jnp.repeat(draws, extent[position] // shards_of).reshape([-1 if axis == position else 1 for axis in range(len(extent))])
    return gain


def centred(own_key, shape, scale, bound, shards=(), held_as=jnp.bfloat16):
    gain = block_levels(own_key, shape, shards, -0.22, 0.18) if shards else 1.0
    result = jax.random.normal(own_key, shape, jnp.float32) * scale * gain
    return jnp.minimum(jnp.maximum(result, -bound), bound).astype(held_as)


def setup_inputs(seed: int = 0) -> dict:
    key_of = jax.random.split(jax.random.key(seed), 11)
    state = centred(key_of[0], (ADOS, 2, N, N), 1.0, 6.0, ((0, 8), (2, 4)))
    prev_slope = centred(key_of[1], (ADOS, 2, N, N), 1.0, 6.0, ((0, 8), (2, 4)), jnp.float32)
    accumulated = centred(key_of[2], (ADOS, 2, N, N), 1.0, 6.0, ((0, 8), (2, 4)), jnp.float32)
    hamiltonian = draw_hamiltonian(jax.random.fold_in(key_of[10], 71), 0)
    couple_v = centred(key_of[4], (MODES, N), 1.0, 4.0, (), jnp.float32)
    coupling = jnp.clip(jax.random.uniform(key_of[5], (2, MODES), jnp.float32, 0.2, 1.0), 0.2, 1.0)
    damping = jnp.clip(jnp.exp(jax.random.uniform(key_of[6], (MODES,), jnp.float32, math.log(0.2), math.log(2.0))), 0.2, 2.0)
    occupation = draw_occupation(jax.random.fold_in(key_of[10], 71), 0)
    parents = draw_parents(jax.random.fold_in(key_of[10], 71), 0)
    children = draw_children(jax.random.fold_in(key_of[10], 71), 0)
    return {"state": state, "prev_slope": prev_slope, "accumulated": accumulated, "hamiltonian": hamiltonian, "couple_v": couple_v, "coupling": coupling, "damping": damping, "occupation": occupation, "parents": parents, "children": children}


step_size = 0.5


def complex_dot(left, right):
    real_part = jnp.dot(left[0], right[0], preferred_element_type=jnp.float32) - jnp.dot(left[1], right[1], preferred_element_type=jnp.float32)
    imag_part = jnp.dot(left[0], right[1], preferred_element_type=jnp.float32) + jnp.dot(left[1], right[0], preferred_element_type=jnp.float32)
    return real_part, imag_part


def reference(state, prev_slope, accumulated, hamiltonian, couple_v, coupling, damping, occupation, parents, children):
    section = (state.astype(jnp.float32) + 0.5 * step_size * prev_slope).astype(jnp.bfloat16)

    def single(index):
        operator = section[index]
        left_real, left_imag = complex_dot(hamiltonian, operator)
        right_real, right_imag = complex_dot(operator, hamiltonian)
        wide = operator.astype(jnp.float32)
        counts = occupation[index].astype(jnp.float32)
        decay = jnp.sum(counts * damping)
        out_real = (left_imag - right_imag) - decay * wide[0]
        out_imag = -(left_real - right_real) - decay * wide[1]
        for mode in range(MODES):
            vrows = couple_v[mode][:, None]
            vcols = couple_v[mode][None, :]
            diff = vrows - vcols
            total = vrows + vcols
            child = children[index, mode]
            keep_up = (child >= 0).astype(jnp.float32)
            upper = section[jnp.maximum(child, 0)].astype(jnp.float32) * keep_up
            out_real = out_real + diff * upper[1]
            out_imag = out_imag - diff * upper[0]
            parent = parents[index, mode]
            keep_down = (parent >= 0).astype(jnp.float32)
            lower = section[jnp.maximum(parent, 0)].astype(jnp.float32) * (keep_down * counts[mode])
            g_real = coupling[0, mode] * diff
            g_imag = coupling[1, mode] * total
            prod_real = g_real * lower[0] - g_imag * lower[1]
            prod_imag = g_real * lower[1] + g_imag * lower[0]
            out_real = out_real + prod_imag
            out_imag = out_imag - prod_real
        return jnp.stack([out_real, out_imag])

    slope = lax.map(single, jnp.arange(ADOS, dtype=jnp.int32))
    return slope, accumulated + (step_size / 3.0) * slope
```

```python
import functools

import jax
import jax.numpy as jnp
import numpy as np
from jax import lax
from jax.experimental import pallas as pl
from jax.experimental.pallas import tpu as pltpu
from jax.sharding import PartitionSpec as P

step_size = 0.5
highest_total = 4
row_tile = 16
pieces = 2
MIB = 1024 * 1024
f32 = jnp.float32
bf16 = jnp.bfloat16


def index_rows(slots, modes):
    entries = [()]
    for _ in range(modes):
        entries = [
            entry + (level,)
            for entry in entries
            for level in range(highest_total + 1)
            if sum(entry) + level <= highest_total
        ]
    return sorted(entries, key=lambda entry: (sum(entry), entry))[:slots]


def coupled_to(rows):
    lookup = {entry: place for place, entry in enumerate(rows)}
    result = []
    for entry in rows:
        terms = []
        for mode, level in enumerate(entry):
            raised = entry[:mode] + (level + 1,) + entry[mode + 1 :]
            if raised in lookup:
                terms.append((lookup[raised], mode, True, 1))
            if level > 0:
                lowered = entry[:mode] + (level - 1,) + entry[mode + 1 :]
                terms.append((lookup[lowered], mode, False, level))
        result.append(terms)
    return result


def smaller_class(rows):
    classes = [[c for c, entry in enumerate(rows) if sum(entry) % 2 == rest] for rest in (0, 1)]
    return min(classes, key=len)


def params(megabytes):
    return pltpu.CompilerParams(vmem_limit_bytes=megabytes * MIB)


def whole():
    return pl.BlockSpec(memory_space=pltpu.VMEM)


def scalars():
    return pl.BlockSpec(memory_space=pltpu.SMEM)


def swap(array, axis, size, bit):
    return lax.ppermute(array, axis, [(i, i ^ bit) for i in range(size)])


def section_kernel(group, split, where, state, slope, section, *chunks):
    value = (state[...].astype(f32) + (0.5 * step_size) * slope[...]).astype(bf16)
    section[...] = value
    width = chunks[0].shape[-1]
    height = chunks[0].shape[-2]
    for b in range(group):
        columns = pl.ds(pl.multiple_of((where[0] ^ b) * width, 128), width)
        for p in range(split):
            chunks[b * split + p][...] = section[:, :, p * height : (p + 1) * height, columns]


def make_section(state, prev_slope, place, group, split):
    ops, parts, rows, columns = state.shape
    height, width = rows // split, columns // group
    block = pl.BlockSpec((1, 1, rows, columns), lambda a, x, _: (a, x, 0, 0))
    chunk = pl.BlockSpec((1, 1, height, width), lambda a, x, _: (a, x, 0, 0))
    count = group * split
    out = pl.pallas_call(
        functools.partial(section_kernel, group, split),
        grid_spec=pltpu.PrefetchScalarGridSpec(
            num_scalar_prefetch=1,
            grid=(ops, parts),
            in_specs=[block, block],
            out_specs=[block] + [chunk] * count,
        ),
        out_shape=[jax.ShapeDtypeStruct(state.shape, bf16)]
        + [jax.ShapeDtypeStruct((ops, parts, height, width), bf16)] * count,
        compiler_params=params(24),
        cost_estimate=pl.CostEstimate(
            flops=2 * state.size, bytes_accessed=10 * state.size, transcendentals=0
        ),
        name="section",
    )(place, state, prev_slope)
    return out[0], [[out[1 + b * split + p] for b in range(group)] for p in range(split)]


def fill_factors(vrows, vcols, coupling, factors):
    modes = vrows.shape[0]
    for k in range(modes):
        first = vrows[k]
        second = vcols[k : k + 1, :]
        diff = first - second
        factors[k] = diff
        factors[modes + k] = coupling[0, k] * diff
        factors[2 * modes + k] = coupling[1, k] * (first + second)


def add_terms(terms, places, held, factors, modes, rows, real, imag):
    for other, mode, child, count in terms:
        place = places[other]
        x_real = held[place, 0, rows, :].astype(f32)
        x_imag = held[place, 1, rows, :].astype(f32)
        if child:
            diff = factors[mode, rows, :]
            real = real + diff * x_imag
            imag = imag - diff * x_real
        else:
            first = factors[modes + mode, rows, :]
            second = factors[2 * modes + mode, rows, :]
            if count != 1:
                first, second = count * first, count * second
            real = real + (first * x_imag + second * x_real)
            imag = imag + (second * x_imag - first * x_real)
    return real, imag


def load_held(chunks, held):
    ops = chunks[0].shape[0]
    for b, chunk in enumerate(chunks):
        held[b * ops : (b + 1) * ops] = chunk[...]
    held[len(chunks) * ops] = jnp.zeros(held.shape[1:], bf16)


def partial_kernel(links, sides, group, places, coupling, vrows, vcols, *refs):
    chunks, out, held, factors = refs[:group], refs[group], refs[group + 1], refs[group + 2]
    modes = vrows.shape[0]
    height, width = held.shape[2:]
    empty = group * chunks[0].shape[0]
    fill_factors(vrows, vcols, coupling, factors)
    load_held(chunks, held)
    for u, c in enumerate(sides):

        @pl.when(places[c] < empty)
        def _():
            out[u] = held[places[c]]

        @pl.when(places[c] == empty)
        def _():
            @pl.loop(0, height // row_tile)
            def _(i):
                rows = pl.ds(pl.multiple_of(i * row_tile, row_tile), row_tile)
                zero = jnp.zeros((row_tile, width), f32)
                real, imag = add_terms(links[c], places, held, factors, modes, rows, zero, zero)
                out[u, 0, rows, :] = real.astype(bf16)
                out[u, 1, rows, :] = imag.astype(bf16)


def coupled_kernel(links, sides, group, places, coupling, vrows, vcols, *refs):
    chunks, received, outs = refs[:group], refs[group], refs[group + 1 : 2 * group + 1]
    held, done, factors, spots = refs[2 * group + 1 :]
    modes = vrows.shape[0]
    height, width = held.shape[2:]
    ops = chunks[0].shape[0]
    empty = group * ops
    fill_factors(vrows, vcols, coupling, factors)
    load_held(chunks, held)
    held[empty + 1 :] = received[...]
    for c in range(len(links)):
        spots[c] = places[c]
    for u, c in enumerate(sides):
        spots[c] = jnp.where(places[c] == empty, empty + 1 + u, places[c])
    for c in range(len(links)):

        @pl.when(places[c] < empty)
        def _():
            @pl.loop(0, height // row_tile)
            def _(i):
                rows = pl.ds(pl.multiple_of(i * row_tile, row_tile), row_tile)
                if c in sides:
                    u = empty + 1 + sides.index(c)
                    real, imag = held[u, 0, rows, :].astype(f32), held[u, 1, rows, :].astype(f32)
                else:
                    real = imag = jnp.zeros((row_tile, width), f32)
                real, imag = add_terms(links[c], spots, held, factors, modes, rows, real, imag)
                done[places[c], 0, rows, :] = real.astype(bf16)
                done[places[c], 1, rows, :] = imag.astype(bf16)

    for b, out in enumerate(outs):
        out[...] = done[b * ops : (b + 1) * ops]


def coupling_scratch(entries, height, width, modes):
    return [pltpu.VMEM((entries, 2, height, width), bf16)], [pltpu.VMEM((3 * modes, height, width), f32)]


def make_partial(chunks, places, coupling, vrows, vcols, links, sides):
    group = len(chunks)
    ops, _, height, width = chunks[0].shape
    held, factors = coupling_scratch(group * ops + 1, height, width, vrows.shape[0])
    size = height * width
    return pl.pallas_call(
        functools.partial(partial_kernel, links, sides, group),
        in_specs=[scalars(), scalars()] + [whole()] * (2 + group),
        out_specs=whole(),
        out_shape=jax.ShapeDtypeStruct((len(sides), 2, height, width), bf16),
        scratch_shapes=held + factors,
        compiler_params=params(32),
        cost_estimate=pl.CostEstimate(
            flops=40 * len(sides) * size,
            bytes_accessed=4 * size * (group * ops + len(sides)),
            transcendentals=0,
        ),
        name="partial_sums",
    )(places, coupling, vrows, vcols, *chunks)


def make_coupled(chunks, received, places, coupling, vrows, vcols, links, sides):
    group = len(chunks)
    ops, _, height, width = chunks[0].shape
    held, factors = coupling_scratch(group * ops + 1 + len(sides), height, width, vrows.shape[0])
    size = height * width
    return pl.pallas_call(
        functools.partial(coupled_kernel, links, sides, group),
        in_specs=[scalars(), scalars()] + [whole()] * (3 + group),
        out_specs=[whole()] * group,
        out_shape=[jax.ShapeDtypeStruct(chunks[0].shape, bf16)] * group,
        scratch_shapes=held
        + [pltpu.VMEM((group * ops, 2, height, width), bf16)]
        + factors
        + [pltpu.SMEM((len(links),), jnp.int32)],
        compiler_params=params(32),
        cost_estimate=pl.CostEstimate(
            flops=40 * group * ops * size,
            bytes_accessed=4 * size * (2 * group * ops + len(sides)),
            transcendentals=0,
        ),
        name="coupling_sums",
    )(places, coupling, vrows, vcols, *chunks, received)


def product_kernel(count, where, decay, h_own, s_own, *refs):
    s_parts, h_parts, out = refs[:count], refs[count : 2 * count], refs[2 * count]
    s_all, h_all = refs[2 * count + 1 :]
    a = pl.program_id(1)
    height = h_own.shape[1]

    def place(b):
        return pl.ds(pl.multiple_of((where[0] ^ b) * height, row_tile), height)

    @pl.when(a == 0)
    def _():
        for b in range(count):
            h_all[:, place(b), :] = h_parts[b][...]

    for b in range(count):
        s_all[:, place(b), :] = s_parts[b][0]

    def dot(left, right):
        return jnp.dot(left, right, preferred_element_type=f32)

    h_real, h_imag = h_own[0], h_own[1]
    s_real, s_imag = s_own[a, 0], s_own[a, 1]
    lost = decay[a]
    imag = dot(h_real, s_all[1]) + dot(h_imag, s_all[0])
    imag = imag - dot(s_real, h_all[1]) - dot(s_imag, h_all[0])
    out[0, 0] = imag - lost * s_parts[0][0, 0].astype(f32)
    real = dot(h_real, s_all[0]) - dot(h_imag, s_all[1])
    real = real - dot(s_real, h_all[0]) + dot(s_imag, h_all[1])
    out[0, 1] = -real - lost * s_parts[0][0, 1].astype(f32)


def make_product(s_parts, h_parts, place, decay):
    ops, _, rows, columns = s_parts[0].shape
    count = len(s_parts)
    tile = min(columns, 256)
    return pl.pallas_call(
        functools.partial(product_kernel, count),
        grid=(columns // tile, ops),
        in_specs=[
            scalars(),
            scalars(),
            pl.BlockSpec((2, rows, columns), lambda j, a: (0, 0, 0)),
            pl.BlockSpec((ops, 2, rows, columns), lambda j, a: (0, 0, 0, 0)),
        ]
        + [pl.BlockSpec((1, 2, rows, tile), lambda j, a: (a, 0, 0, j))] * count
        + [pl.BlockSpec((2, rows, tile), lambda j, a: (0, 0, j))] * count,
        out_specs=pl.BlockSpec((1, 2, rows, tile), lambda j, a: (a, 0, 0, j)),
        out_shape=jax.ShapeDtypeStruct((ops, 2, rows, columns), f32),
        scratch_shapes=[pltpu.VMEM((2, count * rows, tile), bf16)] * 2,
        compiler_params=params(32),
        cost_estimate=pl.CostEstimate(
            flops=16 * ops * rows * columns * columns,
            bytes_accessed=4 * count * (ops + 1) * rows * columns + 8 * ops * rows * columns,
            transcendentals=0,
        ),
        name="products",
    )(place, decay, h_parts[0], s_parts[0], *s_parts, *h_parts)


def final_kernel(group, split, where, product, accumulated, *refs):
    sums, slope, total = refs[: group * split], refs[group * split], refs[group * split + 1]
    b, a = pl.program_id(0), pl.program_id(1)
    height = sums[0].shape[2]
    for i in range(group):

        @pl.when(b == i)
        def _():
            for p in range(split):
                rows = slice(p * height, (p + 1) * height)
                value = product[0, :, rows, :] + sums[i * split + p][a].astype(f32)
                slope[0, :, rows, :] = value
                total[0, :, rows, :] = accumulated[0, :, rows, :] + (step_size / 3.0) * value


def make_final(product, accumulated, sums, place):
    ops, parts, rows, columns = product.shape
    split, group = len(sums), len(sums[0])
    width = columns // group
    block = pl.BlockSpec((1, parts, rows, width), lambda b, a, g: (a, 0, 0, g[0] ^ b))
    held = pl.BlockSpec(sums[0][0].shape, lambda b, a, g: (0, 0, 0, 0))
    return pl.pallas_call(
        functools.partial(final_kernel, group, split),
        grid_spec=pltpu.PrefetchScalarGridSpec(
            num_scalar_prefetch=1,
            grid=(group, ops),
            in_specs=[block, block] + [held] * (group * split),
            out_specs=[block, block],
        ),
        out_shape=[jax.ShapeDtypeStruct(product.shape, f32)] * 2,
        compiler_params=params(24),
        cost_estimate=pl.CostEstimate(
            flops=4 * product.size, bytes_accessed=18 * product.size, transcendentals=0
        ),
        name="outputs",
    )(place, product, accumulated, *[sums[p][b] for b in range(group) for p in range(split)])


def shards(
    hier,
    row,
    state,
    prev_slope,
    accumulated,
    hamiltonian,
    couple_v,
    coupling,
    damping,
    occupation,
    parents,
    children,
):
    ops, _, rows, columns = state.shape
    modes = occupation.shape[1]
    group = hier // 2
    width = columns // group
    split = pieces
    height = rows // split
    table = index_rows(hier * ops, modes)
    links, sides = coupled_to(table), smaller_class(table)

    hier_at, row_at = lax.axis_index("hier"), lax.axis_index("row")
    own = hier_at % group
    own_place, row_place = own.reshape(1).astype(jnp.int32), row_at.reshape(1).astype(jnp.int32)

    def gather_rows(array):
        parts = {0: array}
        bit = row // 2
        while bit:
            for mask in list(parts):
                parts[mask ^ bit] = swap(parts[mask], "row", row, bit)
            bit //= 2
        return [parts[b] for b in range(row)]

    h_parts = gather_rows(hamiltonian)
    section, chunks = make_section(state, prev_slope, own_place, group, split)

    everyone = lax.all_gather(occupation, "hier", axis=0, tiled=True)
    known = jnp.asarray(np.array(table, np.int32))
    same = jnp.all(everyone[:, None, :] == known[None, :, :], axis=2)
    slot = jnp.sum(jnp.where(same, jnp.arange(hier * ops, dtype=jnp.int32)[:, None], 0), axis=0)
    device = slot // ops
    places = jnp.where(
        device // group == hier_at // group,
        ((device % group) ^ own) * ops + slot % ops,
        group * ops,
    ).astype(jnp.int32)
    vrows = lax.dynamic_slice_in_dim(couple_v, row_at * rows, rows, 1)[:, :, None]
    vcols = lax.dynamic_slice_in_dim(couple_v, own * width, width, 1)
    decay = jnp.sum(occupation.astype(f32) * damping[None, :], axis=1)

    sums = []
    for p in range(split):
        here = vrows[:, p * height : (p + 1) * height]
        got = [chunks[p][0]] + [swap(chunks[p][b], "hier", hier, b) for b in range(1, group)]
        sent = make_partial(got, places, coupling, here, vcols, links, sides)
        received = swap(sent, "hier", hier, group)
        done = make_coupled(got, received, places, coupling, here, vcols, links, sides)
        sums.append([done[0]] + [swap(done[b], "hier", hier, b) for b in range(1, group)])

    s_parts = gather_rows(section)
    product = make_product(s_parts, h_parts, row_place, decay)
    slope, total = make_final(product, accumulated, sums, own_place)
    return slope, total


def solution(mesh):
    return jax.shard_map(
        functools.partial(shards, mesh.shape["hier"], mesh.shape["row"]),
        mesh=mesh,
        in_specs=(
            P("hier", None, "row", None),
            P("hier", None, "row", None),
            P("hier", None, "row", None),
            P(None, "row", None),
            P(),
            P(),
            P(),
            P("hier", None),
            P("hier", None),
            P("hier", None),
        ),
        out_specs=(P("hier", None, "row", None), P("hier", None, "row", None)),
        check_vma=False,
    )
```

```python
import functools

import jax
import jax.numpy as jnp
import numpy as np
from jax import lax
from jax.experimental import pallas as pl
from jax.experimental.pallas import tpu as pltpu
from jax.sharding import PartitionSpec as P

step_size = 0.5
highest_total = 4
row_tile = 16
pieces = 2
MIB = 1024 * 1024
f32 = jnp.float32
bf16 = jnp.bfloat16


def index_rows(slots, modes):
    entries = [()]
    for _ in range(modes):
        entries = [
            entry + (level,)
            for entry in entries
            for level in range(highest_total + 1)
            if sum(entry) + level <= highest_total
        ]
    return sorted(entries, key=lambda entry: (sum(entry), entry))[:slots]


def coupled_to(rows):
    lookup = {entry: place for place, entry in enumerate(rows)}
    result = []
    for entry in rows:
        terms = []
        for mode, level in enumerate(entry):
            raised = entry[:mode] + (level + 1,) + entry[mode + 1 :]
            if raised in lookup:
                terms.append((lookup[raised], mode, True, 1))
            if level > 0:
                lowered = entry[:mode] + (level - 1,) + entry[mode + 1 :]
                terms.append((lookup[lowered], mode, False, level))
        result.append(terms)
    return result


def smaller_class(rows):
    classes = [[c for c, entry in enumerate(rows) if sum(entry) % 2 == rest] for rest in (0, 1)]
    return min(classes, key=len)


def params(megabytes):
    return pltpu.CompilerParams(vmem_limit_bytes=megabytes * MIB)


def whole():
    return pl.BlockSpec(memory_space=pltpu.VMEM)


def scalars():
    return pl.BlockSpec(memory_space=pltpu.SMEM)


def swap(array, axis, size, bit):
    return lax.ppermute(array, axis, [(i, i ^ bit) for i in range(size)])


def tie(arrays):
    return lax.optimization_barrier(arrays)


def row_bits(size):
    return [1 << i for i in reversed(range(size.bit_length() - 1))]


def tree(array, size, bits):
    parts = {0: array}
    for bit in bits:
        for mask in list(parts):
            parts[mask ^ bit] = swap(parts[mask], "row", size, bit)
    return parts


def section_kernel(group, split, where, state, slope, section, *outs):
    value = (state[...].astype(f32) + (0.5 * step_size) * slope[...]).astype(bf16)
    section[...] = value
    a, ops = pl.program_id(0), len(outs) - group * split
    singles, chunks = outs[:ops], outs[ops:]
    for i, single in enumerate(singles):

        @pl.when(a == i)
        def _():
            single[...] = value[0]

    width = chunks[0].shape[-1]
    height = chunks[0].shape[-2]
    for b in range(group):
        columns = pl.ds(pl.multiple_of((where[0] ^ b) * width, 128), width)
        for p in range(split):
            chunks[b * split + p][...] = section[:, :, p * height : (p + 1) * height, columns]


def make_section(state, prev_slope, place, group, split):
    ops, parts, rows, columns = state.shape
    height, width = rows // split, columns // group
    block = pl.BlockSpec((1, 1, rows, columns), lambda a, x, _: (a, x, 0, 0))
    chunk = pl.BlockSpec((1, 1, height, width), lambda a, x, _: (a, x, 0, 0))
    count = group * split

    def single(i):
        def place(a, x, _):
            return jnp.where(a == i, x, jnp.where(a < i, 0, parts - 1)), 0, 0

        return pl.BlockSpec((1, rows, columns), place)

    out = pl.pallas_call(
        functools.partial(section_kernel, group, split),
        grid_spec=pltpu.PrefetchScalarGridSpec(
            num_scalar_prefetch=1,
            grid=(ops, parts),
            in_specs=[block, block],
            out_specs=[block] + [single(i) for i in range(ops)] + [chunk] * count,
        ),
        out_shape=[jax.ShapeDtypeStruct(state.shape, bf16)]
        + [jax.ShapeDtypeStruct(state.shape[1:], bf16)] * ops
        + [jax.ShapeDtypeStruct((ops, parts, height, width), bf16)] * count,
        compiler_params=params(56),
        cost_estimate=pl.CostEstimate(
            flops=2 * state.size, bytes_accessed=10 * state.size, transcendentals=0
        ),
        name="section",
    )(place, state, prev_slope)
    singles, chunks = out[1 : 1 + ops], out[1 + ops :]
    return out[0], singles, [[chunks[b * split + p] for b in range(group)] for p in range(split)]


def fill_factors(vrows, vcols, coupling, factors):
    modes = vrows.shape[0]
    for k in range(modes):
        first = vrows[k]
        second = vcols[k : k + 1, :]
        diff = first - second
        factors[k] = diff
        factors[modes + k] = coupling[0, k] * diff
        factors[2 * modes + k] = coupling[1, k] * (first + second)


def add_terms(terms, places, held, factors, modes, rows, real, imag):
    for other, mode, child, count in terms:
        place = places[other]
        x_real = held[place, 0, rows, :].astype(f32)
        x_imag = held[place, 1, rows, :].astype(f32)
        if child:
            diff = factors[mode, rows, :]
            real = real + diff * x_imag
            imag = imag - diff * x_real
        else:
            first = factors[modes + mode, rows, :]
            second = factors[2 * modes + mode, rows, :]
            if count != 1:
                first, second = count * first, count * second
            real = real + (first * x_imag + second * x_real)
            imag = imag + (second * x_imag - first * x_real)
    return real, imag


def load_held(chunks, held):
    ops = chunks[0].shape[0]
    for b, chunk in enumerate(chunks):
        held[b * ops : (b + 1) * ops] = chunk[...]
    held[len(chunks) * ops] = jnp.zeros(held.shape[1:], bf16)


def partial_kernel(links, sides, group, places, coupling, vrows, vcols, *refs):
    chunks, out, held, factors = refs[:group], refs[group], refs[group + 1], refs[group + 2]
    modes = vrows.shape[0]
    height, width = held.shape[2:]
    empty = group * chunks[0].shape[0]
    fill_factors(vrows, vcols, coupling, factors)
    load_held(chunks, held)
    for u, c in enumerate(sides):

        @pl.when(places[c] < empty)
        def _():
            out[u] = held[places[c]]

        @pl.when(places[c] == empty)
        def _():
            @pl.loop(0, height // row_tile)
            def _(i):
                rows = pl.ds(pl.multiple_of(i * row_tile, row_tile), row_tile)
                zero = jnp.zeros((row_tile, width), f32)
                real, imag = add_terms(links[c], places, held, factors, modes, rows, zero, zero)
                out[u, 0, rows, :] = real.astype(bf16)
                out[u, 1, rows, :] = imag.astype(bf16)


def coupled_kernel(links, sides, group, places, coupling, vrows, vcols, *refs):
    chunks, received, outs = refs[:group], refs[group], refs[group + 1 : 2 * group + 1]
    held, done, factors, spots = refs[2 * group + 1 :]
    modes = vrows.shape[0]
    height, width = held.shape[2:]
    ops = chunks[0].shape[0]
    empty = group * ops
    fill_factors(vrows, vcols, coupling, factors)
    load_held(chunks, held)
    held[empty + 1 :] = received[...]
    for c in range(len(links)):
        spots[c] = places[c]
    for u, c in enumerate(sides):
        spots[c] = jnp.where(places[c] == empty, empty + 1 + u, places[c])
    for c in range(len(links)):

        @pl.when(places[c] < empty)
        def _():
            @pl.loop(0, height // row_tile)
            def _(i):
                rows = pl.ds(pl.multiple_of(i * row_tile, row_tile), row_tile)
                if c in sides:
                    u = empty + 1 + sides.index(c)
                    real, imag = held[u, 0, rows, :].astype(f32), held[u, 1, rows, :].astype(f32)
                else:
                    real = imag = jnp.zeros((row_tile, width), f32)
                real, imag = add_terms(links[c], spots, held, factors, modes, rows, real, imag)
                done[places[c], 0, rows, :] = real.astype(bf16)
                done[places[c], 1, rows, :] = imag.astype(bf16)

    for b, out in enumerate(outs):
        out[...] = done[b * ops : (b + 1) * ops]


def coupling_scratch(entries, height, width, modes):
    return [pltpu.VMEM((entries, 2, height, width), bf16)], [pltpu.VMEM((3 * modes, height, width), f32)]


def make_partial(chunks, places, coupling, vrows, vcols, links, sides):
    group = len(chunks)
    ops, _, height, width = chunks[0].shape
    held, factors = coupling_scratch(group * ops + 1, height, width, vrows.shape[0])
    size = height * width
    return pl.pallas_call(
        functools.partial(partial_kernel, links, sides, group),
        in_specs=[scalars(), scalars()] + [whole()] * (2 + group),
        out_specs=whole(),
        out_shape=jax.ShapeDtypeStruct((len(sides), 2, height, width), bf16),
        scratch_shapes=held + factors,
        compiler_params=params(32),
        cost_estimate=pl.CostEstimate(
            flops=40 * len(sides) * size,
            bytes_accessed=4 * size * (group * ops + len(sides)),
            transcendentals=0,
        ),
        name="partial_sums",
    )(places, coupling, vrows, vcols, *chunks)


def make_coupled(chunks, received, places, coupling, vrows, vcols, links, sides):
    group = len(chunks)
    ops, _, height, width = chunks[0].shape
    held, factors = coupling_scratch(group * ops + 1 + len(sides), height, width, vrows.shape[0])
    size = height * width
    return pl.pallas_call(
        functools.partial(coupled_kernel, links, sides, group),
        in_specs=[scalars(), scalars()] + [whole()] * (3 + group),
        out_specs=[whole()] * group,
        out_shape=[jax.ShapeDtypeStruct(chunks[0].shape, bf16)] * group,
        scratch_shapes=held
        + [pltpu.VMEM((group * ops, 2, height, width), bf16)]
        + factors
        + [pltpu.SMEM((len(links),), jnp.int32)],
        compiler_params=params(32),
        cost_estimate=pl.CostEstimate(
            flops=40 * group * ops * size,
            bytes_accessed=4 * size * (2 * group * ops + len(sides)),
            transcendentals=0,
        ),
        name="coupling_sums",
    )(places, coupling, vrows, vcols, *chunks, received)


def product_kernel(op, count, where, decay, h_own, s_own, *refs):
    s_parts, h_parts, out = refs[:count], refs[count : 2 * count], refs[2 * count]
    s_all, h_all = refs[2 * count + 1 :]
    height, depth = h_own.shape[1:]
    for b in range(count):
        rows = pl.ds(pl.multiple_of((where[0] ^ b) * height, row_tile), height)
        h_all[:, rows, :] = h_parts[b][...]
        s_all[:, rows, :] = s_parts[b][...].reshape(s_all.shape[0], height, -1)

    def product(left, right):
        left = left.reshape(2 * height, depth)
        first = jnp.dot(left, right[0], preferred_element_type=f32)
        second = jnp.dot(left, right[1], preferred_element_type=f32)
        return first[:height] - second[height:], second[:height] + first[height:]

    left_real, left_imag = product(h_own[...], s_all)
    right_real, right_imag = product(s_own[0], h_all)
    lost = decay[op]
    own = s_parts[0]
    out[0] = (left_imag - right_imag) - lost * own[0, 0].astype(f32)
    out[1] = (right_real - left_real) - lost * own[0, 1].astype(f32)


def make_product(op, near, far, h_parts, place, decay):
    ops, _, rows, columns = near[0].shape
    count = 2 * len(near)
    tile = min(columns, 256)
    s_parts = [{**near, **far}[b] for b in range(count)]
    held = pl.BlockSpec((2, rows, columns), lambda j: (0, 0, 0))
    own = pl.BlockSpec((1, 2, rows, columns), lambda j: (op, 0, 0, 0))
    three = pl.BlockSpec((2, rows, tile), lambda j: (0, 0, j))
    four = pl.BlockSpec((1, 2, rows, tile), lambda j: (op, 0, 0, j))
    return pl.pallas_call(
        functools.partial(product_kernel, op, count),
        grid=(columns // tile,),
        in_specs=[scalars(), scalars(), held, own]
        + [four if b in near else three for b in range(count)]
        + [three] * count,
        out_specs=three,
        out_shape=jax.ShapeDtypeStruct((2, rows, columns), f32),
        scratch_shapes=[pltpu.VMEM((2, count * rows, tile), bf16)] * 2,
        compiler_params=params(48),
        cost_estimate=pl.CostEstimate(
            flops=16 * rows * columns * columns,
            bytes_accessed=8 * count * rows * columns + 16 * rows * columns,
            transcendentals=0,
        ),
        name="products",
    )(place, decay, h_parts[0], near[0], *s_parts, *h_parts)


def final_kernel(ops, group, split, where, accumulated, *refs):
    products, sums, (slope, total) = refs[:ops], refs[ops:-2], refs[-2:]
    a, b = pl.program_id(0), pl.program_id(1)
    height = sums[0].shape[2]
    for i in range(ops):
        for k in range(group):

            @pl.when(jnp.logical_and(a == i, b == k))
            def _():
                for p in range(split):
                    rows = slice(p * height, (p + 1) * height)
                    value = products[i][:, rows, :] + sums[k * split + p][i].astype(f32)
                    slope[0, :, rows, :] = value
                    total[0, :, rows, :] = accumulated[0, :, rows, :] + (step_size / 3.0) * value


def make_final(products, accumulated, sums, place):
    ops, parts, rows, columns = accumulated.shape
    split, group = len(sums), len(sums[0])
    width = columns // group
    block = pl.BlockSpec((1, parts, rows, width), lambda a, b, g: (a, 0, 0, g[0] ^ b))
    held = pl.BlockSpec(sums[0][0].shape, lambda a, b, g: (0, 0, 0, 0))

    def single(i):
        def place(a, b, g):
            return 0, 0, g[0] ^ jnp.where(a == i, b, jnp.where(a < i, 0, group - 1))

        return pl.BlockSpec((parts, rows, width), place)

    return pl.pallas_call(
        functools.partial(final_kernel, ops, group, split),
        grid_spec=pltpu.PrefetchScalarGridSpec(
            num_scalar_prefetch=1,
            grid=(ops, group),
            in_specs=[block] + [single(i) for i in range(ops)] + [held] * (group * split),
            out_specs=[block, block],
        ),
        out_shape=[jax.ShapeDtypeStruct(accumulated.shape, f32)] * 2,
        compiler_params=params(56),
        cost_estimate=pl.CostEstimate(
            flops=4 * accumulated.size, bytes_accessed=18 * accumulated.size, transcendentals=0
        ),
        name="outputs",
    )(place, accumulated, *products, *[sums[p][b] for b in range(group) for p in range(split)])


def shards(
    hier,
    row,
    state,
    prev_slope,
    accumulated,
    hamiltonian,
    couple_v,
    coupling,
    damping,
    occupation,
    parents,
    children,
):
    ops, _, rows, columns = state.shape
    modes = occupation.shape[1]
    group = hier // 2
    width = columns // group
    split = pieces
    height = rows // split
    table = index_rows(hier * ops, modes)
    links, sides = coupled_to(table), smaller_class(table)

    hier_at, row_at = lax.axis_index("hier"), lax.axis_index("row")
    own = hier_at % group
    own_place, row_place = own.reshape(1).astype(jnp.int32), row_at.reshape(1).astype(jnp.int32)

    half = {0: occupation}
    for b in range(1, group):
        half[b] = swap(occupation, "hier", hier, b)
    bits = row_bits(row)
    top, low = bits[0], bits[1:]
    h_near, h_top = tree(hamiltonian, row, low), swap(hamiltonian, "row", row, top)
    section, singles, chunks = make_section(state, prev_slope, own_place, group, split)
    section, singles, chunks, half, h_near, h_top = tie(
        (section, singles, chunks, half, h_near, h_top)
    )

    known = jnp.asarray(np.array(table, np.int32))
    found = jnp.concatenate([half[b] for b in range(group)], axis=0)
    same = jnp.all(found[None, :, :] == known[:, None, :], axis=2)
    spot = jnp.arange(group * ops, dtype=jnp.int32)[None, :]
    places = jnp.min(jnp.where(same, spot, group * ops), axis=1).astype(jnp.int32)
    vrows = lax.dynamic_slice_in_dim(couple_v, row_at * rows, rows, 1)[:, :, None]
    vcols = lax.dynamic_slice_in_dim(couple_v, own * width, width, 1)
    decay = jnp.sum(occupation.astype(f32) * damping[None, :], axis=1)

    heres = [vrows[:, p * height : (p + 1) * height] for p in range(split)]

    def spread(p):
        return [chunks[p][0]] + [swap(chunks[p][b], "hier", hier, b) for b in range(1, group)]

    def partial(p):
        return make_partial(got[p], places, coupling, heres[p], vcols, links, sides)

    def coupled(p):
        return make_coupled(got[p], received[p], places, coupling, heres[p], vcols, links, sides)

    def gather_back(done):
        return [done[0]] + [swap(done[b], "hier", hier, b) for b in range(1, group)]

    def across(array):
        return {mask ^ top: part for mask, part in tree(array, row, low).items()}

    def product(a):
        return make_product(a, near, far[a], h_parts, row_place, decay)

    got, sent, received, sums, tops, far = [], [], [], [], [], []

    got.append(spread(0))
    tops.append(swap(singles[0], "row", row, top))
    h_far = across(h_top)
    got, tops, h_far, singles, chunks, section, places, heres, vcols, decay = tie(
        (got, tops, h_far, singles, chunks, section, places, heres, vcols, decay)
    )
    h_parts = [{**h_near, **h_far}[b] for b in range(row)]

    sent.append(partial(0))
    received.append(swap(sent[0], "hier", hier, group))
    got.append(spread(1))
    tops.append(swap(singles[1], "row", row, top))
    got, tops, received, singles, section = tie((got, tops, received, singles, section))

    sent.append(partial(1))
    received.append(swap(sent[1], "hier", hier, group))
    tops.append(swap(singles[2], "row", row, top))
    near = tree(section, row, low)
    far = [across(tops[0]), across(tops[1])]
    sums.append(coupled(0))
    sums, near, far = tie((sums, near, far))
    sums[0] = gather_back(sums[0])
    products = [product(0), product(1)]
    received, tops, sums, products = tie((received, tops, sums, products))

    sums.append(gather_back(coupled(1)))
    far.append(across(tops[2]))
    products.append(product(2))
    slope, total = make_final(products, accumulated, sums, own_place)
    return slope, total


def solution(mesh):
    return jax.shard_map(
        functools.partial(shards, mesh.shape["hier"], mesh.shape["row"]),
        mesh=mesh,
        in_specs=(
            P("hier", None, "row", None),
            P("hier", None, "row", None),
            P("hier", None, "row", None),
            P(None, "row", None),
            P(),
            P(),
            P(),
            P("hier", None),
            P("hier", None),
            P("hier", None),
        ),
        out_specs=(P("hier", None, "row", None), P("hier", None, "row", None)),
        check_vma=False,
    )
```

```python
import functools

import jax
import jax.numpy as jnp
import numpy as np
from jax import lax
from jax.experimental import pallas as pl
from jax.experimental.pallas import tpu as pltpu
from jax.sharding import PartitionSpec as P

step_size = 0.5
highest_total = 4
row_tile = 16
pieces = 2
MIB = 1024 * 1024
f32 = jnp.float32
bf16 = jnp.bfloat16


def index_rows(slots, modes):
    entries = [()]
    for _ in range(modes):
        entries = [
            entry + (level,)
            for entry in entries
            for level in range(highest_total + 1)
            if sum(entry) + level <= highest_total
        ]
    return sorted(entries, key=lambda entry: (sum(entry), entry))[:slots]


def coupled_to(rows):
    lookup = {entry: place for place, entry in enumerate(rows)}
    result = []
    for entry in rows:
        terms = []
        for mode, level in enumerate(entry):
            raised = entry[:mode] + (level + 1,) + entry[mode + 1 :]
            if raised in lookup:
                terms.append((lookup[raised], mode, True, 1))
            if level > 0:
                lowered = entry[:mode] + (level - 1,) + entry[mode + 1 :]
                terms.append((lookup[lowered], mode, False, level))
        result.append(terms)
    return result


def smaller_class(rows):
    classes = [[c for c, entry in enumerate(rows) if sum(entry) % 2 == rest] for rest in (0, 1)]
    return min(classes, key=len)


def params(megabytes):
    return pltpu.CompilerParams(vmem_limit_bytes=megabytes * MIB)


def whole():
    return pl.BlockSpec(memory_space=pltpu.VMEM)


def anywhere():
    return pl.BlockSpec(memory_space=pl.ANY)


def scalars():
    return pl.BlockSpec(memory_space=pltpu.SMEM)


def swap(array, axis, size, bit):
    return lax.ppermute(array, axis, [(i, i ^ bit) for i in range(size)])


def tie(arrays):
    return lax.optimization_barrier(arrays)


def row_bits(size):
    return [1 << i for i in reversed(range(size.bit_length() - 1))]


def tree(array, size, bits):
    parts = {0: array}
    for bit in bits:
        for mask in list(parts):
            parts[mask ^ bit] = swap(parts[mask], "row", size, bit)
    return parts


def section_kernel(where, state, slope, section, *chunks):
    value = (state[...].astype(f32) + (0.5 * step_size) * slope[...]).astype(bf16)
    section[...] = value
    width = chunks[0].shape[-1]
    for b, chunk in enumerate(chunks):
        columns = pl.ds(pl.multiple_of((where[0] ^ b) * width, 128), width)
        chunk[...] = section[:, :, :, columns]


def make_section(p, split, state, prev_slope, place, group):
    ops, parts, rows, columns = state.shape
    height, width = rows // split, columns // group
    block = pl.BlockSpec((1, parts, height, columns), lambda a, _: (a, 0, p, 0))
    out = pl.BlockSpec((1, parts, height, columns), lambda a, _: (a, 0, 0, 0))
    chunk = pl.BlockSpec((1, parts, height, width), lambda a, _: (a, 0, 0, 0))
    section, *chunks = pl.pallas_call(
        section_kernel,
        grid_spec=pltpu.PrefetchScalarGridSpec(
            num_scalar_prefetch=1,
            grid=(ops,),
            in_specs=[block, block],
            out_specs=[out] + [chunk] * group,
        ),
        out_shape=[jax.ShapeDtypeStruct((ops, parts, height, columns), bf16)]
        + [jax.ShapeDtypeStruct((ops, parts, height, width), bf16)] * group,
        compiler_params=params(56),
        cost_estimate=pl.CostEstimate(flops=1, bytes_accessed=1, transcendentals=0),
        name="section",
    )(place, state, prev_slope)
    return section, chunks


def fill_factors(vrows, vcols, coupling, factors):
    modes = vrows.shape[0]
    for k in range(modes):
        first = vrows[k]
        second = vcols[k : k + 1, :]
        diff = first - second
        factors[k] = diff
        factors[modes + k] = coupling[0, k] * diff
        factors[2 * modes + k] = coupling[1, k] * (first + second)


def add_terms(terms, places, held, factors, modes, rows, real, imag):
    for other, mode, child, count in terms:
        place = places[other]
        x_real = held[place, 0, rows, :].astype(f32)
        x_imag = held[place, 1, rows, :].astype(f32)
        if child:
            diff = factors[mode, rows, :]
            real = real + diff * x_imag
            imag = imag - diff * x_real
        else:
            first = factors[modes + mode, rows, :]
            second = factors[2 * modes + mode, rows, :]
            if count != 1:
                first, second = count * first, count * second
            real = real + (first * x_imag + second * x_real)
            imag = imag + (second * x_imag - first * x_real)
    return real, imag


def partial_kernel(links, sides, group, places, coupling, vrows, vcols, *refs):
    chunks, out, held, factors, sems = refs[:group], *refs[group:]
    modes = vrows.shape[0]
    height, width = held.shape[2:]
    ops = chunks[0].shape[0]
    empty = group * ops
    loads = [
        pltpu.make_async_copy(chunk, held.at[pl.ds(b * ops, ops)], sems.at[b])
        for b, chunk in enumerate(chunks)
    ]
    for load in loads:
        load.start()
    fill_factors(vrows, vcols, coupling, factors)
    held[empty] = jnp.zeros(held.shape[1:], bf16)
    for load in loads:
        load.wait()
    for u, c in enumerate(sides):

        @pl.when(places[c] < empty)
        def _():
            out[u] = held[places[c]]

        @pl.when(places[c] == empty)
        def _():
            @pl.loop(0, height // row_tile)
            def _(i):
                rows = pl.ds(pl.multiple_of(i * row_tile, row_tile), row_tile)
                zero = jnp.zeros((row_tile, width), f32)
                real, imag = add_terms(links[c], places, held, factors, modes, rows, zero, zero)
                out[u, 0, rows, :] = real.astype(bf16)
                out[u, 1, rows, :] = imag.astype(bf16)


def coupled_kernel(links, sides, group, places, coupling, vrows, vcols, *refs):
    chunks, received, outs = refs[:group], refs[group], refs[group + 1 : 2 * group + 1]
    held, done, factors, spots, sems = refs[2 * group + 1 :]
    modes = vrows.shape[0]
    height, width = held.shape[2:]
    ops = chunks[0].shape[0]
    empty = group * ops
    loads = [
        pltpu.make_async_copy(chunk, held.at[pl.ds(b * ops, ops)], sems.at[b])
        for b, chunk in enumerate(chunks)
    ]
    loads.append(
        pltpu.make_async_copy(received, held.at[pl.ds(empty + 1, len(sides))], sems.at[group])
    )
    for load in loads:
        load.start()
    fill_factors(vrows, vcols, coupling, factors)
    held[empty] = jnp.zeros(held.shape[1:], bf16)
    for c in range(len(links)):
        spots[c] = places[c]
    for u, c in enumerate(sides):
        spots[c] = jnp.where(places[c] == empty, empty + 1 + u, places[c])
    for load in loads:
        load.wait()
    for c in range(len(links)):

        @pl.when(places[c] < empty)
        def _():
            @pl.loop(0, height // row_tile)
            def _(i):
                rows = pl.ds(pl.multiple_of(i * row_tile, row_tile), row_tile)
                if c in sides:
                    u = empty + 1 + sides.index(c)
                    real, imag = held[u, 0, rows, :].astype(f32), held[u, 1, rows, :].astype(f32)
                else:
                    real = imag = jnp.zeros((row_tile, width), f32)
                real, imag = add_terms(links[c], spots, held, factors, modes, rows, real, imag)
                done[places[c], 0, rows, :] = real.astype(bf16)
                done[places[c], 1, rows, :] = imag.astype(bf16)

    stores = [
        pltpu.make_async_copy(done.at[pl.ds(b * ops, ops)], out, sems.at[group + 1 + b])
        for b, out in enumerate(outs)
    ]
    for store in stores:
        store.start()
    for store in stores:
        store.wait()


def coupling_scratch(entries, height, width, modes):
    return [pltpu.VMEM((entries, 2, height, width), bf16)], [pltpu.VMEM((3 * modes, height, width), f32)]


def make_partial(chunks, places, coupling, vrows, vcols, links, sides):
    group = len(chunks)
    ops, _, height, width = chunks[0].shape
    held, factors = coupling_scratch(group * ops + 1, height, width, vrows.shape[0])
    size = height * width
    return pl.pallas_call(
        functools.partial(partial_kernel, links, sides, group),
        in_specs=[scalars(), scalars()] + [whole()] * 2 + [anywhere()] * group,
        out_specs=whole(),
        out_shape=jax.ShapeDtypeStruct((len(sides), 2, height, width), bf16),
        scratch_shapes=held + factors + [pltpu.SemaphoreType.DMA((group,))],
        compiler_params=params(32),
        cost_estimate=pl.CostEstimate(
            flops=40 * len(sides) * size,
            bytes_accessed=4 * size * (group * ops + len(sides)),
            transcendentals=0,
        ),
        name="partial_sums",
    )(places, coupling, vrows, vcols, *chunks)


def make_coupled(chunks, received, places, coupling, vrows, vcols, links, sides):
    group = len(chunks)
    ops, _, height, width = chunks[0].shape
    held, factors = coupling_scratch(group * ops + 1 + len(sides), height, width, vrows.shape[0])
    size = height * width
    return pl.pallas_call(
        functools.partial(coupled_kernel, links, sides, group),
        in_specs=[scalars(), scalars()] + [whole()] * 2 + [anywhere()] * (1 + group),
        out_specs=[anywhere()] * group,
        out_shape=[jax.ShapeDtypeStruct(chunks[0].shape, bf16)] * group,
        scratch_shapes=held
        + [pltpu.VMEM((group * ops, 2, height, width), bf16)]
        + factors
        + [pltpu.SMEM((len(links),), jnp.int32), pltpu.SemaphoreType.DMA((2 * group + 1,))],
        compiler_params=params(32),
        cost_estimate=pl.CostEstimate(
            flops=40 * group * ops * size,
            bytes_accessed=4 * size * (2 * group * ops + len(sides)),
            transcendentals=0,
        ),
        name="coupling_sums",
    )(places, coupling, vrows, vcols, *chunks, received)


def complex_rows(left, right):
    _, height, depth = left.shape
    left = left.reshape(2 * height, depth)
    first = jnp.dot(left, right[0], preferred_element_type=f32)
    second = jnp.dot(left, right[1], preferred_element_type=f32)
    return first[:height] - second[height:], second[:height] + first[height:]


def right_kernel(split, count, where, decay, *refs):
    sections, h_parts, (out, h_all) = refs[:split], refs[split:-2], refs[-2:]
    j, a = pl.program_id(0), pl.program_id(1)
    rows, tile = h_parts[0].shape[1:]
    height = sections[0].shape[2]

    @pl.when(a == 0)
    def _():
        for b in range(count):
            place = pl.ds(pl.multiple_of((where[0] ^ b) * rows, row_tile), rows)
            h_all[:, place, :] = h_parts[b][...]

    columns = pl.ds(pl.multiple_of(j * tile, 128), tile)
    lost = decay[a]
    for p, section in enumerate(sections):
        real, imag = complex_rows(section[a], h_all)
        here = slice(p * height, (p + 1) * height)
        out[0, 0, here, :] = -imag - lost * section[a, 0, :, columns].astype(f32)
        out[0, 1, here, :] = real - lost * section[a, 1, :, columns].astype(f32)


def make_right(sections, h_parts, place, decay):
    ops, _, height, columns = sections[0].shape
    split, count = len(sections), len(h_parts)
    rows, tile = height * split, min(columns, 256)
    held = pl.BlockSpec((ops, 2, height, columns), lambda j, a: (0, 0, 0, 0))
    return pl.pallas_call(
        functools.partial(right_kernel, split, count),
        grid=(columns // tile, ops),
        in_specs=[scalars(), scalars()]
        + [held] * split
        + [pl.BlockSpec((2, rows, tile), lambda j, a: (0, 0, j))] * count,
        out_specs=pl.BlockSpec((1, 2, rows, tile), lambda j, a: (a, 0, 0, j)),
        out_shape=jax.ShapeDtypeStruct((ops, 2, rows, columns), f32),
        scratch_shapes=[pltpu.VMEM((2, count * rows, tile), bf16)],
        compiler_params=params(40),
        cost_estimate=pl.CostEstimate(
            flops=8 * ops * rows * columns * columns,
            bytes_accessed=4 * columns * (columns + 3 * ops * rows),
            transcendentals=0,
        ),
        name="right_products",
    )(place, decay, *sections, *h_parts)


def left_kernel(count, where, h_own, base, *refs):
    s_parts, (out, s_all) = refs[:count], refs[count:]
    height = s_parts[0].shape[2]
    for b in range(count):
        place = pl.ds(pl.multiple_of((where[0] ^ b) * height, row_tile), height)
        s_all[:, place, :] = s_parts[b][0]
    real, imag = complex_rows(h_own[...], s_all)
    out[0, 0] = base[0, 0] + imag
    out[0, 1] = base[0, 1] - real


def make_left(s_parts, h_columns, base, place):
    ops, _, height, columns = s_parts[0].shape
    count, rows, tile = len(s_parts), base.shape[2], min(columns, 256)
    block = pl.BlockSpec((1, 2, rows, tile), lambda j, a: (a, 0, 0, j))
    return pl.pallas_call(
        functools.partial(left_kernel, count),
        grid=(columns // tile, ops),
        in_specs=[
            scalars(),
            pl.BlockSpec(h_columns.shape, lambda j, a: (0, 0, 0)),
            block,
        ]
        + [pl.BlockSpec((1, 2, height, tile), lambda j, a: (a, 0, 0, j))] * count,
        out_specs=block,
        out_shape=jax.ShapeDtypeStruct(base.shape, f32),
        scratch_shapes=[pltpu.VMEM((2, count * height, tile), bf16)],
        compiler_params=params(40),
        cost_estimate=pl.CostEstimate(
            flops=8 * ops * rows * columns * count * height,
            bytes_accessed=4 * ops * columns * (count * height + 4 * rows),
            transcendentals=0,
        ),
        name="left_products",
    )(place, h_columns, base, *s_parts)


def final_kernel(group, where, product, accumulated, *refs):
    sums, (slope, total) = refs[:group], refs[-2:]
    a, i = pl.program_id(0), pl.program_id(1)
    height, width = slope.shape[2], sums[0].shape[3]
    rows = pl.ds(pl.multiple_of(i * height, row_tile), height)
    for b in range(group):
        columns = pl.ds(pl.multiple_of((where[0] ^ b) * width, 128), width)
        value = product[0, :, :, columns] + sums[b][a, :, rows, :].astype(f32)
        slope[0, :, :, columns] = value
        total[0, :, :, columns] = accumulated[0, :, :, columns] + (step_size / 3.0) * value


def make_final(p, split, product, accumulated, sums, place, earlier=()):
    ops, parts, rows, columns = product.shape
    group, steps = len(sums), 2
    height = rows // split // steps
    block = pl.BlockSpec((1, parts, height, columns), lambda a, i, _: (a, 0, p * steps + i, 0))
    held = pl.BlockSpec(sums[0].shape, lambda a, i, _: (0, 0, 0, 0))
    return pl.pallas_call(
        functools.partial(final_kernel, group),
        grid_spec=pltpu.PrefetchScalarGridSpec(
            num_scalar_prefetch=1,
            grid=(ops, steps),
            in_specs=[block, block] + [held] * group + [anywhere()] * len(earlier),
            out_specs=[block, block],
        ),
        out_shape=[jax.ShapeDtypeStruct(product.shape, f32)] * 2,
        input_output_aliases={3 + group + k: k for k in range(len(earlier))},
        compiler_params=params(56),
        cost_estimate=pl.CostEstimate(
            flops=4 * product.size // split,
            bytes_accessed=18 * product.size // split,
            transcendentals=0,
        ),
        name="outputs",
    )(place, product, accumulated, *sums, *earlier)


def shards(
    hier,
    row,
    state,
    prev_slope,
    accumulated,
    hamiltonian,
    couple_v,
    coupling,
    damping,
    occupation,
    parents,
    children,
):
    ops, _, rows, columns = state.shape
    modes = occupation.shape[1]
    group = hier // 2
    width = columns // group
    split = pieces
    height = rows // split
    table = index_rows(hier * ops, modes)
    links, sides = coupled_to(table), smaller_class(table)

    hier_at, row_at = lax.axis_index("hier"), lax.axis_index("row")
    own = hier_at % group
    own_place, row_place = own.reshape(1).astype(jnp.int32), row_at.reshape(1).astype(jnp.int32)

    bits = row_bits(row)
    top, low = bits[0], bits[1:]

    def spread(p):
        return [chunks[p][0]] + [swap(chunks[p][b], "hier", hier, b) for b in range(1, group)]

    def partial(p):
        return make_partial(got[p], places, coupling, heres[p], vcols, links, sides)

    def coupled(p):
        return make_coupled(got[p], received[p], places, coupling, heres[p], vcols, links, sides)

    def gather_back(done):
        return [done[0]] + [swap(done[b], "hier", hier, b) for b in range(1, group)]

    def joined(near, across):
        far = {mask ^ top: part for mask, part in tree(across, row, low).items()}
        parts = {**near, **far}
        return [parts[b] for b in range(row)]

    got, sent, received, sums, outs = [], [], [], [], []

    half = [occupation] + [swap(occupation, "hier", hier, b) for b in range(1, group)]
    first, first_chunks = make_section(0, split, state, prev_slope, own_place, group)
    first, first_chunks, half, state, prev_slope, couple_v, hamiltonian = tie(
        (first, first_chunks, half, state, prev_slope, couple_v, hamiltonian)
    )

    h_top, h_near = swap(hamiltonian, "row", row, top), tree(hamiltonian, row, low)
    second, second_chunks = make_section(1, split, state, prev_slope, own_place, group)
    chunks, sections = [first_chunks, second_chunks], [first, second]
    got.append(spread(0))

    known = jnp.asarray(np.array(table, np.int32))
    found = jnp.concatenate(half, axis=0)
    same = jnp.all(found[None, :, :] == known[:, None, :], axis=2)
    spot = jnp.arange(group * ops, dtype=jnp.int32)[None, :]
    places = jnp.min(jnp.where(same, spot, group * ops), axis=1).astype(jnp.int32)
    vrows = lax.dynamic_slice_in_dim(couple_v, row_at * rows, rows, 1)[:, :, None]
    vcols = lax.dynamic_slice_in_dim(couple_v, own * width, width, 1)
    heres = [vrows[:, p * height : (p + 1) * height] for p in range(split)]
    decay = jnp.sum(occupation.astype(f32) * damping[None, :], axis=1)
    blocks = hamiltonian.reshape(2, rows, row, split, height)
    h_columns = [blocks[:, :, :, p].reshape(2, rows, row * height) for p in range(split)]
    got, chunks, sections, places, heres, vcols, decay, h_columns, h_top, h_near = tie(
        (got, chunks, sections, places, heres, vcols, decay, h_columns, h_top, h_near)
    )

    sent.append(partial(0))
    received.append(swap(sent[0], "hier", hier, group))
    got.append(spread(1))
    across = swap(sections[0], "row", row, top)
    got, received, across, sections, h_top, h_near = tie(
        (got, received, across, sections, h_top, h_near)
    )

    sent.append(partial(1))
    received.append(swap(sent[1], "hier", hier, group))
    last_across = swap(sections[1], "row", row, top)
    s_parts = joined(tree(sections[0], row, low), across)
    h_parts = joined(h_near, h_top)
    done, s_parts, h_parts = tie((coupled(0), s_parts, h_parts))
    sums.append(gather_back(done))
    base = make_right(sections, h_parts, row_place, decay)
    base = make_left(s_parts, h_columns[0], base, row_place)
    received, last_across, sums, base, sections = tie(
        (received, last_across, sums, base, sections)
    )

    s_parts = joined(tree(sections[1], row, low), last_across)
    sums.append(gather_back(coupled(1)))
    base = make_left(s_parts, h_columns[1], base, row_place)
    for p in range(split):
        outs = make_final(p, split, base, accumulated, sums[p], own_place, outs)
    slope, total = outs
    return slope, total


def solution(mesh):
    return jax.shard_map(
        functools.partial(shards, mesh.shape["hier"], mesh.shape["row"]),
        mesh=mesh,
        in_specs=(
            P("hier", None, "row", None),
            P("hier", None, "row", None),
            P("hier", None, "row", None),
            P(None, "row", None),
            P(),
            P(),
            P(),
            P("hier", None),
            P("hier", None),
            P("hier", None),
        ),
        out_specs=(P("hier", None, "row", None), P("hier", None, "row", None)),
        check_vma=False,
    )
```

```python
import functools

import jax
import jax.numpy as jnp
import numpy as np
from jax import lax
from jax.experimental import pallas as pl
from jax.experimental.pallas import tpu as pltpu
from jax.sharding import PartitionSpec as P

step_size = 0.5
highest_total = 4
row_tile = 16
pieces = 2
MIB = 1024 * 1024
f32 = jnp.float32
bf16 = jnp.bfloat16


def index_rows(slots, modes):
    entries = [()]
    for _ in range(modes):
        entries = [
            entry + (level,)
            for entry in entries
            for level in range(highest_total + 1)
            if sum(entry) + level <= highest_total
        ]
    return sorted(entries, key=lambda entry: (sum(entry), entry))[:slots]


def coupled_to(rows):
    lookup = {entry: place for place, entry in enumerate(rows)}
    result = []
    for entry in rows:
        terms = []
        for mode, level in enumerate(entry):
            raised = entry[:mode] + (level + 1,) + entry[mode + 1 :]
            if raised in lookup:
                terms.append((lookup[raised], mode, True, 1))
            if level > 0:
                lowered = entry[:mode] + (level - 1,) + entry[mode + 1 :]
                terms.append((lookup[lowered], mode, False, level))
        result.append(terms)
    return result


def smaller_class(rows):
    classes = [[c for c, entry in enumerate(rows) if sum(entry) % 2 == rest] for rest in (0, 1)]
    return min(classes, key=len)


def params(megabytes):
    return pltpu.CompilerParams(vmem_limit_bytes=megabytes * MIB)


def whole():
    return pl.BlockSpec(memory_space=pltpu.VMEM)


def anywhere():
    return pl.BlockSpec(memory_space=pl.ANY)


def scalars():
    return pl.BlockSpec(memory_space=pltpu.SMEM)


def swap(array, axis, size, bit):
    return lax.ppermute(array, axis, [(i, i ^ bit) for i in range(size)])


def tie(arrays):
    return lax.optimization_barrier(arrays)


def row_bits(size):
    return [1 << i for i in reversed(range(size.bit_length() - 1))]


def tree(array, size, bits):
    parts = {0: array}
    for bit in bits:
        for mask in list(parts):
            parts[mask ^ bit] = swap(parts[mask], "row", size, bit)
    return parts


def section_kernel(where, state, slope, section, *chunks):
    value = (state[...].astype(f32) + (0.5 * step_size) * slope[...]).astype(bf16)
    section[...] = value
    width = chunks[0].shape[-1]
    for b, chunk in enumerate(chunks):
        columns = pl.ds(pl.multiple_of((where[0] ^ b) * width, 128), width)
        chunk[...] = section[:, :, :, columns]


def make_section(p, split, state, prev_slope, place, group):
    ops, parts, rows, columns = state.shape
    height, width = rows // split, columns // group
    block = pl.BlockSpec((1, parts, height, columns), lambda a, _: (a, 0, p, 0))
    out = pl.BlockSpec((1, parts, height, columns), lambda a, _: (a, 0, 0, 0))
    chunk = pl.BlockSpec((1, parts, height, width), lambda a, _: (a, 0, 0, 0))
    section, *chunks = pl.pallas_call(
        section_kernel,
        grid_spec=pltpu.PrefetchScalarGridSpec(
            num_scalar_prefetch=1,
            grid=(ops,),
            in_specs=[block, block],
            out_specs=[out] + [chunk] * group,
        ),
        out_shape=[jax.ShapeDtypeStruct((ops, parts, height, columns), bf16)]
        + [jax.ShapeDtypeStruct((ops, parts, height, width), bf16)] * group,
        compiler_params=params(60),
        cost_estimate=pl.CostEstimate(flops=1, bytes_accessed=1, transcendentals=0),
        name="section",
    )(place, state, prev_slope)
    return section, chunks


def fill_factors(vrows, vcols, coupling, factors):
    modes = vrows.shape[0]
    for k in range(modes):
        first = vrows[k]
        second = vcols[k : k + 1, :]
        diff = first - second
        factors[k] = diff
        factors[modes + k] = coupling[0, k] * diff
        factors[2 * modes + k] = coupling[1, k] * (first + second)


def add_terms(terms, places, held, factors, modes, rows, real, imag):
    for other, mode, child, count in terms:
        place = places[other]
        x_real = held[place, 0, rows, :].astype(f32)
        x_imag = held[place, 1, rows, :].astype(f32)
        if child:
            diff = factors[mode, rows, :]
            real = real + diff * x_imag
            imag = imag - diff * x_real
        else:
            first = factors[modes + mode, rows, :]
            second = factors[2 * modes + mode, rows, :]
            if count != 1:
                first, second = count * first, count * second
            real = real + (first * x_imag + second * x_real)
            imag = imag + (second * x_imag - first * x_real)
    return real, imag


def partial_kernel(links, sides, group, places, coupling, vrows, vcols, *refs):
    chunks, out, held, factors, sems = refs[:group], *refs[group:]
    modes = vrows.shape[0]
    height, width = held.shape[2:]
    ops = chunks[0].shape[0]
    empty = group * ops
    loads = [
        pltpu.make_async_copy(chunk, held.at[pl.ds(b * ops, ops)], sems.at[b])
        for b, chunk in enumerate(chunks)
    ]
    for load in loads:
        load.start()
    fill_factors(vrows, vcols, coupling, factors)
    held[empty] = jnp.zeros(held.shape[1:], bf16)
    for load in loads:
        load.wait()
    for u, c in enumerate(sides):

        @pl.when(places[c] < empty)
        def _():
            out[u] = held[places[c]]

        @pl.when(places[c] == empty)
        def _():
            @pl.loop(0, height // row_tile)
            def _(i):
                rows = pl.ds(pl.multiple_of(i * row_tile, row_tile), row_tile)
                zero = jnp.zeros((row_tile, width), f32)
                real, imag = add_terms(links[c], places, held, factors, modes, rows, zero, zero)
                out[u, 0, rows, :] = real.astype(bf16)
                out[u, 1, rows, :] = imag.astype(bf16)


def coupled_kernel(links, sides, group, places, coupling, vrows, vcols, *refs):
    chunks, received, outs = refs[:group], refs[group], refs[group + 1 : 2 * group + 1]
    held, done, factors, spots, sems = refs[2 * group + 1 :]
    modes = vrows.shape[0]
    height, width = held.shape[2:]
    ops = chunks[0].shape[0]
    empty = group * ops
    loads = [
        pltpu.make_async_copy(chunk, held.at[pl.ds(b * ops, ops)], sems.at[b])
        for b, chunk in enumerate(chunks)
    ]
    loads.append(
        pltpu.make_async_copy(received, held.at[pl.ds(empty + 1, len(sides))], sems.at[group])
    )
    for load in loads:
        load.start()
    fill_factors(vrows, vcols, coupling, factors)
    held[empty] = jnp.zeros(held.shape[1:], bf16)
    for c in range(len(links)):
        spots[c] = places[c]
    for u, c in enumerate(sides):
        spots[c] = jnp.where(places[c] == empty, empty + 1 + u, places[c])
    for load in loads:
        load.wait()
    for c in range(len(links)):

        @pl.when(places[c] < empty)
        def _():
            @pl.loop(0, height // row_tile)
            def _(i):
                rows = pl.ds(pl.multiple_of(i * row_tile, row_tile), row_tile)
                if c in sides:
                    u = empty + 1 + sides.index(c)
                    real, imag = held[u, 0, rows, :].astype(f32), held[u, 1, rows, :].astype(f32)
                else:
                    real = imag = jnp.zeros((row_tile, width), f32)
                real, imag = add_terms(links[c], spots, held, factors, modes, rows, real, imag)
                done[places[c], 0, rows, :] = real.astype(bf16)
                done[places[c], 1, rows, :] = imag.astype(bf16)

    stores = [
        pltpu.make_async_copy(done.at[pl.ds(b * ops, ops)], out, sems.at[group + 1 + b])
        for b, out in enumerate(outs)
    ]
    for store in stores:
        store.start()
    for store in stores:
        store.wait()


def coupling_scratch(entries, height, width, modes):
    return [pltpu.VMEM((entries, 2, height, width), bf16)], [pltpu.VMEM((3 * modes, height, width), f32)]


def make_partial(chunks, places, coupling, vrows, vcols, links, sides):
    group = len(chunks)
    ops, _, height, width = chunks[0].shape
    held, factors = coupling_scratch(group * ops + 1, height, width, vrows.shape[0])
    size = height * width
    return pl.pallas_call(
        functools.partial(partial_kernel, links, sides, group),
        in_specs=[scalars(), scalars()] + [whole()] * 2 + [anywhere()] * group,
        out_specs=whole(),
        out_shape=jax.ShapeDtypeStruct((len(sides), 2, height, width), bf16),
        scratch_shapes=held + factors + [pltpu.SemaphoreType.DMA((group,))],
        compiler_params=params(60),
        cost_estimate=pl.CostEstimate(
            flops=40 * len(sides) * size,
            bytes_accessed=4 * size * (group * ops + len(sides)),
            transcendentals=0,
        ),
        name="partial_sums",
    )(places, coupling, vrows, vcols, *chunks)


def make_coupled(chunks, received, places, coupling, vrows, vcols, links, sides):
    group = len(chunks)
    ops, _, height, width = chunks[0].shape
    held, factors = coupling_scratch(group * ops + 1 + len(sides), height, width, vrows.shape[0])
    size = height * width
    return pl.pallas_call(
        functools.partial(coupled_kernel, links, sides, group),
        in_specs=[scalars(), scalars()] + [whole()] * 2 + [anywhere()] * (1 + group),
        out_specs=[anywhere()] * group,
        out_shape=[jax.ShapeDtypeStruct(chunks[0].shape, bf16)] * group,
        scratch_shapes=held
        + [pltpu.VMEM((group * ops, 2, height, width), bf16)]
        + factors
        + [pltpu.SMEM((len(links),), jnp.int32), pltpu.SemaphoreType.DMA((2 * group + 1,))],
        compiler_params=params(60),
        cost_estimate=pl.CostEstimate(
            flops=40 * group * ops * size,
            bytes_accessed=4 * size * (2 * group * ops + len(sides)),
            transcendentals=0,
        ),
        name="coupling_sums",
    )(places, coupling, vrows, vcols, *chunks, received)


def complex_rows(left, right):
    _, height, depth = left.shape
    left = left.reshape(2 * height, depth)
    first = jnp.dot(left, right[0], preferred_element_type=f32)
    second = jnp.dot(left, right[1], preferred_element_type=f32)
    return first[:height] - second[height:], second[:height] + first[height:]


def right_kernel(split, count, where, decay, *refs):
    sections, h_parts, (out, h_all) = refs[:split], refs[split:-2], refs[-2:]
    j, a = pl.program_id(0), pl.program_id(1)
    rows, tile = h_parts[0].shape[1:]
    height = sections[0].shape[2]

    @pl.when(a == 0)
    def _():
        for b in range(count):
            place = pl.ds(pl.multiple_of((where[0] ^ b) * rows, row_tile), rows)
            h_all[:, place, :] = h_parts[b][...]

    columns = pl.ds(pl.multiple_of(j * tile, 128), tile)
    lost = decay[a]
    for p, section in enumerate(sections):
        real, imag = complex_rows(section[a], h_all)
        here = slice(p * height, (p + 1) * height)
        out[0, 0, here, :] = -imag - lost * section[a, 0, :, columns].astype(f32)
        out[0, 1, here, :] = real - lost * section[a, 1, :, columns].astype(f32)


def make_right(sections, h_parts, place, decay):
    ops, _, height, columns = sections[0].shape
    split, count = len(sections), len(h_parts)
    rows, tile = height * split, min(columns, 256)
    held = pl.BlockSpec((ops, 2, height, columns), lambda j, a: (0, 0, 0, 0))
    return pl.pallas_call(
        functools.partial(right_kernel, split, count),
        grid=(columns // tile, ops),
        in_specs=[scalars(), scalars()]
        + [held] * split
        + [pl.BlockSpec((2, rows, tile), lambda j, a: (0, 0, j))] * count,
        out_specs=pl.BlockSpec((1, 2, rows, tile), lambda j, a: (a, 0, 0, j)),
        out_shape=jax.ShapeDtypeStruct((ops, 2, rows, columns), f32),
        scratch_shapes=[pltpu.VMEM((2, count * rows, tile), bf16)],
        compiler_params=params(60),
        cost_estimate=pl.CostEstimate(
            flops=8 * ops * rows * columns * columns,
            bytes_accessed=4 * columns * (columns + 3 * ops * rows),
            transcendentals=0,
        ),
        name="right_products",
    )(place, decay, *sections, *h_parts)


def left_kernel(count, where, h_own, base, *refs):
    s_parts, (out, s_all) = refs[:count], refs[count:]
    height = s_parts[0].shape[2]
    for b in range(count):
        place = pl.ds(pl.multiple_of((where[0] ^ b) * height, row_tile), height)
        s_all[:, place, :] = s_parts[b][0]
    real, imag = complex_rows(h_own[...], s_all)
    out[0, 0] = base[0, 0] + imag
    out[0, 1] = base[0, 1] - real


def make_left(s_parts, h_columns, base, place):
    ops, _, height, columns = s_parts[0].shape
    count, rows, tile = len(s_parts), base.shape[2], min(columns, 256)
    block = pl.BlockSpec((1, 2, rows, tile), lambda j, a: (a, 0, 0, j))
    return pl.pallas_call(
        functools.partial(left_kernel, count),
        grid=(columns // tile, ops),
        in_specs=[
            scalars(),
            pl.BlockSpec(h_columns.shape, lambda j, a: (0, 0, 0)),
            block,
        ]
        + [pl.BlockSpec((1, 2, height, tile), lambda j, a: (a, 0, 0, j))] * count,
        out_specs=block,
        out_shape=jax.ShapeDtypeStruct(base.shape, f32),
        scratch_shapes=[pltpu.VMEM((2, count * height, tile), bf16)],
        compiler_params=params(60),
        cost_estimate=pl.CostEstimate(
            flops=8 * ops * rows * columns * count * height,
            bytes_accessed=4 * ops * columns * (count * height + 4 * rows),
            transcendentals=0,
        ),
        name="left_products",
    )(place, h_columns, base, *s_parts)


def final_kernel(group, count, where, h_own, base, accumulated, *refs):
    s_parts, sums = refs[:count], refs[count : count + group]
    slope, total, s_all = refs[-3:]
    a, j = pl.program_id(0), pl.program_id(1)
    height, tile, width = s_parts[0].shape[2], slope.shape[3], sums[0].shape[3]
    for b in range(count):
        place = pl.ds(pl.multiple_of((where[1] ^ b) * height, row_tile), height)
        s_all[:, place, :] = s_parts[b][0]
    real, imag = complex_rows(h_own[...], s_all)
    slope[0, 0] = base[0, 0] + imag
    slope[0, 1] = base[0, 1] - real
    for b in range(group):
        first = (where[0] ^ b) * width - j * tile

        @pl.when(jnp.logical_and(first >= 0, first < tile))
        def _():
            columns = pl.ds(pl.multiple_of(first, 128), width)
            slope[0, :, :, columns] += sums[b][a].astype(f32)

    total[...] = accumulated[...] + (step_size / 3.0) * slope[...]


def make_final(p, split, base, accumulated, s_parts, h_columns, sums, places, earlier=()):
    ops, parts, rows, columns = base.shape
    group, count = len(sums), len(s_parts)
    height, tile = rows // split, min(columns, 256)
    block = pl.BlockSpec((1, parts, height, tile), lambda a, j, _: (a, 0, p, j))
    held = pl.BlockSpec(sums[0].shape, lambda a, j, _: (0, 0, 0, 0))
    own = pl.BlockSpec((2, height, h_columns.shape[2]), lambda a, j, _: (0, p, 0))
    part = pl.BlockSpec((1, parts, height, tile), lambda a, j, _: (a, 0, 0, j))
    inputs = [own, block, block] + [part] * count + [held] * group
    return pl.pallas_call(
        lambda *refs: final_kernel(
            group, count, *refs[: 1 + len(inputs)], *refs[1 + len(inputs) + len(earlier) :]
        ),
        grid_spec=pltpu.PrefetchScalarGridSpec(
            num_scalar_prefetch=1,
            grid=(ops, columns // tile),
            in_specs=inputs + [anywhere()] * len(earlier),
            out_specs=[block, block],
            scratch_shapes=[pltpu.VMEM((2, count * height, tile), bf16)],
        ),
        out_shape=[jax.ShapeDtypeStruct(base.shape, f32)] * 2,
        input_output_aliases={1 + len(inputs) + k: k for k in range(len(earlier))},
        compiler_params=params(60),
        cost_estimate=pl.CostEstimate(
            flops=8 * ops * height * columns * count * height,
            bytes_accessed=36 * base.size // split,
            transcendentals=0,
        ),
        name="outputs",
    )(places, h_columns, base, accumulated, *s_parts, *sums, *earlier)


def shards(
    hier,
    row,
    state,
    prev_slope,
    accumulated,
    hamiltonian,
    couple_v,
    coupling,
    damping,
    occupation,
    parents,
    children,
):
    ops, _, rows, columns = state.shape
    modes = occupation.shape[1]
    group = hier // 2
    width = columns // group
    split = pieces
    height = rows // split
    table = index_rows(hier * ops, modes)
    links, sides = coupled_to(table), smaller_class(table)

    hier_at, row_at = lax.axis_index("hier"), lax.axis_index("row")
    own = hier_at % group
    own_place, row_place = own.reshape(1).astype(jnp.int32), row_at.reshape(1).astype(jnp.int32)

    bits = row_bits(row)
    top, low = bits[0], bits[1:]

    def spread(p):
        return [chunks[p][0]] + [swap(chunks[p][b], "hier", hier, b) for b in range(1, group)]

    def partial(p):
        return make_partial(got[p], places, coupling, heres[p], vcols, links, sides)

    def coupled(p):
        return make_coupled(got[p], received[p], places, coupling, heres[p], vcols, links, sides)

    def gather_back(done):
        return [done[0]] + [swap(done[b], "hier", hier, b) for b in range(1, group)]

    def joined(near, across):
        far = {mask ^ top: part for mask, part in tree(across, row, low).items()}
        parts = {**near, **far}
        return [parts[b] for b in range(row)]

    got, sent, received, sums, outs = [], [], [], [], []

    half = [occupation] + [swap(occupation, "hier", hier, b) for b in range(1, group)]
    first, first_chunks = make_section(0, split, state, prev_slope, own_place, group)
    first, first_chunks, half, state, prev_slope, couple_v, hamiltonian = tie(
        (first, first_chunks, half, state, prev_slope, couple_v, hamiltonian)
    )

    h_top, h_near = swap(hamiltonian, "row", row, top), tree(hamiltonian, row, low)
    second, second_chunks = make_section(1, split, state, prev_slope, own_place, group)
    chunks, sections = [first_chunks, second_chunks], [first, second]
    got.append(spread(0))

    known = jnp.asarray(np.array(table, np.int32))
    found = jnp.concatenate(half, axis=0)
    same = jnp.all(found[None, :, :] == known[:, None, :], axis=2)
    spot = jnp.arange(group * ops, dtype=jnp.int32)[None, :]
    places = jnp.min(jnp.where(same, spot, group * ops), axis=1).astype(jnp.int32)
    vrows = lax.dynamic_slice_in_dim(couple_v, row_at * rows, rows, 1)[:, :, None]
    vcols = lax.dynamic_slice_in_dim(couple_v, own * width, width, 1)
    heres = [vrows[:, p * height : (p + 1) * height] for p in range(split)]
    decay = jnp.sum(occupation.astype(f32) * damping[None, :], axis=1)
    blocks = hamiltonian.reshape(2, rows, row, split, height)
    h_columns = [blocks[:, :, :, p].reshape(2, rows, row * height) for p in range(split)]
    got, chunks, sections, places, heres, vcols, decay, h_columns, h_top, h_near = tie(
        (got, chunks, sections, places, heres, vcols, decay, h_columns, h_top, h_near)
    )

    sent.append(partial(0))
    received.append(swap(sent[0], "hier", hier, group))
    got.append(spread(1))
    across = swap(sections[0], "row", row, top)
    got, received, across, sections, h_top, h_near = tie(
        (got, received, across, sections, h_top, h_near)
    )

    sent.append(partial(1))
    received.append(swap(sent[1], "hier", hier, group))
    last_across = swap(sections[1], "row", row, top)
    s_parts = joined(tree(sections[0], row, low), across)
    h_parts = joined(h_near, h_top)
    done, s_parts, h_parts = tie((coupled(0), s_parts, h_parts))
    sums.append(gather_back(done))
    base = make_right(sections, h_parts, row_place, decay)
    base = make_left(s_parts, h_columns[0], base, row_place)
    received, last_across, sums, base, sections = tie(
        (received, last_across, sums, base, sections)
    )

    s_parts = joined(tree(sections[1], row, low), last_across)
    sums.append(gather_back(coupled(1)))
    both = jnp.concatenate([own_place, row_place])
    for p in range(split):
        outs = make_final(
            p, split, base, accumulated, s_parts, h_columns[1], sums[p], both, outs
        )
    slope, total = outs
    return slope, total


def solution(mesh):
    return jax.shard_map(
        functools.partial(shards, mesh.shape["hier"], mesh.shape["row"]),
        mesh=mesh,
        in_specs=(
            P("hier", None, "row", None),
            P("hier", None, "row", None),
            P("hier", None, "row", None),
            P(None, "row", None),
            P(),
            P(),
            P(),
            P("hier", None),
            P("hier", None),
            P("hier", None),
        ),
        out_specs=(P("hier", None, "row", None), P("hier", None, "row", None)),
        check_vma=False,
    )
```

```python
import functools

import jax
import jax.numpy as jnp
import numpy as np
from jax import lax
from jax.experimental import pallas as pl
from jax.experimental.pallas import tpu as pltpu
from jax.sharding import PartitionSpec as P

step_size = 0.5
highest_total = 4
row_tile = 16
pieces = 2
MIB = 1024 * 1024
f32 = jnp.float32
bf16 = jnp.bfloat16


def index_rows(slots, modes):
    entries = [()]
    for _ in range(modes):
        entries = [
            entry + (level,)
            for entry in entries
            for level in range(highest_total + 1)
            if sum(entry) + level <= highest_total
        ]
    return sorted(entries, key=lambda entry: (sum(entry), entry))[:slots]


def coupled_to(rows):
    lookup = {entry: place for place, entry in enumerate(rows)}
    result = []
    for entry in rows:
        terms = []
        for mode, level in enumerate(entry):
            raised = entry[:mode] + (level + 1,) + entry[mode + 1 :]
            if raised in lookup:
                terms.append((lookup[raised], mode, True, 1))
            if level > 0:
                lowered = entry[:mode] + (level - 1,) + entry[mode + 1 :]
                terms.append((lookup[lowered], mode, False, level))
        result.append(terms)
    return result


def smaller_class(rows):
    classes = [[c for c, entry in enumerate(rows) if sum(entry) % 2 == rest] for rest in (0, 1)]
    return min(classes, key=len)


def params(megabytes):
    return pltpu.CompilerParams(vmem_limit_bytes=megabytes * MIB)


def whole():
    return pl.BlockSpec(memory_space=pltpu.VMEM)


def anywhere():
    return pl.BlockSpec(memory_space=pl.ANY)


def scalars():
    return pl.BlockSpec(memory_space=pltpu.SMEM)


def swap(array, axis, size, bit):
    return lax.ppermute(array, axis, [(i, i ^ bit) for i in range(size)])


def tie(arrays):
    return lax.optimization_barrier(arrays)


def row_bits(size):
    return [1 << i for i in reversed(range(size.bit_length() - 1))]


def tree(array, size, bits):
    parts = {0: array}
    for bit in bits:
        for mask in list(parts):
            parts[mask ^ bit] = swap(parts[mask], "row", size, bit)
    return parts


def section_kernel(where, state, slope, section, *chunks):
    value = (state[...].astype(f32) + (0.5 * step_size) * slope[...]).astype(bf16)
    section[...] = value
    width = chunks[0].shape[-1]
    for b, chunk in enumerate(chunks):
        columns = pl.ds(pl.multiple_of((where[0] ^ b) * width, 128), width)
        chunk[...] = section[:, :, :, columns]


def make_section(p, split, state, prev_slope, place, group):
    ops, parts, rows, columns = state.shape
    height, width = rows // split, columns // group
    block = pl.BlockSpec((1, parts, height, columns), lambda a, _: (a, 0, p, 0))
    out = pl.BlockSpec((1, parts, height, columns), lambda a, _: (a, 0, 0, 0))
    chunk = pl.BlockSpec((1, parts, height, width), lambda a, _: (a, 0, 0, 0))
    section, *chunks = pl.pallas_call(
        section_kernel,
        grid_spec=pltpu.PrefetchScalarGridSpec(
            num_scalar_prefetch=1,
            grid=(ops,),
            in_specs=[block, block],
            out_specs=[out] + [chunk] * group,
        ),
        out_shape=[jax.ShapeDtypeStruct((ops, parts, height, columns), bf16)]
        + [jax.ShapeDtypeStruct((ops, parts, height, width), bf16)] * group,
        compiler_params=params(60 if p == 0 else 16),
        cost_estimate=pl.CostEstimate(flops=1, bytes_accessed=1, transcendentals=0),
        name="section",
    )(place, state, prev_slope)
    return section, chunks


def fill_factors(vrows, vcols, coupling, factors):
    modes = vrows.shape[0]
    for k in range(modes):
        first = vrows[k]
        second = vcols[k : k + 1, :]
        diff = first - second
        factors[k] = diff
        factors[modes + k] = coupling[0, k] * diff
        factors[2 * modes + k] = coupling[1, k] * (first + second)


def add_terms(terms, places, held, factors, modes, rows, real, imag):
    for other, mode, child, count in terms:
        place = places[other]
        x_real = held[place, 0, rows, :].astype(f32)
        x_imag = held[place, 1, rows, :].astype(f32)
        if child:
            diff = factors[mode, rows, :]
            real = real + diff * x_imag
            imag = imag - diff * x_real
        else:
            first = factors[modes + mode, rows, :]
            second = factors[2 * modes + mode, rows, :]
            if count != 1:
                first, second = count * first, count * second
            real = real + (first * x_imag + second * x_real)
            imag = imag + (second * x_imag - first * x_real)
    return real, imag


def partial_kernel(links, sides, group, places, coupling, vrows, vcols, *refs):
    chunks, out, held, factors, sems = refs[:group], *refs[group:]
    modes = vrows.shape[0]
    height, width = held.shape[2:]
    ops = chunks[0].shape[0]
    empty = group * ops
    loads = [
        pltpu.make_async_copy(chunk, held.at[pl.ds(b * ops, ops)], sems.at[b])
        for b, chunk in enumerate(chunks)
    ]
    for load in loads:
        load.start()
    fill_factors(vrows, vcols, coupling, factors)
    held[empty] = jnp.zeros(held.shape[1:], bf16)
    for load in loads:
        load.wait()
    for u, c in enumerate(sides):

        @pl.when(places[c] < empty)
        def _():
            out[u] = held[places[c]]

        @pl.when(places[c] == empty)
        def _():
            @pl.loop(0, height // row_tile)
            def _(i):
                rows = pl.ds(pl.multiple_of(i * row_tile, row_tile), row_tile)
                zero = jnp.zeros((row_tile, width), f32)
                real, imag = add_terms(links[c], places, held, factors, modes, rows, zero, zero)
                out[u, 0, rows, :] = real.astype(bf16)
                out[u, 1, rows, :] = imag.astype(bf16)


def coupled_kernel(links, sides, group, places, coupling, vrows, vcols, *refs):
    chunks, received, outs = refs[:group], refs[group], refs[group + 1 : 2 * group + 1]
    held, done, factors, spots, sems = refs[2 * group + 1 :]
    modes = vrows.shape[0]
    height, width = held.shape[2:]
    ops = chunks[0].shape[0]
    empty = group * ops
    loads = [
        pltpu.make_async_copy(chunk, held.at[pl.ds(b * ops, ops)], sems.at[b])
        for b, chunk in enumerate(chunks)
    ]
    loads.append(
        pltpu.make_async_copy(received, held.at[pl.ds(empty + 1, len(sides))], sems.at[group])
    )
    for load in loads:
        load.start()
    fill_factors(vrows, vcols, coupling, factors)
    held[empty] = jnp.zeros(held.shape[1:], bf16)
    for c in range(len(links)):
        spots[c] = places[c]
    for u, c in enumerate(sides):
        spots[c] = jnp.where(places[c] == empty, empty + 1 + u, places[c])
    for load in loads:
        load.wait()
    for c in range(len(links)):

        @pl.when(places[c] < empty)
        def _():
            @pl.loop(0, height // row_tile)
            def _(i):
                rows = pl.ds(pl.multiple_of(i * row_tile, row_tile), row_tile)
                if c in sides:
                    u = empty + 1 + sides.index(c)
                    real, imag = held[u, 0, rows, :].astype(f32), held[u, 1, rows, :].astype(f32)
                else:
                    real = imag = jnp.zeros((row_tile, width), f32)
                real, imag = add_terms(links[c], spots, held, factors, modes, rows, real, imag)
                done[places[c], 0, rows, :] = real.astype(bf16)
                done[places[c], 1, rows, :] = imag.astype(bf16)

    stores = [
        pltpu.make_async_copy(done.at[pl.ds(b * ops, ops)], out, sems.at[group + 1 + b])
        for b, out in enumerate(outs)
    ]
    for store in stores:
        store.start()
    for store in stores:
        store.wait()


def coupling_scratch(entries, height, width, modes):
    return [pltpu.VMEM((entries, 2, height, width), bf16)], [pltpu.VMEM((3 * modes, height, width), f32)]


def make_partial(chunks, places, coupling, vrows, vcols, links, sides):
    group = len(chunks)
    ops, _, height, width = chunks[0].shape
    held, factors = coupling_scratch(group * ops + 1, height, width, vrows.shape[0])
    size = height * width
    return pl.pallas_call(
        functools.partial(partial_kernel, links, sides, group),
        in_specs=[scalars(), scalars()] + [whole()] * 2 + [anywhere()] * group,
        out_specs=whole(),
        out_shape=jax.ShapeDtypeStruct((len(sides), 2, height, width), bf16),
        scratch_shapes=held + factors + [pltpu.SemaphoreType.DMA((group,))],
        compiler_params=params(12),
        cost_estimate=pl.CostEstimate(
            flops=40 * len(sides) * size,
            bytes_accessed=4 * size * (group * ops + len(sides)),
            transcendentals=0,
        ),
        name="partial_sums",
    )(places, coupling, vrows, vcols, *chunks)


def make_coupled(chunks, received, places, coupling, vrows, vcols, links, sides):
    group = len(chunks)
    ops, _, height, width = chunks[0].shape
    held, factors = coupling_scratch(group * ops + 1 + len(sides), height, width, vrows.shape[0])
    size = height * width
    return pl.pallas_call(
        functools.partial(coupled_kernel, links, sides, group),
        in_specs=[scalars(), scalars()] + [whole()] * 2 + [anywhere()] * (1 + group),
        out_specs=[anywhere()] * group,
        out_shape=[jax.ShapeDtypeStruct(chunks[0].shape, bf16)] * group,
        scratch_shapes=held
        + [pltpu.VMEM((group * ops, 2, height, width), bf16)]
        + factors
        + [pltpu.SMEM((len(links),), jnp.int32), pltpu.SemaphoreType.DMA((2 * group + 1,))],
        compiler_params=params(16),
        cost_estimate=pl.CostEstimate(
            flops=40 * group * ops * size,
            bytes_accessed=4 * size * (2 * group * ops + len(sides)),
            transcendentals=0,
        ),
        name="coupling_sums",
    )(places, coupling, vrows, vcols, *chunks, received)


def complex_rows(left, right):
    _, height, depth = left.shape
    left = left.reshape(2 * height, depth)
    first = jnp.dot(left, right[0], preferred_element_type=f32)
    second = jnp.dot(left, right[1], preferred_element_type=f32)
    return first[:height] - second[height:], second[:height] + first[height:]


def right_kernel(split, count, where, decay, *refs):
    sections, h_parts, (out, h_all) = refs[:split], refs[split:-2], refs[-2:]
    j, a = pl.program_id(0), pl.program_id(1)
    rows, tile = h_parts[0].shape[1:]
    height = sections[0].shape[2]

    @pl.when(a == 0)
    def _():
        for b in range(count):
            place = pl.ds(pl.multiple_of((where[0] ^ b) * rows, row_tile), rows)
            h_all[:, place, :] = h_parts[b][...]

    columns = pl.ds(pl.multiple_of(j * tile, 128), tile)
    lost = decay[a]
    for p, section in enumerate(sections):
        real, imag = complex_rows(section[a], h_all)
        here = slice(p * height, (p + 1) * height)
        out[0, 0, here, :] = -imag - lost * section[a, 0, :, columns].astype(f32)
        out[0, 1, here, :] = real - lost * section[a, 1, :, columns].astype(f32)


def make_right(sections, h_parts, place, decay):
    ops, _, height, columns = sections[0].shape
    split, count = len(sections), len(h_parts)
    rows, tile = height * split, min(columns, 512)
    held = pl.BlockSpec((ops, 2, height, columns), lambda j, a: (0, 0, 0, 0))
    return pl.pallas_call(
        functools.partial(right_kernel, split, count),
        grid=(columns // tile, ops),
        in_specs=[scalars(), scalars()]
        + [held] * split
        + [pl.BlockSpec((2, rows, tile), lambda j, a: (0, 0, j))] * count,
        out_specs=pl.BlockSpec((1, 2, rows, tile), lambda j, a: (a, 0, 0, j)),
        out_shape=jax.ShapeDtypeStruct((ops, 2, rows, columns), f32),
        scratch_shapes=[pltpu.VMEM((2, count * rows, tile), bf16)],
        compiler_params=params(24),
        cost_estimate=pl.CostEstimate(
            flops=8 * ops * rows * columns * columns,
            bytes_accessed=4 * columns * (columns + 3 * ops * rows),
            transcendentals=0,
        ),
        name="right_products",
    )(place, decay, *sections, *h_parts)


def left_kernel(count, where, h_own, base, *refs):
    s_parts, (out, s_all) = refs[:count], refs[count:]
    height = s_parts[0].shape[2]
    for b in range(count):
        place = pl.ds(pl.multiple_of((where[0] ^ b) * height, row_tile), height)
        s_all[:, place, :] = s_parts[b][0]
    real, imag = complex_rows(h_own[...], s_all)
    out[0, 0] = base[0, 0] + imag
    out[0, 1] = base[0, 1] - real


def make_left(s_parts, h_columns, base, place):
    ops, _, height, columns = s_parts[0].shape
    count, rows, tile = len(s_parts), base.shape[2], min(columns, 512)
    block = pl.BlockSpec((1, 2, rows, tile), lambda j, a: (a, 0, 0, j))
    return pl.pallas_call(
        functools.partial(left_kernel, count),
        grid=(columns // tile, ops),
        in_specs=[
            scalars(),
            pl.BlockSpec(h_columns.shape, lambda j, a: (0, 0, 0)),
            block,
        ]
        + [pl.BlockSpec((1, 2, height, tile), lambda j, a: (a, 0, 0, j))] * count,
        out_specs=block,
        out_shape=jax.ShapeDtypeStruct(base.shape, f32),
        scratch_shapes=[pltpu.VMEM((2, count * height, tile), bf16)],
        compiler_params=params(16),
        cost_estimate=pl.CostEstimate(
            flops=8 * ops * rows * columns * count * height,
            bytes_accessed=4 * ops * columns * (count * height + 4 * rows),
            transcendentals=0,
        ),
        name="left_products",
    )(place, h_columns, base, *s_parts)


def final_kernel(group, count, where, h_own, base, accumulated, *refs):
    s_parts, sums = refs[:count], refs[count : count + group]
    slope, total, s_all = refs[-3:]
    a, j = pl.program_id(0), pl.program_id(1)
    height, tile, width = s_parts[0].shape[2], slope.shape[3], sums[0].shape[3]
    for b in range(count):
        place = pl.ds(pl.multiple_of((where[1] ^ b) * height, row_tile), height)
        s_all[:, place, :] = s_parts[b][0]
    real, imag = complex_rows(h_own[...], s_all)
    slope[0, 0] = base[0, 0] + imag
    slope[0, 1] = base[0, 1] - real
    for b in range(group):
        first = (where[0] ^ b) * width - j * tile

        @pl.when(jnp.logical_and(first >= 0, first < tile))
        def _():
            columns = pl.ds(pl.multiple_of(first, 128), width)
            slope[0, :, :, columns] += sums[b][a].astype(f32)

    total[...] = accumulated[...] + (step_size / 3.0) * slope[...]


def make_final(p, split, base, accumulated, s_parts, h_columns, sums, places, earlier=()):
    ops, parts, rows, columns = base.shape
    group, count = len(sums), len(s_parts)
    height, tile = rows // split, min(columns, 512)
    block = pl.BlockSpec((1, parts, height, tile), lambda a, j, _: (a, 0, p, j))
    held = pl.BlockSpec(sums[0].shape, lambda a, j, _: (0, 0, 0, 0))
    own = pl.BlockSpec((2, height, h_columns.shape[2]), lambda a, j, _: (0, p, 0))
    part = pl.BlockSpec((1, parts, height, tile), lambda a, j, _: (a, 0, 0, j))
    inputs = [own, block, block] + [part] * count + [held] * group
    return pl.pallas_call(
        lambda *refs: final_kernel(
            group, count, *refs[: 1 + len(inputs)], *refs[1 + len(inputs) + len(earlier) :]
        ),
        grid_spec=pltpu.PrefetchScalarGridSpec(
            num_scalar_prefetch=1,
            grid=(ops, columns // tile),
            in_specs=inputs + [anywhere()] * len(earlier),
            out_specs=[block, block],
            scratch_shapes=[pltpu.VMEM((2, count * height, tile), bf16)],
        ),
        out_shape=[jax.ShapeDtypeStruct(base.shape, f32)] * 2,
        input_output_aliases={1 + len(inputs) + k: k for k in range(len(earlier))},
        compiler_params=params(16),
        cost_estimate=pl.CostEstimate(
            flops=8 * ops * height * columns * count * height,
            bytes_accessed=36 * base.size // split,
            transcendentals=0,
        ),
        name="outputs",
    )(places, h_columns, base, accumulated, *s_parts, *sums, *earlier)


def shards(
    hier,
    row,
    state,
    prev_slope,
    accumulated,
    hamiltonian,
    couple_v,
    coupling,
    damping,
    occupation,
    parents,
    children,
):
    ops, _, rows, columns = state.shape
    modes = occupation.shape[1]
    group = hier // 2
    width = columns // group
    split = pieces
    height = rows // split
    table = index_rows(hier * ops, modes)
    links, sides = coupled_to(table), smaller_class(table)

    hier_at, row_at = lax.axis_index("hier"), lax.axis_index("row")
    own = hier_at % group
    own_place, row_place = own.reshape(1).astype(jnp.int32), row_at.reshape(1).astype(jnp.int32)

    bits = row_bits(row)
    top, low = bits[0], bits[1:]

    def spread(p):
        return [chunks[p][0]] + [swap(chunks[p][b], "hier", hier, b) for b in range(1, group)]

    def partial(p):
        return make_partial(got[p], places, coupling, heres[p], vcols, links, sides)

    def coupled(p):
        return make_coupled(got[p], received[p], places, coupling, heres[p], vcols, links, sides)

    def gather_back(done):
        return [done[0]] + [swap(done[b], "hier", hier, b) for b in range(1, group)]

    def joined(near, across):
        far = {mask ^ top: part for mask, part in tree(across, row, low).items()}
        parts = {**near, **far}
        return [parts[b] for b in range(row)]

    got, sent, received, sums, outs = [], [], [], [], []

    half = [occupation] + [swap(occupation, "hier", hier, b) for b in range(1, group)]
    first, first_chunks = make_section(0, split, state, prev_slope, own_place, group)
    first, first_chunks, half, state, prev_slope, couple_v, hamiltonian = tie(
        (first, first_chunks, half, state, prev_slope, couple_v, hamiltonian)
    )

    h_top, h_near = swap(hamiltonian, "row", row, top), tree(hamiltonian, row, low)
    second, second_chunks = make_section(1, split, state, prev_slope, own_place, group)
    chunks, sections = [first_chunks, second_chunks], [first, second]
    got.append(spread(0))

    known = jnp.asarray(np.array(table, np.int32))
    found = jnp.concatenate(half, axis=0)
    same = jnp.all(found[None, :, :] == known[:, None, :], axis=2)
    spot = jnp.arange(group * ops, dtype=jnp.int32)[None, :]
    places = jnp.min(jnp.where(same, spot, group * ops), axis=1).astype(jnp.int32)
    vrows = lax.dynamic_slice_in_dim(couple_v, row_at * rows, rows, 1)[:, :, None]
    vcols = lax.dynamic_slice_in_dim(couple_v, own * width, width, 1)
    heres = [vrows[:, p * height : (p + 1) * height] for p in range(split)]
    decay = jnp.sum(half[0].astype(f32) * damping[None, :], axis=1)
    second, kept = tie((second, hamiltonian))
    sections[1] = second
    blocks = kept.reshape(2, rows, row, split, height)
    h_columns = [blocks[:, :, :, p].reshape(2, rows, row * height) for p in range(split)]
    got, chunks, sections, places, heres, vcols, decay, h_columns, h_top, h_near = tie(
        (got, chunks, sections, places, heres, vcols, decay, h_columns, h_top, h_near)
    )

    sent.append(partial(0))
    received.append(swap(sent[0], "hier", hier, group))
    got.append(spread(1))
    across = swap(sections[0], "row", row, top)
    got, received, across, sections, h_top, h_near = tie(
        (got, received, across, sections, h_top, h_near)
    )

    sent.append(partial(1))
    received.append(swap(sent[1], "hier", hier, group))
    last_across = swap(sections[1], "row", row, top)
    s_parts = joined(tree(sections[0], row, low), across)
    h_parts = joined(h_near, h_top)
    done, s_parts, h_parts = tie((coupled(0), s_parts, h_parts))
    sums.append(gather_back(done))
    base = make_right(sections, h_parts, row_place, decay)
    base = make_left(s_parts, h_columns[0], base, row_place)
    received, last_across, sums, base, sections = tie(
        (received, last_across, sums, base, sections)
    )

    s_parts = joined(tree(sections[1], row, low), last_across)
    sums.append(gather_back(coupled(1)))
    both = jnp.concatenate([own_place, row_place])
    for p in range(split):
        outs = make_final(
            p, split, base, accumulated, s_parts, h_columns[1], sums[p], both, outs
        )
    slope, total = outs
    return slope, total


def solution(mesh):
    return jax.shard_map(
        functools.partial(shards, mesh.shape["hier"], mesh.shape["row"]),
        mesh=mesh,
        in_specs=(
            P("hier", None, "row", None),
            P("hier", None, "row", None),
            P("hier", None, "row", None),
            P(None, "row", None),
            P(),
            P(),
            P(),
            P("hier", None),
            P("hier", None),
            P("hier", None),
        ),
        out_specs=(P("hier", None, "row", None), P("hier", None, "row", None)),
        check_vma=False,
    )
```

```python
import functools

import jax
import jax.numpy as jnp
import numpy as np
from jax import lax
from jax.experimental import pallas as pl
from jax.experimental.pallas import tpu as pltpu
from jax.sharding import PartitionSpec as P

step_size = 0.5
highest_total = 4
row_tile = 16
pieces = 2
MIB = 1024 * 1024
f32 = jnp.float32
bf16 = jnp.bfloat16


def index_rows(slots, modes):
    entries = [()]
    for _ in range(modes):
        entries = [
            entry + (level,)
            for entry in entries
            for level in range(highest_total + 1)
            if sum(entry) + level <= highest_total
        ]
    return sorted(entries, key=lambda entry: (sum(entry), entry))[:slots]


def coupled_to(rows):
    lookup = {entry: place for place, entry in enumerate(rows)}
    result = []
    for entry in rows:
        terms = []
        for mode, level in enumerate(entry):
            raised = entry[:mode] + (level + 1,) + entry[mode + 1 :]
            if raised in lookup:
                terms.append((lookup[raised], mode, True, 1))
            if level > 0:
                lowered = entry[:mode] + (level - 1,) + entry[mode + 1 :]
                terms.append((lookup[lowered], mode, False, level))
        result.append(terms)
    return result


def smaller_class(rows):
    classes = [[c for c, entry in enumerate(rows) if sum(entry) % 2 == rest] for rest in (0, 1)]
    return min(classes, key=len)


def params(megabytes):
    return pltpu.CompilerParams(vmem_limit_bytes=megabytes * MIB)


def whole():
    return pl.BlockSpec(memory_space=pltpu.VMEM)


def anywhere():
    return pl.BlockSpec(memory_space=pl.ANY)


def scalars():
    return pl.BlockSpec(memory_space=pltpu.SMEM)


def swap(array, axis, size, bit):
    return lax.ppermute(array, axis, [(i, i ^ bit) for i in range(size)])


def tie(arrays):
    return lax.optimization_barrier(arrays)


def row_bits(size):
    return [1 << i for i in reversed(range(size.bit_length() - 1))]


def tree(array, size, bits):
    parts = {0: array}
    for bit in bits:
        for mask in list(parts):
            parts[mask ^ bit] = swap(parts[mask], "row", size, bit)
    return [parts[mask] for mask in sorted(parts)]


def section_kernel(where, state, slope, section, *chunks):
    value = (state[...].astype(f32) + (0.5 * step_size) * slope[...]).astype(bf16)
    section[...] = value
    width = chunks[0].shape[-1]
    for b, chunk in enumerate(chunks):
        columns = pl.ds(pl.multiple_of((where[0] ^ b) * width, 128), width)
        chunk[...] = section[:, :, :, columns]


def make_section(p, split, state, prev_slope, place, group):
    ops, parts, rows, columns = state.shape
    height, width = rows // split, columns // group
    block = pl.BlockSpec((1, parts, height, columns), lambda a, _: (a, 0, p, 0))
    out = pl.BlockSpec((1, parts, height, columns), lambda a, _: (a, 0, 0, 0))
    chunk = pl.BlockSpec((1, parts, height, width), lambda a, _: (a, 0, 0, 0))
    section, *chunks = pl.pallas_call(
        section_kernel,
        grid_spec=pltpu.PrefetchScalarGridSpec(
            num_scalar_prefetch=1,
            grid=(ops,),
            in_specs=[block, block],
            out_specs=[out] + [chunk] * group,
        ),
        out_shape=[jax.ShapeDtypeStruct((ops, parts, height, columns), bf16)]
        + [jax.ShapeDtypeStruct((ops, parts, height, width), bf16)] * group,
        compiler_params=params(60 if p == 0 else 16),
        cost_estimate=pl.CostEstimate(flops=1, bytes_accessed=1, transcendentals=0),
        name="section",
    )(place, state, prev_slope)
    return section, chunks


def fill_factors(vrows, vcols, coupling, factors):
    modes = vrows.shape[0]
    for k in range(modes):
        first = vrows[k]
        second = vcols[k : k + 1, :]
        diff = first - second
        factors[k] = diff
        factors[modes + k] = coupling[0, k] * diff
        factors[2 * modes + k] = coupling[1, k] * (first + second)


def add_terms(terms, places, held, factors, modes, rows, real, imag):
    for other, mode, child, count in terms:
        place = places[other]
        x_real = held[place, 0, rows, :].astype(f32)
        x_imag = held[place, 1, rows, :].astype(f32)
        if child:
            diff = factors[mode, rows, :]
            real = real + diff * x_imag
            imag = imag - diff * x_real
        else:
            first = factors[modes + mode, rows, :]
            second = factors[2 * modes + mode, rows, :]
            if count != 1:
                first, second = count * first, count * second
            real = real + (first * x_imag + second * x_real)
            imag = imag + (second * x_imag - first * x_real)
    return real, imag


def partial_kernel(links, sides, group, places, coupling, vrows, vcols, *refs):
    chunks, out, held, factors, sems = refs[:group], *refs[group:]
    modes = vrows.shape[0]
    height, width = held.shape[2:]
    ops = chunks[0].shape[0]
    empty = group * ops
    loads = [
        pltpu.make_async_copy(chunk, held.at[pl.ds(b * ops, ops)], sems.at[b])
        for b, chunk in enumerate(chunks)
    ]
    for load in loads:
        load.start()
    fill_factors(vrows, vcols, coupling, factors)
    held[empty] = jnp.zeros(held.shape[1:], bf16)
    for load in loads:
        load.wait()
    for u, c in enumerate(sides):

        @pl.when(places[c] < empty)
        def _():
            out[u] = held[places[c]]

        @pl.when(places[c] == empty)
        def _():
            @pl.loop(0, height // row_tile)
            def _(i):
                rows = pl.ds(pl.multiple_of(i * row_tile, row_tile), row_tile)
                zero = jnp.zeros((row_tile, width), f32)
                real, imag = add_terms(links[c], places, held, factors, modes, rows, zero, zero)
                out[u, 0, rows, :] = real.astype(bf16)
                out[u, 1, rows, :] = imag.astype(bf16)


def coupled_kernel(links, sides, group, places, coupling, vrows, vcols, *refs):
    chunks, received, outs = refs[:group], refs[group], refs[group + 1 : 2 * group + 1]
    held, done, factors, spots, sems = refs[2 * group + 1 :]
    modes = vrows.shape[0]
    height, width = held.shape[2:]
    ops = chunks[0].shape[0]
    empty = group * ops
    loads = [
        pltpu.make_async_copy(chunk, held.at[pl.ds(b * ops, ops)], sems.at[b])
        for b, chunk in enumerate(chunks)
    ]
    loads.append(
        pltpu.make_async_copy(received, held.at[pl.ds(empty + 1, len(sides))], sems.at[group])
    )
    for load in loads:
        load.start()
    fill_factors(vrows, vcols, coupling, factors)
    held[empty] = jnp.zeros(held.shape[1:], bf16)
    for c in range(len(links)):
        spots[c] = places[c]
    for u, c in enumerate(sides):
        spots[c] = jnp.where(places[c] == empty, empty + 1 + u, places[c])
    for load in loads:
        load.wait()
    for c in range(len(links)):

        @pl.when(places[c] < empty)
        def _():
            @pl.loop(0, height // row_tile)
            def _(i):
                rows = pl.ds(pl.multiple_of(i * row_tile, row_tile), row_tile)
                if c in sides:
                    u = empty + 1 + sides.index(c)
                    real, imag = held[u, 0, rows, :].astype(f32), held[u, 1, rows, :].astype(f32)
                else:
                    real = imag = jnp.zeros((row_tile, width), f32)
                real, imag = add_terms(links[c], spots, held, factors, modes, rows, real, imag)
                done[places[c], 0, rows, :] = real.astype(bf16)
                done[places[c], 1, rows, :] = imag.astype(bf16)

    stores = [
        pltpu.make_async_copy(done.at[pl.ds(b * ops, ops)], out, sems.at[group + 1 + b])
        for b, out in enumerate(outs)
    ]
    for store in stores:
        store.start()
    for store in stores:
        store.wait()


def coupling_scratch(entries, height, width, modes):
    return [pltpu.VMEM((entries, 2, height, width), bf16)], [pltpu.VMEM((3 * modes, height, width), f32)]


def make_partial(chunks, places, coupling, vrows, vcols, links, sides):
    group = len(chunks)
    ops, _, height, width = chunks[0].shape
    held, factors = coupling_scratch(group * ops + 1, height, width, vrows.shape[0])
    size = height * width
    return pl.pallas_call(
        functools.partial(partial_kernel, links, sides, group),
        in_specs=[scalars(), scalars()] + [whole()] * 2 + [anywhere()] * group,
        out_specs=whole(),
        out_shape=jax.ShapeDtypeStruct((len(sides), 2, height, width), bf16),
        scratch_shapes=held + factors + [pltpu.SemaphoreType.DMA((group,))],
        compiler_params=params(12),
        cost_estimate=pl.CostEstimate(
            flops=40 * len(sides) * size,
            bytes_accessed=4 * size * (group * ops + len(sides)),
            transcendentals=0,
        ),
        name="partial_sums",
    )(places, coupling, vrows, vcols, *chunks)


def make_coupled(chunks, received, places, coupling, vrows, vcols, links, sides):
    group = len(chunks)
    ops, _, height, width = chunks[0].shape
    held, factors = coupling_scratch(group * ops + 1 + len(sides), height, width, vrows.shape[0])
    size = height * width
    return pl.pallas_call(
        functools.partial(coupled_kernel, links, sides, group),
        in_specs=[scalars(), scalars()] + [whole()] * 2 + [anywhere()] * (1 + group),
        out_specs=[anywhere()] * group,
        out_shape=[jax.ShapeDtypeStruct(chunks[0].shape, bf16)] * group,
        scratch_shapes=held
        + [pltpu.VMEM((group * ops, 2, height, width), bf16)]
        + factors
        + [pltpu.SMEM((len(links),), jnp.int32), pltpu.SemaphoreType.DMA((2 * group + 1,))],
        compiler_params=params(16),
        cost_estimate=pl.CostEstimate(flops=1, bytes_accessed=1, transcendentals=0),
        name="coupling_sums",
    )(places, coupling, vrows, vcols, *chunks, received)


def complex_rows(left, right):
    _, height, depth = left.shape
    left = left.reshape(2 * height, depth)
    first = jnp.dot(left, right[0], preferred_element_type=f32)
    second = jnp.dot(left, right[1], preferred_element_type=f32)
    return first[:height] - second[height:], second[:height] + first[height:]


def right_kernel(split, count, where, decay, h_own, *refs):
    sections, refs, (out, h_all) = refs[:split], refs[split:-2], refs[-2:]
    h_near, h_far = refs[: 2 * count - 2], refs[2 * count - 2 :]
    j, a = pl.program_id(0), pl.program_id(1)
    rows, size = h_own.shape[1:]
    height, tile = sections[0].shape[2], out.shape[3]
    half, block = size // 2, size // 4
    own = pl.multiple_of((where[0] // count) * half, half)
    other = pl.multiple_of(half - own, half)

    @pl.when(jnp.logical_and(j == 0, a == 0))
    def _():
        for b in range(count):
            place = pl.multiple_of((where[0] ^ b) * rows, row_tile)
            for x in range(2):
                near = h_near[2 * b - 2 + x][...] if b else h_own[x]
                h_all[x, pl.ds(place, rows), :] = near
            place = pl.multiple_of((where[0] ^ (count + b)) * rows, row_tile)
            h_all[:, pl.ds(place, rows), pl.ds(other, half)] = h_far[b][...]
        for r in range(0, half, block):
            for c in range(0, half, block):
                here = pl.ds(pl.multiple_of(own + r, block), block)
                there = pl.ds(pl.multiple_of(other + c, block), block)
                h_all[0, there, here] = h_all[0, here, there].T
                h_all[1, there, here] = -h_all[1, here, there].T

    columns = pl.ds(pl.multiple_of(j * tile, 128), tile)
    lost = decay[a]
    for p, section in enumerate(sections):
        real, imag = complex_rows(section[a], h_all.at[:, :, columns])
        here = slice(p * height, (p + 1) * height)
        out[0, 0, here, :] = -imag - lost * section[a, 0, :, columns].astype(f32)
        out[0, 1, here, :] = real - lost * section[a, 1, :, columns].astype(f32)


def make_right(sections, h_own, bundles, h_far, place, decay):
    ops, _, height, columns = sections[0].shape
    split, count = len(sections), len(h_far)
    rows, tile = height * split, min(columns, 512)
    held = pl.BlockSpec((ops, 2, height, columns), lambda j, a: (0, 0, 0, 0))
    return pl.pallas_call(
        functools.partial(right_kernel, split, count),
        grid=(columns // tile, ops),
        in_specs=[scalars(), scalars(), pl.BlockSpec(h_own.shape, lambda j, a: (0, 0, 0))]
        + [held] * split
        + [pl.BlockSpec((rows, columns), lambda j, a, x=x: (ops + x, 0)) for x in range(2)]
        * len(bundles)
        + [pl.BlockSpec(h.shape, lambda j, a: (0, 0, 0)) for h in h_far],
        out_specs=pl.BlockSpec((1, 2, rows, tile), lambda j, a: (a, 0, 0, j)),
        out_shape=jax.ShapeDtypeStruct((ops, 2, rows, columns), f32),
        scratch_shapes=[pltpu.VMEM((2, columns, columns), bf16)],
        compiler_params=params(28),
        cost_estimate=pl.CostEstimate(
            flops=8 * ops * rows * columns * columns,
            bytes_accessed=4 * columns * (columns + 3 * ops * rows),
            transcendentals=0,
        ),
        name="right_products",
    )(place, decay, h_own, *sections, *[h for h in bundles for _ in range(2)], *h_far)


def left_kernel(count, where, h_own, base, *refs):
    s_parts, (out, s_all) = refs[:count], refs[count:]
    height, tile = s_parts[0].shape[2:]
    for b in range(count):
        place = pl.ds(pl.multiple_of((where[0] ^ b) * height, row_tile), height)
        s_all[:, place, :] = s_parts[b][...].reshape(2, height, tile)
    real, imag = complex_rows(h_own[...], s_all)
    out[0, 0] = base[0, 0] + imag
    out[0, 1] = base[0, 1] - real


def make_left(s_parts, h_columns, base, place):
    ops, _, height, columns = s_parts[0].shape
    count, rows, tile = len(s_parts), base.shape[2], min(columns, 512)
    block = pl.BlockSpec((1, 2, rows, tile), lambda j, a: (a, 0, 0, j))
    return pl.pallas_call(
        functools.partial(left_kernel, count),
        grid=(columns // tile, ops),
        in_specs=[
            scalars(),
            pl.BlockSpec(h_columns.shape, lambda j, a: (0, 0, 0)),
            block,
        ]
        + [
            pl.BlockSpec((1, 2, height, tile), lambda j, a: (a, 0, 0, j))
            if part.ndim == 4
            else pl.BlockSpec((2 * height, tile), lambda j, a: (a, j))
            for part in s_parts
        ],
        out_specs=block,
        out_shape=jax.ShapeDtypeStruct(base.shape, f32),
        scratch_shapes=[pltpu.VMEM((2, count * height, tile), bf16)],
        compiler_params=params(16),
        cost_estimate=pl.CostEstimate(
            flops=8 * ops * rows * columns * count * height,
            bytes_accessed=4 * ops * columns * (count * height + 4 * rows),
            transcendentals=0,
        ),
        name="left_products",
    )(place, h_columns, base, *s_parts)


def final_kernel(group, where, base, accumulated, *refs):
    sums, (slope, total) = refs[:group], refs[-2:]
    j = pl.program_id(1)
    tile, width = slope.shape[3], sums[0].shape[3]
    for b in range(group):
        first = (where[0] ^ b) * width - j * tile

        @pl.when(jnp.logical_and(first >= 0, first < tile))
        def _():
            columns = pl.ds(pl.multiple_of(first, 128), width)
            value = base[0, :, :, columns] + sums[b][0].astype(f32)
            slope[0, :, :, columns] = value
            total[0, :, :, columns] = accumulated[0, :, :, columns] + (step_size / 3.0) * value


def make_final(p, split, base, accumulated, sums, place, earlier=()):
    ops, parts, rows, columns = base.shape
    group = len(sums)
    height, width, tile = rows // split, sums[0].shape[3], min(columns, 512)
    block = pl.BlockSpec((1, parts, height, tile), lambda a, j, _: (a, 0, p, j))
    chunk = pl.BlockSpec((1, parts, height, width), lambda a, j, _: (a, 0, 0, 0))
    return pl.pallas_call(
        functools.partial(final_kernel, group),
        grid_spec=pltpu.PrefetchScalarGridSpec(
            num_scalar_prefetch=1,
            grid=(ops, columns // tile),
            in_specs=[block, block] + [chunk] * group + [anywhere()] * len(earlier),
            out_specs=[block, block],
        ),
        out_shape=[jax.ShapeDtypeStruct(base.shape, f32)] * 2,
        input_output_aliases={3 + group + k: k for k in range(len(earlier))},
        compiler_params=params(16),
        cost_estimate=pl.CostEstimate(
            flops=4 * base.size // split,
            bytes_accessed=18 * base.size // split,
            transcendentals=0,
        ),
        name="outputs",
    )(place, base, accumulated, *sums, *earlier)


def shards(
    hier,
    row,
    state,
    prev_slope,
    accumulated,
    hamiltonian,
    couple_v,
    coupling,
    damping,
    occupation,
    parents,
    children,
):
    ops, _, rows, columns = state.shape
    modes = occupation.shape[1]
    group = hier // 2
    width = columns // group
    split = pieces
    height = rows // split
    table = index_rows(hier * ops, modes)
    links, sides = coupled_to(table), smaller_class(table)

    hier_at, row_at = lax.axis_index("hier"), lax.axis_index("row")
    own = hier_at % group
    own_place, row_place = own.reshape(1).astype(jnp.int32), row_at.reshape(1).astype(jnp.int32)

    bits = row_bits(row)
    top, low = bits[0], bits[1:]

    def spread(p):
        return [chunks[p][0]] + [swap(chunks[p][b], "hier", hier, b) for b in range(1, group)]

    def partial(p):
        return make_partial(got[p], places, coupling, heres[p], vcols, links, sides)

    def coupled(p):
        return make_coupled(got[p], received[p], places, coupling, heres[p], vcols, links, sides)

    def gather_back(done):
        return [done[0]] + [swap(done[b], "hier", hier, b) for b in range(1, group)]

    got, sent, received, sums, outs = [], [], [], [], []

    first, first_chunks = make_section(0, split, state, prev_slope, own_place, group)
    first, first_chunks, occupation, state, prev_slope, couple_v, hamiltonian = tie(
        (first, first_chunks, occupation, state, prev_slope, couple_v, hamiltonian)
    )
    half = [occupation] + [swap(occupation, "hier", hier, b) for b in range(1, group)]

    half_columns = lax.dynamic_slice_in_dim(
        hamiltonian, row_at // (row // 2) * (columns // 2), columns // 2, 2
    )
    h_top = swap(half_columns, "row", row, top)
    second, second_chunks = make_section(1, split, state, prev_slope, own_place, group)
    chunks, sections = [first_chunks, second_chunks], [first, second]
    got.append(spread(0))

    known = jnp.asarray(np.array(table, np.int32))
    found = jnp.concatenate(half, axis=0)
    same = jnp.all(found[None, :, :] == known[:, None, :], axis=2)
    spot = jnp.arange(group * ops, dtype=jnp.int32)[None, :]
    places = jnp.min(jnp.where(same, spot, group * ops), axis=1).astype(jnp.int32)
    vrows = lax.dynamic_slice_in_dim(couple_v, row_at * rows, rows, 1)[:, :, None]
    vcols = lax.dynamic_slice_in_dim(couple_v, own * width, width, 1)
    heres = [vrows[:, p * height : (p + 1) * height] for p in range(split)]
    decay = jnp.sum(half[0].astype(f32) * damping[None, :], axis=1)
    got, chunks, sections, places, heres, vcols, decay, h_top, kept = tie(
        (got, chunks, sections, places, heres, vcols, decay, h_top, hamiltonian)
    )

    sent.append(partial(0))
    received.append(swap(sent[0], "hier", hier, group))
    got.append(spread(1))
    across = swap(sections[0], "row", row, top)
    near = jnp.concatenate([sections[0].reshape(-1, columns), kept.reshape(-1, columns)])
    blocks = kept.reshape(2, rows, row, split, height)
    h_columns = [blocks[:, :, :, p].reshape(2, rows, row * height) for p in range(split)]
    got, received, across, sections, h_top, near, h_columns = tie(
        (got, received, across, sections, h_top, near, h_columns)
    )

    sent.append(partial(1))
    received.append(swap(sent[1], "hier", hier, group))
    last_across = swap(sections[1], "row", row, top)
    near, s_far, h_far = tree(near, row, low), tree(across, row, low), tree(h_top, row, low)
    done, near, s_far, h_far = tie((coupled(0), near, s_far, h_far))
    sums.append(gather_back(done))
    base = make_right(sections, hamiltonian, near[1:], h_far, row_place, decay)
    base = make_left([sections[0], *near[1:], *s_far], h_columns[0], base, row_place)
    received, last_across, sums, base, sections = tie(
        (received, last_across, sums, base, sections)
    )

    s_parts = tree(sections[1], row, low) + tree(last_across, row, low)
    sums.append(gather_back(coupled(1)))
    base = make_left(s_parts, h_columns[1], base, row_place)
    for p in range(split):
        outs = make_final(p, split, base, accumulated, sums[p], own_place, outs)
    slope, total = outs
    return slope, total


def solution(mesh):
    return jax.shard_map(
        functools.partial(shards, mesh.shape["hier"], mesh.shape["row"]),
        mesh=mesh,
        in_specs=(
            P("hier", None, "row", None),
            P("hier", None, "row", None),
            P("hier", None, "row", None),
            P(None, "row", None),
            P(),
            P(),
            P(),
            P("hier", None),
            P("hier", None),
            P("hier", None),
        ),
        out_specs=(P("hier", None, "row", None), P("hier", None, "row", None)),
        check_vma=False,
    )
```

```python
import functools

import jax
import jax.numpy as jnp
import numpy as np
from jax import lax
from jax.experimental import pallas as pl
from jax.experimental.pallas import tpu as pltpu
from jax.sharding import PartitionSpec as P

step_size = 0.5
highest_total = 4
row_tile = 16
pieces = 2
MIB = 1024 * 1024
f32 = jnp.float32
bf16 = jnp.bfloat16


def index_rows(slots, modes):
    entries = [()]
    for _ in range(modes):
        entries = [
            entry + (level,)
            for entry in entries
            for level in range(highest_total + 1)
            if sum(entry) + level <= highest_total
        ]
    return sorted(entries, key=lambda entry: (sum(entry), entry))[:slots]


def coupled_to(rows):
    lookup = {entry: place for place, entry in enumerate(rows)}
    result = []
    for entry in rows:
        terms = []
        for mode, level in enumerate(entry):
            raised = entry[:mode] + (level + 1,) + entry[mode + 1 :]
            if raised in lookup:
                terms.append((lookup[raised], mode, True, 1))
            if level > 0:
                lowered = entry[:mode] + (level - 1,) + entry[mode + 1 :]
                terms.append((lookup[lowered], mode, False, level))
        result.append(terms)
    return result


def smaller_class(rows):
    classes = [[c for c, entry in enumerate(rows) if sum(entry) % 2 == rest] for rest in (0, 1)]
    return min(classes, key=len)


def params(megabytes):
    return pltpu.CompilerParams(vmem_limit_bytes=megabytes * MIB)


def whole():
    return pl.BlockSpec(memory_space=pltpu.VMEM)


def anywhere():
    return pl.BlockSpec(memory_space=pl.ANY)


def scalars():
    return pl.BlockSpec(memory_space=pltpu.SMEM)


def swap(array, axis, size, bit):
    return lax.ppermute(array, axis, [(i, i ^ bit) for i in range(size)])


def tie(arrays):
    return lax.optimization_barrier(arrays)


def row_bits(size):
    return [1 << i for i in reversed(range(size.bit_length() - 1))]


def tree(array, size, bits):
    parts = {0: array}
    for bit in bits:
        for mask in list(parts):
            parts[mask ^ bit] = swap(parts[mask], "row", size, bit)
    return [parts[mask] for mask in sorted(parts)]


def section_kernel(group, where, _, state, slope, *refs):
    extra, section, chunks = refs[: -group - 1], refs[-group - 1], refs[-group:]
    value = (state[...].astype(f32) + (0.5 * step_size) * slope[...]).astype(bf16)
    section[...] = value
    width = chunks[0].shape[-1]
    for b, chunk in enumerate(chunks):
        columns = pl.ds(pl.multiple_of((where[0] ^ b) * width, 128), width)
        chunk[...] = section[:, :, :, columns]
    if extra:
        source, target = extra

        @pl.when(pl.program_id(0) == 0)
        def _():
            target[...] = source[...]


def make_section(p, split, state, prev_slope, place, half_at, group, hamiltonian=None):
    ops, parts, rows, columns = state.shape
    height, width = rows // split, columns // group
    block = pl.BlockSpec((1, parts, height, columns), lambda a, *_: (a, 0, p, 0))
    out = pl.BlockSpec((1, parts, height, columns), lambda a, *_: (a, 0, 0, 0))
    chunk = pl.BlockSpec((1, parts, height, width), lambda a, *_: (a, 0, 0, 0))
    half = (2, rows, columns // 2)
    extra = [] if hamiltonian is None else [hamiltonian]
    return pl.pallas_call(
        functools.partial(section_kernel, group),
        grid_spec=pltpu.PrefetchScalarGridSpec(
            num_scalar_prefetch=2,
            grid=(ops,),
            in_specs=[block, block] + [pl.BlockSpec(half, lambda a, _, h: (0, 0, h[0])) for _ in extra],
            out_specs=[pl.BlockSpec(half, lambda a, *_: (0, 0, 0)) for _ in extra]
            + [out]
            + [chunk] * group,
        ),
        out_shape=[jax.ShapeDtypeStruct(half, bf16) for _ in extra]
        + [jax.ShapeDtypeStruct((ops, parts, height, columns), bf16)]
        + [jax.ShapeDtypeStruct((ops, parts, height, width), bf16)] * group,
        compiler_params=params(54 if p == 0 else 16),
        cost_estimate=pl.CostEstimate(flops=1, bytes_accessed=1, transcendentals=0),
        name="section",
    )(place, half_at, state, prev_slope, *extra)


def fill_factors(vrows, vcols, coupling, factors):
    modes = vrows.shape[0]
    for k in range(modes):
        first = vrows[k]
        second = vcols[k : k + 1, :]
        diff = first - second
        factors[k] = diff
        factors[modes + k] = coupling[0, k] * diff
        factors[2 * modes + k] = coupling[1, k] * (first + second)


def add_terms(terms, places, held, factors, modes, rows, real, imag):
    for other, mode, child, count in terms:
        place = places[other]
        x_real = held[place, 0, rows, :].astype(f32)
        x_imag = held[place, 1, rows, :].astype(f32)
        if child:
            diff = factors[mode, rows, :]
            real = real + diff * x_imag
            imag = imag - diff * x_real
        else:
            first = factors[modes + mode, rows, :]
            second = factors[2 * modes + mode, rows, :]
            if count != 1:
                first, second = count * first, count * second
            real = real + (first * x_imag + second * x_real)
            imag = imag + (second * x_imag - first * x_real)
    return real, imag


def partial_kernel(links, sides, group, places, coupling, vrows, vcols, *refs):
    chunks, out, held, factors = refs[:group], *refs[group:]
    modes = vrows.shape[0]
    height, width = held.shape[2:]
    ops = chunks[0].shape[0]
    empty = group * ops
    fill_factors(vrows, vcols, coupling, factors)
    for b, chunk in enumerate(chunks):
        held[b * ops : (b + 1) * ops] = chunk[...]
    held[empty] = jnp.zeros(held.shape[1:], bf16)
    for u, c in enumerate(sides):

        @pl.when(places[c] < empty)
        def _():
            out[u] = held[places[c]]

        @pl.when(places[c] == empty)
        def _():
            @pl.loop(0, height // row_tile)
            def _(i):
                rows = pl.ds(pl.multiple_of(i * row_tile, row_tile), row_tile)
                zero = jnp.zeros((row_tile, width), f32)
                real, imag = add_terms(links[c], places, held, factors, modes, rows, zero, zero)
                out[u, 0, rows, :] = real.astype(bf16)
                out[u, 1, rows, :] = imag.astype(bf16)


def coupled_kernel(links, sides, group, places, coupling, vrows, vcols, *refs):
    chunks, received, outs = refs[:group], refs[group], refs[group + 1 : 2 * group + 1]
    held, done, factors, spots = refs[2 * group + 1 :]
    modes = vrows.shape[0]
    height, width = held.shape[2:]
    ops = chunks[0].shape[0]
    empty = group * ops
    fill_factors(vrows, vcols, coupling, factors)
    for b, chunk in enumerate(chunks):
        held[b * ops : (b + 1) * ops] = chunk[...]
    held[empty] = jnp.zeros(held.shape[1:], bf16)
    held[empty + 1 :] = received[...]
    for c in range(len(links)):
        spots[c] = places[c]
    for u, c in enumerate(sides):
        spots[c] = jnp.where(places[c] == empty, empty + 1 + u, places[c])
    for c in range(len(links)):

        @pl.when(places[c] < empty)
        def _():
            @pl.loop(0, height // row_tile)
            def _(i):
                rows = pl.ds(pl.multiple_of(i * row_tile, row_tile), row_tile)
                if c in sides:
                    u = empty + 1 + sides.index(c)
                    real, imag = held[u, 0, rows, :].astype(f32), held[u, 1, rows, :].astype(f32)
                else:
                    real = imag = jnp.zeros((row_tile, width), f32)
                real, imag = add_terms(links[c], spots, held, factors, modes, rows, real, imag)
                done[places[c], 0, rows, :] = real.astype(bf16)
                done[places[c], 1, rows, :] = imag.astype(bf16)

    for b, out in enumerate(outs):
        out[...] = done[b * ops : (b + 1) * ops]


def coupling_scratch(entries, height, width, modes):
    return [pltpu.VMEM((entries, 2, height, width), bf16)], [pltpu.VMEM((3 * modes, height, width), f32)]


def make_partial(chunks, places, coupling, vrows, vcols, links, sides):
    group = len(chunks)
    ops, _, height, width = chunks[0].shape
    held, factors = coupling_scratch(group * ops + 1, height, width, vrows.shape[0])
    size = height * width
    return pl.pallas_call(
        functools.partial(partial_kernel, links, sides, group),
        in_specs=[scalars(), scalars()] + [whole()] * (2 + group),
        out_specs=whole(),
        out_shape=jax.ShapeDtypeStruct((len(sides), 2, height, width), bf16),
        scratch_shapes=held + factors,
        compiler_params=params(12),
        cost_estimate=pl.CostEstimate(
            flops=40 * len(sides) * size,
            bytes_accessed=4 * size * (group * ops + len(sides)),
            transcendentals=0,
        ),
        name="partial_sums",
    )(places, coupling, vrows, vcols, *chunks)


def make_coupled(chunks, received, places, coupling, vrows, vcols, links, sides):
    group = len(chunks)
    ops, _, height, width = chunks[0].shape
    held, factors = coupling_scratch(group * ops + 1 + len(sides), height, width, vrows.shape[0])
    size = height * width
    return pl.pallas_call(
        functools.partial(coupled_kernel, links, sides, group),
        in_specs=[scalars(), scalars()] + [whole()] * (3 + group),
        out_specs=[whole()] * group,
        out_shape=[jax.ShapeDtypeStruct(chunks[0].shape, bf16)] * group,
        scratch_shapes=held
        + [pltpu.VMEM((group * ops, 2, height, width), bf16)]
        + factors
        + [pltpu.SMEM((len(links),), jnp.int32)],
        compiler_params=params(16),
        cost_estimate=pl.CostEstimate(flops=1, bytes_accessed=1, transcendentals=0),
        name="coupling_sums",
    )(places, coupling, vrows, vcols, *chunks, received)


def complex_rows(left, right):
    _, height, depth = left.shape
    left = left.reshape(2 * height, depth)
    first = jnp.dot(left, right[0], preferred_element_type=f32)
    second = jnp.dot(left, right[1], preferred_element_type=f32)
    return first[:height] - second[height:], second[:height] + first[height:]


def right_kernel(split, count, where, decay, h_own, *refs):
    sections, refs, (out, h_all) = refs[:split], refs[split:-2], refs[-2:]
    h_near, h_far = refs[: 2 * count - 2], refs[2 * count - 2 :]
    j, a = pl.program_id(0), pl.program_id(1)
    rows, size = h_own.shape[1:]
    height, tile = sections[0].shape[2], out.shape[3]
    half, block = size // 2, size // 4
    own = pl.multiple_of((where[0] // count) * half, half)
    other = pl.multiple_of(half - own, half)

    @pl.when(jnp.logical_and(j == 0, a == 0))
    def _():
        for b in range(count):
            place = pl.multiple_of((where[0] ^ b) * rows, row_tile)
            for x in range(2):
                near = h_near[2 * b - 2 + x][...] if b else h_own[x]
                h_all[x, pl.ds(place, rows), :] = near
            place = pl.multiple_of((where[0] ^ (count + b)) * rows, row_tile)
            h_all[:, pl.ds(place, rows), pl.ds(other, half)] = h_far[b][...]
        for r in range(0, half, block):
            for c in range(0, half, block):
                here = pl.ds(pl.multiple_of(own + r, block), block)
                there = pl.ds(pl.multiple_of(other + c, block), block)
                h_all[0, there, here] = h_all[0, here, there].T
                h_all[1, there, here] = -h_all[1, here, there].T

    columns = pl.ds(pl.multiple_of(j * tile, 128), tile)
    lost = decay[a]
    for p, section in enumerate(sections):
        real, imag = complex_rows(section[a], h_all.at[:, :, columns])
        here = slice(p * height, (p + 1) * height)
        out[0, 0, here, :] = -imag - lost * section[a, 0, :, columns].astype(f32)
        out[0, 1, here, :] = real - lost * section[a, 1, :, columns].astype(f32)


def make_right(sections, h_own, bundles, h_far, place, decay):
    ops, _, height, columns = sections[0].shape
    split, count = len(sections), len(h_far)
    rows, tile = height * split, min(columns, 512)
    held = pl.BlockSpec((ops, 2, height, columns), lambda j, a: (0, 0, 0, 0))
    return pl.pallas_call(
        functools.partial(right_kernel, split, count),
        grid=(columns // tile, ops),
        in_specs=[scalars(), scalars(), pl.BlockSpec(h_own.shape, lambda j, a: (0, 0, 0))]
        + [held] * split
        + [pl.BlockSpec((rows, columns), lambda j, a, x=x: (ops + x, 0)) for x in range(2)]
        * len(bundles)
        + [pl.BlockSpec(h.shape, lambda j, a: (0, 0, 0)) for h in h_far],
        out_specs=pl.BlockSpec((1, 2, rows, tile), lambda j, a: (a, 0, 0, j)),
        out_shape=jax.ShapeDtypeStruct((ops, 2, rows, columns), f32),
        scratch_shapes=[pltpu.VMEM((2, columns, columns), bf16)],
        compiler_params=params(28),
        cost_estimate=pl.CostEstimate(
            flops=8 * ops * rows * columns * columns,
            bytes_accessed=4 * columns * (columns + 3 * ops * rows),
            transcendentals=0,
        ),
        name="right_products",
    )(place, decay, h_own, *sections, *[h for h in bundles for _ in range(2)], *h_far)


def left_kernel(count, where, h_own, base, *refs):
    s_parts, (out, s_all) = refs[:count], refs[count:]
    height, tile = s_parts[0].shape[2:]
    for b in range(count):
        place = pl.ds(pl.multiple_of((where[0] ^ b) * height, row_tile), height)
        s_all[:, place, :] = s_parts[b][...].reshape(2, height, tile)
    real, imag = complex_rows(h_own[...], s_all)
    out[0, 0] = base[0, 0] + imag
    out[0, 1] = base[0, 1] - real


def make_left(s_parts, h_columns, base, place):
    ops, _, height, columns = s_parts[0].shape
    count, rows, tile = len(s_parts), base.shape[2], min(columns, 512)
    block = pl.BlockSpec((1, 2, rows, tile), lambda j, a: (a, 0, 0, j))
    return pl.pallas_call(
        functools.partial(left_kernel, count),
        grid=(columns // tile, ops),
        in_specs=[
            scalars(),
            pl.BlockSpec(h_columns.shape, lambda j, a: (0, 0, 0)),
            block,
        ]
        + [
            pl.BlockSpec((1, 2, height, tile), lambda j, a: (a, 0, 0, j))
            if part.ndim == 4
            else pl.BlockSpec((2 * height, tile), lambda j, a: (a, j))
            for part in s_parts
        ],
        out_specs=block,
        out_shape=jax.ShapeDtypeStruct(base.shape, f32),
        scratch_shapes=[pltpu.VMEM((2, count * height, tile), bf16)],
        compiler_params=params(16),
        cost_estimate=pl.CostEstimate(
            flops=8 * ops * rows * columns * count * height,
            bytes_accessed=4 * ops * columns * (count * height + 4 * rows),
            transcendentals=0,
        ),
        name="left_products",
    )(place, h_columns, base, *s_parts)


def final_kernel(group, where, base, accumulated, *refs):
    sums, (slope, total) = refs[:group], refs[-2:]
    j = pl.program_id(1)
    tile, width = slope.shape[3], sums[0].shape[3]
    for b in range(group):
        first = (where[0] ^ b) * width - j * tile

        @pl.when(jnp.logical_and(first >= 0, first < tile))
        def _():
            columns = pl.ds(pl.multiple_of(first, 128), width)
            value = base[0, :, :, columns] + sums[b][0].astype(f32)
            slope[0, :, :, columns] = value
            total[0, :, :, columns] = accumulated[0, :, :, columns] + (step_size / 3.0) * value


def make_final(p, split, base, accumulated, sums, place, earlier=()):
    ops, parts, rows, columns = base.shape
    group = len(sums)
    height, width, tile = rows // split, sums[0].shape[3], min(columns, 512)
    block = pl.BlockSpec((1, parts, height, tile), lambda a, j, _: (a, 0, p, j))
    chunk = pl.BlockSpec((1, parts, height, width), lambda a, j, _: (a, 0, 0, 0))
    return pl.pallas_call(
        functools.partial(final_kernel, group),
        grid_spec=pltpu.PrefetchScalarGridSpec(
            num_scalar_prefetch=1,
            grid=(ops, columns // tile),
            in_specs=[block, block] + [chunk] * group + [anywhere()] * len(earlier),
            out_specs=[block, block],
        ),
        out_shape=[jax.ShapeDtypeStruct(base.shape, f32)] * 2,
        input_output_aliases={3 + group + k: k for k in range(len(earlier))},
        compiler_params=params(16),
        cost_estimate=pl.CostEstimate(
            flops=4 * base.size // split,
            bytes_accessed=18 * base.size // split,
            transcendentals=0,
        ),
        name="outputs",
    )(place, base, accumulated, *sums, *earlier)


def shards(
    hier,
    row,
    state,
    prev_slope,
    accumulated,
    hamiltonian,
    couple_v,
    coupling,
    damping,
    occupation,
    parents,
    children,
):
    ops, _, rows, columns = state.shape
    modes = occupation.shape[1]
    group = hier // 2
    width = columns // group
    split = pieces
    height = rows // split
    table = index_rows(hier * ops, modes)
    links, sides = coupled_to(table), smaller_class(table)

    hier_at, row_at = lax.axis_index("hier"), lax.axis_index("row")
    own = hier_at % group
    own_place, row_place = own.reshape(1).astype(jnp.int32), row_at.reshape(1).astype(jnp.int32)

    bits = row_bits(row)
    top, low = bits[0], bits[1:]

    def spread(p):
        return [chunks[p][0]] + [swap(chunks[p][b], "hier", hier, b) for b in range(1, group)]

    def partial(p):
        return make_partial(got[p], places, coupling, heres[p], vcols, links, sides)

    def coupled(p):
        return make_coupled(got[p], received[p], places, coupling, heres[p], vcols, links, sides)

    def gather_back(done):
        return [done[0]] + [swap(done[b], "hier", hier, b) for b in range(1, group)]

    got, sent, received, sums, outs = [], [], [], [], []

    half = [occupation] + [swap(occupation, "hier", hier, b) for b in range(1, group)]
    half_at = (row_at // (row // 2)).reshape(1).astype(jnp.int32)
    half_columns, first, *first_chunks = make_section(
        0, split, state, prev_slope, own_place, half_at, group, hamiltonian
    )
    half_columns, first, first_chunks, half, state, prev_slope, couple_v, hamiltonian = tie(
        (half_columns, first, first_chunks, half, state, prev_slope, couple_v, hamiltonian)
    )

    h_top = swap(half_columns, "row", row, top)
    second, *second_chunks = make_section(
        1, split, state, prev_slope, own_place, half_at, group
    )
    chunks, sections = [first_chunks, second_chunks], [first, second]
    got.append(spread(0))

    known = jnp.asarray(np.array(table, np.int32))
    found = jnp.concatenate(half, axis=0)
    same = jnp.all(found[None, :, :] == known[:, None, :], axis=2)
    spot = jnp.arange(group * ops, dtype=jnp.int32)[None, :]
    places = jnp.min(jnp.where(same, spot, group * ops), axis=1).astype(jnp.int32)
    vrows = lax.dynamic_slice_in_dim(couple_v, row_at * rows, rows, 1)[:, :, None]
    vcols = lax.dynamic_slice_in_dim(couple_v, own * width, width, 1)
    heres = [vrows[:, p * height : (p + 1) * height] for p in range(split)]
    decay = jnp.sum(half[0].astype(f32) * damping[None, :], axis=1)
    got, chunks, sections, places, heres, vcols, decay, h_top, kept = tie(
        (got, chunks, sections, places, heres, vcols, decay, h_top, hamiltonian)
    )

    sent.append(partial(0))
    received.append(swap(sent[0], "hier", hier, group))
    got.append(spread(1))
    across = swap(sections[0], "row", row, top)
    near = jnp.concatenate([sections[0].reshape(-1, columns), kept.reshape(-1, columns)])
    blocks = kept.reshape(2, rows, row, split, height)
    h_columns = [blocks[:, :, :, p].reshape(2, rows, row * height) for p in range(split)]
    got, received, across, sections, h_top, near, h_columns = tie(
        (got, received, across, sections, h_top, near, h_columns)
    )

    sent.append(partial(1))
    received.append(swap(sent[1], "hier", hier, group))
    last_across = swap(sections[1], "row", row, top)
    near, s_far, h_far = tree(near, row, low), tree(across, row, low), tree(h_top, row, low)
    done, near, s_far, h_far = tie((coupled(0), near, s_far, h_far))
    sums.append(gather_back(done))
    base = make_right(sections, hamiltonian, near[1:], h_far, row_place, decay)
    base = make_left([sections[0], *near[1:], *s_far], h_columns[0], base, row_place)
    received, last_across, base = tie((received, last_across, base))

    done, sums, last_across, last_own = tie((coupled(1), sums, last_across, sections[1]))
    sums.append(gather_back(done))
    s_parts = tree(last_own, row, low) + tree(last_across, row, low)
    base = make_left(s_parts, h_columns[1], base, row_place)
    for p in range(split):
        outs = make_final(p, split, base, accumulated, sums[p], own_place, outs)
    slope, total = outs
    return slope, total


def solution(mesh):
    return jax.shard_map(
        functools.partial(shards, mesh.shape["hier"], mesh.shape["row"]),
        mesh=mesh,
        in_specs=(
            P("hier", None, "row", None),
            P("hier", None, "row", None),
            P("hier", None, "row", None),
            P(None, "row", None),
            P(),
            P(),
            P(),
            P("hier", None),
            P("hier", None),
            P("hier", None),
        ),
        out_specs=(P("hier", None, "row", None), P("hier", None, "row", None)),
        check_vma=False,
    )
```

```python
import functools

import jax
import jax.numpy as jnp
import numpy as np
from jax import lax
from jax.experimental import pallas as pl
from jax.experimental.pallas import tpu as pltpu
from jax.sharding import PartitionSpec as P

step_size = 0.5
highest_total = 4
row_tile = 16
pieces = 2
MIB = 1024 * 1024
f32 = jnp.float32
bf16 = jnp.bfloat16


def index_rows(slots, modes):
    entries = [()]
    for _ in range(modes):
        entries = [
            entry + (level,)
            for entry in entries
            for level in range(highest_total + 1)
            if sum(entry) + level <= highest_total
        ]
    return sorted(entries, key=lambda entry: (sum(entry), entry))[:slots]


def coupled_to(rows):
    lookup = {entry: place for place, entry in enumerate(rows)}
    result = []
    for entry in rows:
        terms = []
        for mode, level in enumerate(entry):
            raised = entry[:mode] + (level + 1,) + entry[mode + 1 :]
            if raised in lookup:
                terms.append((lookup[raised], mode, True, 1))
            if level > 0:
                lowered = entry[:mode] + (level - 1,) + entry[mode + 1 :]
                terms.append((lookup[lowered], mode, False, level))
        result.append(terms)
    return result


def smaller_class(rows):
    classes = [[c for c, entry in enumerate(rows) if sum(entry) % 2 == rest] for rest in (0, 1)]
    return min(classes, key=len)


def params(megabytes):
    return pltpu.CompilerParams(vmem_limit_bytes=megabytes * MIB)


def whole():
    return pl.BlockSpec(memory_space=pltpu.VMEM)


def anywhere():
    return pl.BlockSpec(memory_space=pl.ANY)


def scalars():
    return pl.BlockSpec(memory_space=pltpu.SMEM)


def swap(array, axis, size, bit):
    return lax.ppermute(array, axis, [(i, i ^ bit) for i in range(size)])


def tie(arrays):
    return lax.optimization_barrier(arrays)


def row_bits(size):
    return [1 << i for i in reversed(range(size.bit_length() - 1))]


def tree(array, size, bits):
    parts = {0: array}
    for bit in bits:
        for mask in list(parts):
            parts[mask ^ bit] = swap(parts[mask], "row", size, bit)
    return [parts[mask] for mask in sorted(parts)]


def section_kernel(group, where, _, state, slope, *refs):
    extra, section, chunks = refs[: -group - 1], refs[-group - 1], refs[-group:]
    value = (state[...].astype(f32) + (0.5 * step_size) * slope[...]).astype(bf16)
    section[...] = value
    width = chunks[0].shape[-1]
    for b, chunk in enumerate(chunks):
        columns = pl.ds(pl.multiple_of((where[0] ^ b) * width, 128), width)
        chunk[...] = section[:, :, :, columns]
    if extra:
        source, target = extra

        @pl.when(pl.program_id(0) == 0)
        def _():
            target[...] = source[...]


def make_section(p, split, state, prev_slope, place, half_at, group, hamiltonian=None):
    ops, parts, rows, columns = state.shape
    height, width = rows // split, columns // group
    block = pl.BlockSpec((1, 1, height, columns), lambda a, x, *_: (a, x, p, 0))
    out = pl.BlockSpec((1, 1, height, columns), lambda a, x, *_: (a, x, 0, 0))
    chunk = pl.BlockSpec((1, 1, height, width), lambda a, x, *_: (a, x, 0, 0))
    half = (1, rows, columns // 2)
    extra = [] if hamiltonian is None else [hamiltonian]
    return pl.pallas_call(
        functools.partial(section_kernel, group),
        grid_spec=pltpu.PrefetchScalarGridSpec(
            num_scalar_prefetch=2,
            grid=(ops, parts),
            in_specs=[block, block] + [pl.BlockSpec(half, lambda a, x, _, h: (jnp.where(a == 0, x, parts - 1), 0, h[0])) for _ in extra],
            out_specs=[pl.BlockSpec(half, lambda a, x, *_: (jnp.where(a == 0, x, parts - 1), 0, 0)) for _ in extra]
            + [out]
            + [chunk] * group,
        ),
        out_shape=[jax.ShapeDtypeStruct((parts, *half[1:]), bf16) for _ in extra]
        + [jax.ShapeDtypeStruct((ops, parts, height, columns), bf16)]
        + [jax.ShapeDtypeStruct((ops, parts, height, width), bf16)] * group,
        compiler_params=params(54 if p == 0 else 16),
        cost_estimate=pl.CostEstimate(flops=1, bytes_accessed=1, transcendentals=0),
        name="section",
    )(place, half_at, state, prev_slope, *extra)


def fill_factors(vrows, vcols, coupling, factors):
    modes = vrows.shape[0]
    for k in range(modes):
        first = vrows[k]
        second = vcols[k : k + 1, :]
        diff = first - second
        factors[k] = diff
        factors[modes + k] = coupling[0, k] * diff
        factors[2 * modes + k] = coupling[1, k] * (first + second)


def add_terms(terms, places, held, factors, modes, rows, real, imag):
    for other, mode, child, count in terms:
        place = places[other]
        x_real = held[place, 0, rows, :].astype(f32)
        x_imag = held[place, 1, rows, :].astype(f32)
        if child:
            diff = factors[mode, rows, :]
            real = real + diff * x_imag
            imag = imag - diff * x_real
        else:
            first = factors[modes + mode, rows, :]
            second = factors[2 * modes + mode, rows, :]
            if count != 1:
                first, second = count * first, count * second
            real = real + (first * x_imag + second * x_real)
            imag = imag + (second * x_imag - first * x_real)
    return real, imag


def partial_kernel(links, sides, group, places, coupling, vrows, vcols, *refs):
    chunks, out, held, factors, sem = refs[:group], *refs[group:]
    modes = vrows.shape[0]
    height, width = held.shape[2:]
    ops = chunks[0].shape[0]
    empty = group * ops
    load = pltpu.make_async_copy(chunks[0], held.at[pl.ds(0, ops)], sem)
    load.start()
    fill_factors(vrows, vcols, coupling, factors)
    for b in range(1, group):
        held[b * ops : (b + 1) * ops] = chunks[b][...]
    held[empty] = jnp.zeros(held.shape[1:], bf16)
    load.wait()
    for u, c in enumerate(sides):

        @pl.when(places[c] < empty)
        def _():
            out[u] = held[places[c]]

        @pl.when(places[c] == empty)
        def _():
            @pl.loop(0, height // row_tile, unroll=2)
            def _(i):
                rows = pl.ds(pl.multiple_of(i * row_tile, row_tile), row_tile)
                zero = jnp.zeros((row_tile, width), f32)
                real, imag = add_terms(links[c], places, held, factors, modes, rows, zero, zero)
                out[u, 0, rows, :] = real.astype(bf16)
                out[u, 1, rows, :] = imag.astype(bf16)


def coupled_kernel(links, sides, group, places, coupling, vrows, vcols, *refs):
    chunks, received, outs = refs[:group], refs[group], refs[group + 1 : 2 * group + 1]
    held, done, factors, spots, sem = refs[2 * group + 1 :]
    modes = vrows.shape[0]
    height, width = held.shape[2:]
    ops = chunks[0].shape[0]
    empty = group * ops
    load = pltpu.make_async_copy(chunks[0], held.at[pl.ds(0, ops)], sem)
    load.start()
    fill_factors(vrows, vcols, coupling, factors)
    for b in range(1, group):
        held[b * ops : (b + 1) * ops] = chunks[b][...]
    held[empty] = jnp.zeros(held.shape[1:], bf16)
    held[empty + 1 :] = received[...]
    load.wait()
    for c in range(len(links)):
        spots[c] = places[c]
    for u, c in enumerate(sides):
        spots[c] = jnp.where(places[c] == empty, empty + 1 + u, places[c])
    for c in range(len(links)):

        @pl.when(places[c] < empty)
        def _():
            @pl.loop(0, height // row_tile, unroll=2)
            def _(i):
                rows = pl.ds(pl.multiple_of(i * row_tile, row_tile), row_tile)
                if c in sides:
                    u = empty + 1 + sides.index(c)
                    real, imag = held[u, 0, rows, :].astype(f32), held[u, 1, rows, :].astype(f32)
                else:
                    real = imag = jnp.zeros((row_tile, width), f32)
                real, imag = add_terms(links[c], spots, held, factors, modes, rows, real, imag)
                done[places[c], 0, rows, :] = real.astype(bf16)
                done[places[c], 1, rows, :] = imag.astype(bf16)

    for b, out in enumerate(outs):
        out[...] = done[b * ops : (b + 1) * ops]


def coupling_scratch(entries, height, width, modes):
    return [pltpu.VMEM((entries, 2, height, width), bf16)], [pltpu.VMEM((3 * modes, height, width), f32)]


def make_partial(chunks, places, coupling, vrows, vcols, links, sides):
    group = len(chunks)
    ops, _, height, width = chunks[0].shape
    held, factors = coupling_scratch(group * ops + 1, height, width, vrows.shape[0])
    size = height * width
    return pl.pallas_call(
        functools.partial(partial_kernel, links, sides, group),
        in_specs=[scalars(), scalars(), whole(), whole(), anywhere()] + [whole()] * (group - 1),
        out_specs=whole(),
        out_shape=jax.ShapeDtypeStruct((len(sides), 2, height, width), bf16),
        scratch_shapes=held + factors + [pltpu.SemaphoreType.DMA],
        compiler_params=params(12),
        cost_estimate=pl.CostEstimate(
            flops=40 * len(sides) * size,
            bytes_accessed=4 * size * (group * ops + len(sides)),
            transcendentals=0,
        ),
        name="partial_sums",
    )(places, coupling, vrows, vcols, *chunks)


def make_coupled(chunks, received, places, coupling, vrows, vcols, links, sides):
    group = len(chunks)
    ops, _, height, width = chunks[0].shape
    held, factors = coupling_scratch(group * ops + 1 + len(sides), height, width, vrows.shape[0])
    size = height * width
    return pl.pallas_call(
        functools.partial(coupled_kernel, links, sides, group),
        in_specs=[scalars(), scalars(), whole(), whole(), anywhere()] + [whole()] * group,
        out_specs=[whole()] * group,
        out_shape=[jax.ShapeDtypeStruct(chunks[0].shape, bf16)] * group,
        scratch_shapes=held
        + [pltpu.VMEM((group * ops, 2, height, width), bf16)]
        + factors
        + [pltpu.SMEM((len(links),), jnp.int32), pltpu.SemaphoreType.DMA],
        compiler_params=params(16),
        cost_estimate=pl.CostEstimate(flops=1, bytes_accessed=1, transcendentals=0),
        name="coupling_sums",
    )(places, coupling, vrows, vcols, *chunks, received)


def complex_rows(left, right):
    _, height, depth = left.shape
    left = left.reshape(2 * height, depth)
    first = jnp.dot(left, right[0], preferred_element_type=f32)
    second = jnp.dot(left, right[1], preferred_element_type=f32)
    return first[:height] - second[height:], second[:height] + first[height:]


def right_kernel(split, count, where, decay, h_own, *refs):
    sections, refs, (out, h_all) = refs[:split], refs[split:-2], refs[-2:]
    h_near, h_far = refs[: 2 * count - 2], refs[2 * count - 2 :]
    j, a = pl.program_id(0), pl.program_id(1)
    rows, size = h_own.shape[1:]
    height, tile = sections[0].shape[2], out.shape[3]
    half, block = size // 2, size // 4
    own = pl.multiple_of((where[0] // count) * half, half)
    other = pl.multiple_of(half - own, half)

    @pl.when(jnp.logical_and(j == 0, a == 0))
    def _():
        for b in range(count):
            place = pl.multiple_of((where[0] ^ b) * rows, row_tile)
            for x in range(2):
                near = h_near[2 * b - 2 + x][...] if b else h_own[x]
                h_all[x, pl.ds(place, rows), :] = near
            place = pl.multiple_of((where[0] ^ (count + b)) * rows, row_tile)
            h_all[:, pl.ds(place, rows), pl.ds(other, half)] = h_far[b][...]
        for r in range(0, half, block):
            for c in range(0, half, block):
                here = pl.ds(pl.multiple_of(own + r, block), block)
                there = pl.ds(pl.multiple_of(other + c, block), block)
                h_all[0, there, here] = h_all[0, here, there].T
                h_all[1, there, here] = -h_all[1, here, there].T

    columns = pl.ds(pl.multiple_of(j * tile, 128), tile)
    lost = decay[a]
    for p, section in enumerate(sections):
        real, imag = complex_rows(section[a], h_all.at[:, :, columns])
        here = slice(p * height, (p + 1) * height)
        out[0, 0, here, :] = -imag - lost * section[a, 0, :, columns].astype(f32)
        out[0, 1, here, :] = real - lost * section[a, 1, :, columns].astype(f32)


def make_right(sections, h_own, bundles, h_far, place, decay):
    ops, _, height, columns = sections[0].shape
    split, count = len(sections), len(h_far)
    rows, tile = height * split, min(columns, 512)
    held = pl.BlockSpec((ops, 2, height, columns), lambda j, a: (0, 0, 0, 0))
    return pl.pallas_call(
        functools.partial(right_kernel, split, count),
        grid=(columns // tile, ops),
        in_specs=[scalars(), scalars(), pl.BlockSpec(h_own.shape, lambda j, a: (0, 0, 0))]
        + [held] * split
        + [pl.BlockSpec((rows, columns), lambda j, a, x=x: (ops + x, 0)) for x in range(2)]
        * len(bundles)
        + [pl.BlockSpec(h.shape, lambda j, a: (0, 0, 0)) for h in h_far],
        out_specs=pl.BlockSpec((1, 2, rows, tile), lambda j, a: (a, 0, 0, j)),
        out_shape=jax.ShapeDtypeStruct((ops, 2, rows, columns), f32),
        scratch_shapes=[pltpu.VMEM((2, columns, columns), bf16)],
        compiler_params=params(28),
        cost_estimate=pl.CostEstimate(
            flops=8 * ops * rows * columns * columns,
            bytes_accessed=4 * columns * (columns + 3 * ops * rows),
            transcendentals=0,
        ),
        name="right_products",
    )(place, decay, h_own, *sections, *[h for h in bundles for _ in range(2)], *h_far)


def left_kernel(count, where, h_own, base, *refs):
    s_parts, (out, s_all) = refs[:count], refs[count:]
    height, tile = s_parts[0].shape[2:]
    for b in range(count):
        place = pl.ds(pl.multiple_of((where[0] ^ b) * height, row_tile), height)
        s_all[:, place, :] = s_parts[b][...].reshape(2, height, tile)
    real, imag = complex_rows(h_own[...], s_all)
    out[0, 0] = base[0, 0] + imag
    out[0, 1] = base[0, 1] - real


def make_left(s_parts, h_columns, base, place):
    ops, _, height, columns = s_parts[0].shape
    count, rows, tile = len(s_parts), base.shape[2], min(columns, 512)
    block = pl.BlockSpec((1, 2, rows, tile), lambda j, a: (a, 0, 0, j))
    return pl.pallas_call(
        functools.partial(left_kernel, count),
        grid=(columns // tile, ops),
        in_specs=[
            scalars(),
            pl.BlockSpec(h_columns.shape, lambda j, a: (0, 0, 0)),
            block,
        ]
        + [
            pl.BlockSpec((1, 2, height, tile), lambda j, a: (a, 0, 0, j))
            if part.ndim == 4
            else pl.BlockSpec((2 * height, tile), lambda j, a: (a, j))
            for part in s_parts
        ],
        out_specs=block,
        out_shape=jax.ShapeDtypeStruct(base.shape, f32),
        scratch_shapes=[pltpu.VMEM((2, count * height, tile), bf16)],
        compiler_params=params(16),
        cost_estimate=pl.CostEstimate(
            flops=8 * ops * rows * columns * count * height,
            bytes_accessed=4 * ops * columns * (count * height + 4 * rows),
            transcendentals=0,
        ),
        name="left_products",
    )(place, h_columns, base, *s_parts)


def final_kernel(group, where, base, accumulated, *refs):
    sums, (slope, total) = refs[:group], refs[-2:]
    j = pl.program_id(1)
    tile, width = slope.shape[3], sums[0].shape[3]
    for b in range(group):
        first = (where[0] ^ b) * width - j * tile

        @pl.when(jnp.logical_and(first >= 0, first < tile))
        def _():
            columns = pl.ds(pl.multiple_of(first, 128), width)
            value = base[0, :, :, columns] + sums[b][0].astype(f32)
            slope[0, :, :, columns] = value
            total[0, :, :, columns] = accumulated[0, :, :, columns] + (step_size / 3.0) * value


def make_final(p, split, base, accumulated, sums, place, earlier=()):
    ops, parts, rows, columns = base.shape
    group = len(sums)
    height, width, tile = rows // split, sums[0].shape[3], min(columns, 512)
    block = pl.BlockSpec((1, parts, height, tile), lambda a, j, _: (a, 0, p, j))
    chunk = pl.BlockSpec((1, parts, height, width), lambda a, j, _: (a, 0, 0, 0))
    return pl.pallas_call(
        functools.partial(final_kernel, group),
        grid_spec=pltpu.PrefetchScalarGridSpec(
            num_scalar_prefetch=1,
            grid=(ops, columns // tile),
            in_specs=[block, block] + [chunk] * group + [anywhere()] * len(earlier),
            out_specs=[block, block],
        ),
        out_shape=[jax.ShapeDtypeStruct(base.shape, f32)] * 2,
        input_output_aliases={3 + group + k: k for k in range(len(earlier))},
        compiler_params=params(16),
        cost_estimate=pl.CostEstimate(
            flops=4 * base.size // split,
            bytes_accessed=18 * base.size // split,
            transcendentals=0,
        ),
        name="outputs",
    )(place, base, accumulated, *sums, *earlier)


def shards(
    hier,
    row,
    state,
    prev_slope,
    accumulated,
    hamiltonian,
    couple_v,
    coupling,
    damping,
    occupation,
    parents,
    children,
):
    ops, _, rows, columns = state.shape
    modes = occupation.shape[1]
    group = hier // 2
    width = columns // group
    split = pieces
    height = rows // split
    table = index_rows(hier * ops, modes)
    links, sides = coupled_to(table), smaller_class(table)

    hier_at, row_at = lax.axis_index("hier"), lax.axis_index("row")
    own = hier_at % group
    own_place, row_place = own.reshape(1).astype(jnp.int32), row_at.reshape(1).astype(jnp.int32)

    bits = row_bits(row)
    top, low = bits[0], bits[1:]

    def spread(p):
        return [chunks[p][0]] + [swap(chunks[p][b], "hier", hier, b) for b in range(1, group)]

    def partial(p):
        return make_partial(got[p], places, coupling, heres[p], vcols, links, sides)

    def coupled(p):
        return make_coupled(got[p], received[p], places, coupling, heres[p], vcols, links, sides)

    def gather_back(done):
        return [done[0]] + [swap(done[b], "hier", hier, b) for b in range(1, group)]

    got, sent, received, sums, outs = [], [], [], [], []

    half = [occupation] + [swap(occupation, "hier", hier, b) for b in range(1, group)]
    half_at = (row_at // (row // 2)).reshape(1).astype(jnp.int32)
    half_columns, first, *first_chunks = make_section(
        0, split, state, prev_slope, own_place, half_at, group, hamiltonian
    )
    half_columns, first, first_chunks, half, state, prev_slope, couple_v, hamiltonian = tie(
        (half_columns, first, first_chunks, half, state, prev_slope, couple_v, hamiltonian)
    )

    h_top = swap(half_columns, "row", row, top)
    second, *second_chunks = make_section(
        1, split, state, prev_slope, own_place, half_at, group
    )
    chunks, sections = [first_chunks, second_chunks], [first, second]
    got.append(spread(0))

    known = jnp.asarray(np.array(table, np.int32))
    found = jnp.concatenate(half, axis=0)
    same = jnp.all(found[None, :, :] == known[:, None, :], axis=2)
    spot = jnp.arange(group * ops, dtype=jnp.int32)[None, :]
    places = jnp.min(jnp.where(same, spot, group * ops), axis=1).astype(jnp.int32)
    vrows = lax.dynamic_slice_in_dim(couple_v, row_at * rows, rows, 1)[:, :, None]
    vcols = lax.dynamic_slice_in_dim(couple_v, own * width, width, 1)
    heres = [vrows[:, p * height : (p + 1) * height] for p in range(split)]
    decay = jnp.sum(half[0].astype(f32) * damping[None, :], axis=1)
    got, chunks, sections, places, heres, vcols, decay, h_top, kept = tie(
        (got, chunks, sections, places, heres, vcols, decay, h_top, hamiltonian)
    )

    sent.append(partial(0))
    received.append(swap(sent[0], "hier", hier, group))
    got.append(spread(1))
    across = swap(sections[0], "row", row, top)
    near = jnp.concatenate([sections[0].reshape(-1, columns), kept.reshape(-1, columns)])
    blocks = kept.reshape(2, rows, row, split, height)
    h_columns = [blocks[:, :, :, p].reshape(2, rows, row * height) for p in range(split)]
    got, received, across, sections, h_top, near, h_columns = tie(
        (got, received, across, sections, h_top, near, h_columns)
    )

    sent.append(partial(1))
    received.append(swap(sent[1], "hier", hier, group))
    last_across = swap(sections[1], "row", row, top)
    near, s_far, h_far = tree(near, row, low), tree(across, row, low), tree(h_top, row, low)
    done, near, s_far, h_far = tie((coupled(0), near, s_far, h_far))
    sums.append(gather_back(done))
    base = make_right(sections, hamiltonian, near[1:], h_far, row_place, decay)
    base = make_left([sections[0], *near[1:], *s_far], h_columns[0], base, row_place)
    received, last_across, base = tie((received, last_across, base))

    done, sums, last_across, last_own = tie((coupled(1), sums, last_across, sections[1]))
    sums.append(gather_back(done))
    s_parts = tree(last_own, row, low) + tree(last_across, row, low)
    base = make_left(s_parts, h_columns[1], base, row_place)
    for p in range(split):
        outs = make_final(p, split, base, accumulated, sums[p], own_place, outs)
    slope, total = outs
    return slope, total


def solution(mesh):
    return jax.shard_map(
        functools.partial(shards, mesh.shape["hier"], mesh.shape["row"]),
        mesh=mesh,
        in_specs=(
            P("hier", None, "row", None),
            P("hier", None, "row", None),
            P("hier", None, "row", None),
            P(None, "row", None),
            P(),
            P(),
            P(),
            P("hier", None),
            P("hier", None),
            P("hier", None),
        ),
        out_specs=(P("hier", None, "row", None), P("hier", None, "row", None)),
        check_vma=False,
    )
```

```python
import functools

import jax
import jax.numpy as jnp
import numpy as np
from jax import lax
from jax.experimental import pallas as pl
from jax.experimental.pallas import tpu as pltpu
from jax.sharding import PartitionSpec as P

step_size = 0.5
highest_total = 4
row_tile = 16
pieces = 2
MIB = 1024 * 1024
f32 = jnp.float32
bf16 = jnp.bfloat16


def index_rows(slots, modes):
    entries = [()]
    for _ in range(modes):
        entries = [
            entry + (level,)
            for entry in entries
            for level in range(highest_total + 1)
            if sum(entry) + level <= highest_total
        ]
    return sorted(entries, key=lambda entry: (sum(entry), entry))[:slots]


def coupled_to(rows):
    lookup = {entry: place for place, entry in enumerate(rows)}
    result = []
    for entry in rows:
        terms = []
        for mode, level in enumerate(entry):
            raised = entry[:mode] + (level + 1,) + entry[mode + 1 :]
            if raised in lookup:
                terms.append((lookup[raised], mode, True, 1))
            if level > 0:
                lowered = entry[:mode] + (level - 1,) + entry[mode + 1 :]
                terms.append((lookup[lowered], mode, False, level))
        result.append(terms)
    return result


def smaller_class(rows):
    classes = [[c for c, entry in enumerate(rows) if sum(entry) % 2 == rest] for rest in (0, 1)]
    return min(classes, key=len)


def params(megabytes):
    return pltpu.CompilerParams(vmem_limit_bytes=megabytes * MIB)


def whole():
    return pl.BlockSpec(memory_space=pltpu.VMEM)


def anywhere():
    return pl.BlockSpec(memory_space=pl.ANY)


def scalars():
    return pl.BlockSpec(memory_space=pltpu.SMEM)


def swap(array, axis, size, bit):
    return lax.ppermute(array, axis, [(i, i ^ bit) for i in range(size)])


def tie(arrays):
    return lax.optimization_barrier(arrays)


def row_bits(size):
    return [1 << i for i in reversed(range(size.bit_length() - 1))]


def tree(array, size, bits):
    parts = {0: array}
    for bit in bits:
        for mask in list(parts):
            parts[mask ^ bit] = swap(parts[mask], "row", size, bit)
    return [parts[mask] for mask in sorted(parts)]


def section_kernel(group, where, _, state, slope, *refs):
    extra, section, chunks = refs[: -group - 1], refs[-group - 1], refs[-group:]
    value = (state[...].astype(f32) + (0.5 * step_size) * slope[...]).astype(bf16)
    section[...] = value
    width = chunks[0].shape[-1]
    for b, chunk in enumerate(chunks):
        columns = pl.ds(pl.multiple_of((where[0] ^ b) * width, 128), width)
        chunk[...] = section[:, :, :, columns]
    if extra:
        source, target = extra

        @pl.when(pl.program_id(0) == 0)
        def _():
            target[...] = source[...]


def make_section(p, split, state, prev_slope, place, half_at, group, hamiltonian=None):
    ops, parts, rows, columns = state.shape
    height, width = rows // split, columns // group
    block = pl.BlockSpec((1, parts, height, columns), lambda a, *_: (a, 0, p, 0))
    out = pl.BlockSpec((1, parts, height, columns), lambda a, *_: (a, 0, 0, 0))
    chunk = pl.BlockSpec((1, parts, height, width), lambda a, *_: (a, 0, 0, 0))
    half = (2, rows, columns // 2)
    extra = [] if hamiltonian is None else [hamiltonian]
    return pl.pallas_call(
        functools.partial(section_kernel, group),
        grid_spec=pltpu.PrefetchScalarGridSpec(
            num_scalar_prefetch=2,
            grid=(ops,),
            in_specs=[block, block] + [pl.BlockSpec(half, lambda a, _, h: (0, 0, h[0])) for _ in extra],
            out_specs=[pl.BlockSpec(half, lambda a, *_: (0, 0, 0)) for _ in extra]
            + [out]
            + [chunk] * group,
        ),
        out_shape=[jax.ShapeDtypeStruct(half, bf16) for _ in extra]
        + [jax.ShapeDtypeStruct((ops, parts, height, columns), bf16)]
        + [jax.ShapeDtypeStruct((ops, parts, height, width), bf16)] * group,
        compiler_params=params(60 if p == 0 else 16),
        cost_estimate=pl.CostEstimate(flops=1, bytes_accessed=1, transcendentals=0),
        name="section",
    )(place, half_at, state, prev_slope, *extra)


def fill_factors(vrows, vcols, coupling, factors):
    modes = vrows.shape[0]
    for k in range(modes):
        first = vrows[k]
        second = vcols[k : k + 1, :]
        diff = first - second
        factors[k] = diff
        factors[modes + k] = coupling[0, k] * diff
        factors[2 * modes + k] = coupling[1, k] * (first + second)


def add_terms(terms, places, held, factors, modes, rows, real, imag):
    for other, mode, child, count in terms:
        place = places[other]
        x_real = held[place, 0, rows, :].astype(f32)
        x_imag = held[place, 1, rows, :].astype(f32)
        if child:
            diff = factors[mode, rows, :]
            real = real + diff * x_imag
            imag = imag - diff * x_real
        else:
            first = factors[modes + mode, rows, :]
            second = factors[2 * modes + mode, rows, :]
            if count != 1:
                first, second = count * first, count * second
            real = real + (first * x_imag + second * x_real)
            imag = imag + (second * x_imag - first * x_real)
    return real, imag


def partial_kernel(links, sides, group, places, coupling, vrows, vcols, *refs):
    chunks, out, held, factors, sem = refs[:group], *refs[group:]
    modes = vrows.shape[0]
    height, width = held.shape[2:]
    ops = chunks[0].shape[0]
    empty = group * ops
    load = pltpu.make_async_copy(chunks[0], held.at[pl.ds(0, ops)], sem)
    load.start()
    fill_factors(vrows, vcols, coupling, factors)
    for b in range(1, group):
        held[b * ops : (b + 1) * ops] = chunks[b][...]
    held[empty] = jnp.zeros(held.shape[1:], bf16)
    load.wait()
    for u, c in enumerate(sides):

        @pl.when(places[c] < empty)
        def _():
            out[u] = held[places[c]]

        @pl.when(places[c] == empty)
        def _():
            @pl.loop(0, height // row_tile, unroll=2)
            def _(i):
                rows = pl.ds(pl.multiple_of(i * row_tile, row_tile), row_tile)
                zero = jnp.zeros((row_tile, width), f32)
                real, imag = add_terms(links[c], places, held, factors, modes, rows, zero, zero)
                out[u, 0, rows, :] = real.astype(bf16)
                out[u, 1, rows, :] = imag.astype(bf16)


def coupled_kernel(links, sides, group, places, coupling, vrows, vcols, *refs):
    chunks, received, outs = refs[:group], refs[group], refs[group + 1 : 2 * group + 1]
    held, done, factors, spots, sem = refs[2 * group + 1 :]
    modes = vrows.shape[0]
    height, width = held.shape[2:]
    ops = chunks[0].shape[0]
    empty = group * ops
    load = pltpu.make_async_copy(chunks[0], held.at[pl.ds(0, ops)], sem)
    load.start()
    fill_factors(vrows, vcols, coupling, factors)
    for b in range(1, group):
        held[b * ops : (b + 1) * ops] = chunks[b][...]
    held[empty] = jnp.zeros(held.shape[1:], bf16)
    held[empty + 1 :] = received[...]
    load.wait()
    for c in range(len(links)):
        spots[c] = places[c]
    for u, c in enumerate(sides):
        spots[c] = jnp.where(places[c] == empty, empty + 1 + u, places[c])
    for c in range(len(links)):

        @pl.when(places[c] < empty)
        def _():
            @pl.loop(0, height // row_tile, unroll=2)
            def _(i):
                rows = pl.ds(pl.multiple_of(i * row_tile, row_tile), row_tile)
                if c in sides:
                    u = empty + 1 + sides.index(c)
                    real, imag = held[u, 0, rows, :].astype(f32), held[u, 1, rows, :].astype(f32)
                else:
                    real = imag = jnp.zeros((row_tile, width), f32)
                real, imag = add_terms(links[c], spots, held, factors, modes, rows, real, imag)
                done[places[c], 0, rows, :] = real.astype(bf16)
                done[places[c], 1, rows, :] = imag.astype(bf16)

    for b, out in enumerate(outs):
        out[...] = done[b * ops : (b + 1) * ops]


def coupling_scratch(entries, height, width, modes):
    return [pltpu.VMEM((entries, 2, height, width), bf16)], [pltpu.VMEM((3 * modes, height, width), f32)]


def make_partial(chunks, places, coupling, vrows, vcols, links, sides):
    group = len(chunks)
    ops, _, height, width = chunks[0].shape
    held, factors = coupling_scratch(group * ops + 1, height, width, vrows.shape[0])
    size = height * width
    return pl.pallas_call(
        functools.partial(partial_kernel, links, sides, group),
        in_specs=[scalars(), scalars(), whole(), whole(), anywhere()] + [whole()] * (group - 1),
        out_specs=whole(),
        out_shape=jax.ShapeDtypeStruct((len(sides), 2, height, width), bf16),
        scratch_shapes=held + factors + [pltpu.SemaphoreType.DMA],
        compiler_params=params(12),
        cost_estimate=pl.CostEstimate(
            flops=40 * len(sides) * size,
            bytes_accessed=4 * size * (group * ops + len(sides)),
            transcendentals=0,
        ),
        name="partial_sums",
    )(places, coupling, vrows, vcols, *chunks)


def make_coupled(chunks, received, places, coupling, vrows, vcols, links, sides):
    group = len(chunks)
    ops, _, height, width = chunks[0].shape
    held, factors = coupling_scratch(group * ops + 1 + len(sides), height, width, vrows.shape[0])
    size = height * width
    return pl.pallas_call(
        functools.partial(coupled_kernel, links, sides, group),
        in_specs=[scalars(), scalars(), whole(), whole(), anywhere()] + [whole()] * group,
        out_specs=[whole()] * group,
        out_shape=[jax.ShapeDtypeStruct(chunks[0].shape, bf16)] * group,
        scratch_shapes=held
        + [pltpu.VMEM((group * ops, 2, height, width), bf16)]
        + factors
        + [pltpu.SMEM((len(links),), jnp.int32), pltpu.SemaphoreType.DMA],
        compiler_params=params(16),
        cost_estimate=pl.CostEstimate(flops=1, bytes_accessed=1, transcendentals=0),
        name="coupling_sums",
    )(places, coupling, vrows, vcols, *chunks, received)


def complex_rows(left, right):
    _, height, depth = left.shape
    left = left.reshape(2 * height, depth)
    first = jnp.dot(left, right[0], preferred_element_type=f32)
    second = jnp.dot(left, right[1], preferred_element_type=f32)
    return first[:height] - second[height:], second[:height] + first[height:]


def right_kernel(split, count, where, decay, h_own, *refs):
    sections, refs, (out, h_all) = refs[:split], refs[split:-2], refs[-2:]
    h_near, h_far = refs[: 2 * count - 2], refs[2 * count - 2 :]
    j, a = pl.program_id(0), pl.program_id(1)
    rows, size = h_own.shape[1:]
    height, tile = sections[0].shape[2], out.shape[3]
    half, block = size // 2, size // 4
    own = pl.multiple_of((where[0] // count) * half, half)
    other = pl.multiple_of(half - own, half)

    @pl.when(jnp.logical_and(j == 0, a == 0))
    def _():
        for b in range(count):
            place = pl.multiple_of((where[0] ^ b) * rows, row_tile)
            for x in range(2):
                near = h_near[2 * b - 2 + x][...] if b else h_own[x]
                h_all[x, pl.ds(place, rows), :] = near
            place = pl.multiple_of((where[0] ^ (count + b)) * rows, row_tile)
            h_all[:, pl.ds(place, rows), pl.ds(other, half)] = h_far[b][...]
        for r in range(0, half, block):
            for c in range(0, half, block):
                here = pl.ds(pl.multiple_of(own + r, block), block)
                there = pl.ds(pl.multiple_of(other + c, block), block)
                h_all[0, there, here] = h_all[0, here, there].T
                h_all[1, there, here] = -h_all[1, here, there].T

    columns = pl.ds(pl.multiple_of(j * tile, 128), tile)
    lost = decay[a]
    for p, section in enumerate(sections):
        real, imag = complex_rows(section[a], h_all.at[:, :, columns])
        here = slice(p * height, (p + 1) * height)
        out[0, 0, here, :] = -imag - lost * section[a, 0, :, columns].astype(f32)
        out[0, 1, here, :] = real - lost * section[a, 1, :, columns].astype(f32)


def make_right(sections, h_own, bundles, h_far, place, decay):
    ops, _, height, columns = sections[0].shape
    split, count = len(sections), len(h_far)
    rows, tile = height * split, min(columns, 512)
    held = pl.BlockSpec((ops, 2, height, columns), lambda j, a: (0, 0, 0, 0))
    return pl.pallas_call(
        functools.partial(right_kernel, split, count),
        grid=(columns // tile, ops),
        in_specs=[scalars(), scalars(), pl.BlockSpec(h_own.shape, lambda j, a: (0, 0, 0))]
        + [held] * split
        + [pl.BlockSpec((rows, columns), lambda j, a, x=x: (ops + x, 0)) for x in range(2)]
        * len(bundles)
        + [pl.BlockSpec(h.shape, lambda j, a: (0, 0, 0)) for h in h_far],
        out_specs=pl.BlockSpec((1, 2, rows, tile), lambda j, a: (a, 0, 0, j)),
        out_shape=jax.ShapeDtypeStruct((ops, 2, rows, columns), f32),
        scratch_shapes=[pltpu.VMEM((2, columns, columns), bf16)],
        compiler_params=params(28),
        cost_estimate=pl.CostEstimate(
            flops=8 * ops * rows * columns * columns,
            bytes_accessed=4 * columns * (columns + 3 * ops * rows),
            transcendentals=0,
        ),
        name="right_products",
    )(place, decay, h_own, *sections, *[h for h in bundles for _ in range(2)], *h_far)


def left_kernel(count, where, h_own, base, *refs):
    s_parts, (out, s_all) = refs[:count], refs[count:]
    height, tile = s_parts[0].shape[2:]
    for b in range(count):
        place = pl.ds(pl.multiple_of((where[0] ^ b) * height, row_tile), height)
        s_all[:, place, :] = s_parts[b][...].reshape(2, height, tile)
    real, imag = complex_rows(h_own[...], s_all)
    out[0, 0] = base[0, 0] + imag
    out[0, 1] = base[0, 1] - real


def make_left(s_parts, h_columns, base, place):
    ops, _, height, columns = s_parts[0].shape
    count, rows, tile = len(s_parts), base.shape[2], min(columns, 512)
    block = pl.BlockSpec((1, 2, rows, tile), lambda j, a: (a, 0, 0, j))
    return pl.pallas_call(
        functools.partial(left_kernel, count),
        grid=(columns // tile, ops),
        in_specs=[
            scalars(),
            pl.BlockSpec(h_columns.shape, lambda j, a: (0, 0, 0)),
            block,
        ]
        + [
            pl.BlockSpec((1, 2, height, tile), lambda j, a: (a, 0, 0, j))
            if part.ndim == 4
            else pl.BlockSpec((2 * height, tile), lambda j, a: (a, j))
            for part in s_parts
        ],
        out_specs=block,
        out_shape=jax.ShapeDtypeStruct(base.shape, f32),
        scratch_shapes=[pltpu.VMEM((2, count * height, tile), bf16)],
        compiler_params=params(16),
        cost_estimate=pl.CostEstimate(
            flops=8 * ops * rows * columns * count * height,
            bytes_accessed=4 * ops * columns * (count * height + 4 * rows),
            transcendentals=0,
        ),
        name="left_products",
    )(place, h_columns, base, *s_parts)


def final_kernel(group, where, base, accumulated, *refs):
    sums, (slope, total) = refs[:group], refs[-2:]
    j = pl.program_id(1)
    tile, width = slope.shape[3], sums[0].shape[3]
    for b in range(group):
        first = (where[0] ^ b) * width - j * tile

        @pl.when(jnp.logical_and(first >= 0, first < tile))
        def _():
            columns = pl.ds(pl.multiple_of(first, 128), width)
            value = base[0, :, :, columns] + sums[b][0].astype(f32)
            slope[0, :, :, columns] = value
            total[0, :, :, columns] = accumulated[0, :, :, columns] + (step_size / 3.0) * value


def make_final(p, split, base, accumulated, sums, place, earlier=()):
    ops, parts, rows, columns = base.shape
    group = len(sums)
    height, width, tile = rows // split, sums[0].shape[3], min(columns, 512)
    block = pl.BlockSpec((1, parts, height, tile), lambda a, j, _: (a, 0, p, j))
    chunk = pl.BlockSpec((1, parts, height, width), lambda a, j, _: (a, 0, 0, 0))
    return pl.pallas_call(
        functools.partial(final_kernel, group),
        grid_spec=pltpu.PrefetchScalarGridSpec(
            num_scalar_prefetch=1,
            grid=(ops, columns // tile),
            in_specs=[block, block] + [chunk] * group + [anywhere()] * len(earlier),
            out_specs=[block, block],
        ),
        out_shape=[jax.ShapeDtypeStruct(base.shape, f32)] * 2,
        input_output_aliases={3 + group + k: k for k in range(len(earlier))},
        compiler_params=params(16),
        cost_estimate=pl.CostEstimate(
            flops=4 * base.size // split,
            bytes_accessed=18 * base.size // split,
            transcendentals=0,
        ),
        name="outputs",
    )(place, base, accumulated, *sums, *earlier)


def shards(
    hier,
    row,
    state,
    prev_slope,
    accumulated,
    hamiltonian,
    couple_v,
    coupling,
    damping,
    occupation,
    parents,
    children,
):
    ops, _, rows, columns = state.shape
    modes = occupation.shape[1]
    group = hier // 2
    width = columns // group
    split = pieces
    height = rows // split
    table = index_rows(hier * ops, modes)
    links, sides = coupled_to(table), smaller_class(table)

    hier_at, row_at = lax.axis_index("hier"), lax.axis_index("row")
    own = hier_at % group
    own_place, row_place = own.reshape(1).astype(jnp.int32), row_at.reshape(1).astype(jnp.int32)

    bits = row_bits(row)
    top, low = bits[0], bits[1:]

    def spread(p):
        return [swap(chunks[p][b], "hier", hier, b) for b in range(1, group)]

    def partial(p):
        return make_partial([owns[p], *got[p]], places, coupling, heres[p], vcols, links, sides)

    def coupled(p):
        return make_coupled([owns[p], *got[p]], received[p], places, coupling, heres[p], vcols, links, sides)

    def gather_back(done):
        return [done[0]] + [swap(done[b], "hier", hier, b) for b in range(1, group)]

    got, sent, received, sums, outs = [], [], [], [], []

    half = [occupation] + [swap(occupation, "hier", hier, b) for b in range(1, group)]
    half_at = (row_at // (row // 2)).reshape(1).astype(jnp.int32)
    half_columns, first, *first_chunks = make_section(
        0, split, state, prev_slope, own_place, half_at, group, hamiltonian
    )
    owns = [first_chunks[0]]
    half_columns, first, first_chunks, half, state, prev_slope, couple_v, hamiltonian = tie(
        (half_columns, first, first_chunks, half, state, prev_slope, couple_v, hamiltonian)
    )

    h_top = swap(half_columns, "row", row, top)
    second, *second_chunks = make_section(
        1, split, state, prev_slope, own_place, half_at, group
    )
    owns.append(second_chunks[0])
    chunks, sections = [first_chunks, second_chunks], [first, second]
    got.append(spread(0))

    known = jnp.asarray(np.array(table, np.int32))
    found = jnp.concatenate(half, axis=0)
    same = jnp.all(found[None, :, :] == known[:, None, :], axis=2)
    spot = jnp.arange(group * ops, dtype=jnp.int32)[None, :]
    places = jnp.min(jnp.where(same, spot, group * ops), axis=1).astype(jnp.int32)
    vrows = lax.dynamic_slice_in_dim(couple_v, row_at * rows, rows, 1)[:, :, None]
    vcols = lax.dynamic_slice_in_dim(couple_v, own * width, width, 1)
    heres = [vrows[:, p * height : (p + 1) * height] for p in range(split)]
    decay = jnp.sum(half[0].astype(f32) * damping[None, :], axis=1)
    got, chunks, sections, places, heres, vcols, decay, h_top, kept = tie(
        (got, chunks, sections, places, heres, vcols, decay, h_top, hamiltonian)
    )

    sent.append(partial(0))
    received.append(swap(sent[0], "hier", hier, group))
    got.append(spread(1))
    across = swap(sections[0], "row", row, top)
    near = jnp.concatenate([sections[0].reshape(-1, columns), kept.reshape(-1, columns)])
    blocks = kept.reshape(2, rows, row, split, height)
    h_columns = [blocks[:, :, :, p].reshape(2, rows, row * height) for p in range(split)]
    got, received, across, sections, h_top, near, h_columns = tie(
        (got, received, across, sections, h_top, near, h_columns)
    )

    sent.append(partial(1))
    received.append(swap(sent[1], "hier", hier, group))
    last_across = swap(sections[1], "row", row, top)
    near, s_far, h_far = tree(near, row, low), tree(across, row, low), tree(h_top, row, low)
    done, near, s_far, h_far = tie((coupled(0), near, s_far, h_far))
    sums.append(gather_back(done))
    base = make_right(sections, hamiltonian, near[1:], h_far, row_place, decay)
    base = make_left([sections[0], *near[1:], *s_far], h_columns[0], base, row_place)
    received, last_across, base = tie((received, last_across, base))

    done, sums, last_across, last_own = tie((coupled(1), sums, last_across, sections[1]))
    sums.append(gather_back(done))
    s_parts = tree(last_own, row, low) + tree(last_across, row, low)
    base = make_left(s_parts, h_columns[1], base, row_place)
    for p in range(split):
        outs = make_final(p, split, base, accumulated, sums[p], own_place, outs)
    slope, total = outs
    return slope, total


def solution(mesh):
    return jax.shard_map(
        functools.partial(shards, mesh.shape["hier"], mesh.shape["row"]),
        mesh=mesh,
        in_specs=(
            P("hier", None, "row", None),
            P("hier", None, "row", None),
            P("hier", None, "row", None),
            P(None, "row", None),
            P(),
            P(),
            P(),
            P("hier", None),
            P("hier", None),
            P("hier", None),
        ),
        out_specs=(P("hier", None, "row", None), P("hier", None, "row", None)),
        check_vma=False,
    )
```

```python
import functools

import jax
import jax.numpy as jnp
import numpy as np
from jax import lax
from jax.experimental import pallas as pl
from jax.experimental.pallas import tpu as pltpu
from jax.sharding import PartitionSpec as P

step_size = 0.5
highest_total = 4
row_tile = 16
pieces = 2
MIB = 1024 * 1024
f32 = jnp.float32
bf16 = jnp.bfloat16


def index_rows(slots, modes):
    entries = [()]
    for _ in range(modes):
        entries = [
            entry + (level,)
            for entry in entries
            for level in range(highest_total + 1)
            if sum(entry) + level <= highest_total
        ]
    return sorted(entries, key=lambda entry: (sum(entry), entry))[:slots]


def coupled_to(rows):
    lookup = {entry: place for place, entry in enumerate(rows)}
    result = []
    for entry in rows:
        terms = []
        for mode, level in enumerate(entry):
            raised = entry[:mode] + (level + 1,) + entry[mode + 1 :]
            if raised in lookup:
                terms.append((lookup[raised], mode, True, 1))
            if level > 0:
                lowered = entry[:mode] + (level - 1,) + entry[mode + 1 :]
                terms.append((lookup[lowered], mode, False, level))
        result.append(terms)
    return result


def smaller_class(rows):
    classes = [[c for c, entry in enumerate(rows) if sum(entry) % 2 == rest] for rest in (0, 1)]
    return min(classes, key=len)


def params(megabytes):
    return pltpu.CompilerParams(vmem_limit_bytes=megabytes * MIB)


def whole():
    return pl.BlockSpec(memory_space=pltpu.VMEM)


def anywhere():
    return pl.BlockSpec(memory_space=pl.ANY)


def scalars():
    return pl.BlockSpec(memory_space=pltpu.SMEM)


def swap(array, axis, size, bit):
    return lax.ppermute(array, axis, [(i, i ^ bit) for i in range(size)])


def tie(arrays):
    return lax.optimization_barrier(arrays)


def row_bits(size):
    return [1 << i for i in reversed(range(size.bit_length() - 1))]


def tree(array, size, bits):
    parts = {0: array}
    for bit in bits:
        for mask in list(parts):
            parts[mask ^ bit] = swap(parts[mask], "row", size, bit)
    return [parts[mask] for mask in sorted(parts)]


def section_kernel(group, where, _, state, slope, *refs):
    extra, section, chunks = refs[: -group - 1], refs[-group - 1], refs[-group:]
    value = (state[...].astype(f32) + (0.5 * step_size) * slope[...]).astype(bf16)
    section[...] = value
    width = chunks[0].shape[-1]
    for b, chunk in enumerate(chunks):
        columns = pl.ds(pl.multiple_of((where[0] ^ b) * width, 128), width)
        chunk[...] = section[:, :, :, columns]
    if extra:
        source, target = extra

        @pl.when(pl.program_id(0) == 0)
        def _():
            target[...] = source[...]


def make_section(p, split, state, prev_slope, place, half_at, group, hamiltonian=None):
    ops, parts, rows, columns = state.shape
    height, width = rows // split, columns // group
    block = pl.BlockSpec((1, parts, height, columns), lambda a, *_: (a, 0, p, 0))
    out = pl.BlockSpec((1, parts, height, columns), lambda a, *_: (a, 0, 0, 0))
    chunk = pl.BlockSpec((1, parts, height, width), lambda a, *_: (a, 0, 0, 0))
    half = (2, rows, columns // 2)
    extra = [] if hamiltonian is None else [hamiltonian]
    return pl.pallas_call(
        functools.partial(section_kernel, group),
        grid_spec=pltpu.PrefetchScalarGridSpec(
            num_scalar_prefetch=2,
            grid=(ops,),
            in_specs=[block, block] + [pl.BlockSpec(half, lambda a, _, h: (0, 0, h[0])) for _ in extra],
            out_specs=[pl.BlockSpec(half, lambda a, *_: (0, 0, 0)) for _ in extra]
            + [out]
            + [chunk] * group,
        ),
        out_shape=[jax.ShapeDtypeStruct(half, bf16) for _ in extra]
        + [jax.ShapeDtypeStruct((ops, parts, height, columns), bf16)]
        + [jax.ShapeDtypeStruct((ops, parts, height, width), bf16)] * group,
        compiler_params=params(60 if p == 0 else 16),
        cost_estimate=pl.CostEstimate(flops=1, bytes_accessed=1, transcendentals=0),
        name="section",
    )(place, half_at, state, prev_slope, *extra)


def fill_factors(vrows, vcols, coupling, factors):
    modes = vrows.shape[0]
    for k in range(modes):
        first = vrows[k]
        second = vcols[k : k + 1, :]
        diff = first - second
        factors[k] = diff
        factors[modes + k] = coupling[0, k] * diff
        factors[2 * modes + k] = coupling[1, k] * (first + second)


def add_terms(terms, places, held, factors, modes, rows, real, imag):
    for other, mode, child, count in terms:
        place = places[other]
        x_real = held[place, 0, rows, :].astype(f32)
        x_imag = held[place, 1, rows, :].astype(f32)
        if child:
            diff = factors[mode, rows, :]
            real = real + diff * x_imag
            imag = imag - diff * x_real
        else:
            first = factors[modes + mode, rows, :]
            second = factors[2 * modes + mode, rows, :]
            if count != 1:
                first, second = count * first, count * second
            real = real + (first * x_imag + second * x_real)
            imag = imag + (second * x_imag - first * x_real)
    return real, imag


def partial_kernel(links, sides, group, places, coupling, vrows, vcols, *refs):
    chunks, out, held, factors, sem = refs[:group], *refs[group:]
    modes = vrows.shape[0]
    height, width = held.shape[2:]
    ops = chunks[0].shape[0]
    empty = group * ops
    load = pltpu.make_async_copy(chunks[0], held.at[pl.ds(0, ops)], sem)
    load.start()
    fill_factors(vrows, vcols, coupling, factors)
    for b in range(1, group):
        held[b * ops : (b + 1) * ops] = chunks[b][...]
    held[empty] = jnp.zeros(held.shape[1:], bf16)
    load.wait()
    for u, c in enumerate(sides):

        @pl.when(places[c] < empty)
        def _():
            out[u] = held[places[c]]

        @pl.when(places[c] == empty)
        def _():
            @pl.loop(0, height // row_tile, unroll=2)
            def _(i):
                rows = pl.ds(pl.multiple_of(i * row_tile, row_tile), row_tile)
                zero = jnp.zeros((row_tile, width), f32)
                real, imag = add_terms(links[c], places, held, factors, modes, rows, zero, zero)
                out[u, 0, rows, :] = real.astype(bf16)
                out[u, 1, rows, :] = imag.astype(bf16)


def coupled_kernel(links, sides, group, places, coupling, vrows, vcols, *refs):
    chunks, received, outs = refs[:group], refs[group], refs[group + 1 : 2 * group + 1]
    held, done, factors, spots, sem = refs[2 * group + 1 :]
    modes = vrows.shape[0]
    height, width = held.shape[2:]
    ops = chunks[0].shape[0]
    empty = group * ops
    load = pltpu.make_async_copy(chunks[0], held.at[pl.ds(0, ops)], sem)
    load.start()
    fill_factors(vrows, vcols, coupling, factors)
    for b in range(1, group):
        held[b * ops : (b + 1) * ops] = chunks[b][...]
    held[empty] = jnp.zeros(held.shape[1:], bf16)
    held[empty + 1 :] = received[...]
    load.wait()
    for c in range(len(links)):
        spots[c] = places[c]
    for u, c in enumerate(sides):
        spots[c] = jnp.where(places[c] == empty, empty + 1 + u, places[c])
    for c in range(len(links)):

        @pl.when(places[c] < empty)
        def _():
            @pl.loop(0, height // row_tile, unroll=2)
            def _(i):
                rows = pl.ds(pl.multiple_of(i * row_tile, row_tile), row_tile)
                if c in sides:
                    u = empty + 1 + sides.index(c)
                    real, imag = held[u, 0, rows, :].astype(f32), held[u, 1, rows, :].astype(f32)
                else:
                    real = imag = jnp.zeros((row_tile, width), f32)
                real, imag = add_terms(links[c], spots, held, factors, modes, rows, real, imag)
                done[places[c], 0, rows, :] = real.astype(bf16)
                done[places[c], 1, rows, :] = imag.astype(bf16)

    for b, out in enumerate(outs):
        out[...] = done[b * ops : (b + 1) * ops]


def coupling_scratch(entries, height, width, modes):
    return [pltpu.VMEM((entries, 2, height, width), bf16)], [pltpu.VMEM((3 * modes, height, width), f32)]


def make_partial(chunks, places, coupling, vrows, vcols, links, sides):
    group = len(chunks)
    ops, _, height, width = chunks[0].shape
    held, factors = coupling_scratch(group * ops + 1, height, width, vrows.shape[0])
    size = height * width
    return pl.pallas_call(
        functools.partial(partial_kernel, links, sides, group),
        in_specs=[scalars(), scalars(), whole(), whole(), anywhere()] + [whole()] * (group - 1),
        out_specs=whole(),
        out_shape=jax.ShapeDtypeStruct((len(sides), 2, height, width), bf16),
        scratch_shapes=held + factors + [pltpu.SemaphoreType.DMA],
        compiler_params=params(12),
        cost_estimate=pl.CostEstimate(
            flops=40 * len(sides) * size,
            bytes_accessed=4 * size * (group * ops + len(sides)),
            transcendentals=0,
        ),
        name="partial_sums",
    )(places, coupling, vrows, vcols, *chunks)


def make_coupled(chunks, received, places, coupling, vrows, vcols, links, sides):
    group = len(chunks)
    ops, _, height, width = chunks[0].shape
    held, factors = coupling_scratch(group * ops + 1 + len(sides), height, width, vrows.shape[0])
    size = height * width
    return pl.pallas_call(
        functools.partial(coupled_kernel, links, sides, group),
        in_specs=[scalars(), scalars(), whole(), whole(), anywhere()] + [whole()] * group,
        out_specs=[whole()] * group,
        out_shape=[jax.ShapeDtypeStruct(chunks[0].shape, bf16)] * group,
        scratch_shapes=held
        + [pltpu.VMEM((group * ops, 2, height, width), bf16)]
        + factors
        + [pltpu.SMEM((len(links),), jnp.int32), pltpu.SemaphoreType.DMA],
        compiler_params=params(16),
        cost_estimate=pl.CostEstimate(flops=1, bytes_accessed=1, transcendentals=0),
        name="coupling_sums",
    )(places, coupling, vrows, vcols, *chunks, received)


def complex_rows(left, right):
    _, height, depth = left.shape
    left = left.reshape(2 * height, depth)
    first = jnp.dot(left, right[0], preferred_element_type=f32)
    second = jnp.dot(left, right[1], preferred_element_type=f32)
    return first[:height] - second[height:], second[:height] + first[height:]


def right_kernel(split, count, where, decay, h_own, *refs):
    sections, refs, (out, h_all) = refs[:split], refs[split:-2], refs[-2:]
    h_near, h_far = refs[: 2 * count - 2], refs[2 * count - 2 :]
    j, a = pl.program_id(0), pl.program_id(1)
    rows, size = h_own.shape[1:]
    height, tile = sections[0].shape[2], out.shape[3]
    half, block = size // 2, size // 4
    own = pl.multiple_of((where[0] // count) * half, half)
    other = pl.multiple_of(half - own, half)

    @pl.when(jnp.logical_and(j == 0, a == 0))
    def _():
        for b in range(count):
            place = pl.multiple_of((where[0] ^ b) * rows, row_tile)
            for x in range(2):
                near = h_near[2 * b - 2 + x][...] if b else h_own[x]
                h_all[x, pl.ds(place, rows), :] = near
            place = pl.multiple_of((where[0] ^ (count + b)) * rows, row_tile)
            h_all[:, pl.ds(place, rows), pl.ds(other, half)] = h_far[b][...]
        for r in range(0, half, block):
            for c in range(0, half, block):
                here = pl.ds(pl.multiple_of(own + r, block), block)
                there = pl.ds(pl.multiple_of(other + c, block), block)
                h_all[0, there, here] = h_all[0, here, there].T
                h_all[1, there, here] = -h_all[1, here, there].T

    columns = pl.ds(pl.multiple_of(j * tile, 128), tile)
    lost = decay[a]
    for p, section in enumerate(sections):
        real, imag = complex_rows(section[a], h_all.at[:, :, columns])
        here = slice(p * height, (p + 1) * height)
        out[0, 0, here, :] = -imag - lost * section[a, 0, :, columns].astype(f32)
        out[0, 1, here, :] = real - lost * section[a, 1, :, columns].astype(f32)


def make_right(sections, h_own, bundles, h_far, place, decay):
    ops, _, height, columns = sections[0].shape
    split, count = len(sections), len(h_far)
    rows, tile = height * split, min(columns, 512)
    held = pl.BlockSpec((ops, 2, height, columns), lambda j, a: (0, 0, 0, 0))
    return pl.pallas_call(
        functools.partial(right_kernel, split, count),
        grid=(columns // tile, ops),
        in_specs=[scalars(), scalars(), pl.BlockSpec(h_own.shape, lambda j, a: (0, 0, 0))]
        + [held] * split
        + [pl.BlockSpec((rows, columns), lambda j, a, x=x: (ops + x, 0)) for x in range(2)]
        * len(bundles)
        + [pl.BlockSpec(h.shape, lambda j, a: (0, 0, 0)) for h in h_far],
        out_specs=pl.BlockSpec((1, 2, rows, tile), lambda j, a: (a, 0, 0, j)),
        out_shape=jax.ShapeDtypeStruct((ops, 2, rows, columns), f32),
        scratch_shapes=[pltpu.VMEM((2, columns, columns), bf16)],
        compiler_params=params(28),
        cost_estimate=pl.CostEstimate(
            flops=8 * ops * rows * columns * columns,
            bytes_accessed=4 * columns * (columns + 3 * ops * rows),
            transcendentals=0,
        ),
        name="right_products",
    )(place, decay, h_own, *sections, *[h for h in bundles for _ in range(2)], *h_far)


def left_kernel(count, where, h_own, base, *refs):
    s_parts, (out, s_all) = refs[:count], refs[count:]
    height, tile = s_parts[0].shape[2:]
    for b in range(count):
        place = pl.ds(pl.multiple_of((where[0] ^ b) * height, row_tile), height)
        s_all[:, place, :] = s_parts[b][...].reshape(2, height, tile)
    real, imag = complex_rows(h_own[...], s_all)
    out[0, 0] = base[0, 0] + imag
    out[0, 1] = base[0, 1] - real


def make_left(s_parts, h_columns, base, place):
    ops, _, height, columns = s_parts[0].shape
    count, rows, tile = len(s_parts), base.shape[2], min(columns, 512)
    block = pl.BlockSpec((1, 2, rows, tile), lambda j, a: (a, 0, 0, j))
    return pl.pallas_call(
        functools.partial(left_kernel, count),
        grid=(columns // tile, ops),
        in_specs=[
            scalars(),
            pl.BlockSpec(h_columns.shape, lambda j, a: (0, 0, 0)),
            block,
        ]
        + [
            pl.BlockSpec((1, 2, height, tile), lambda j, a: (a, 0, 0, j))
            if part.ndim == 4
            else pl.BlockSpec((2 * height, tile), lambda j, a: (a, j))
            for part in s_parts
        ],
        out_specs=block,
        out_shape=jax.ShapeDtypeStruct(base.shape, f32),
        scratch_shapes=[pltpu.VMEM((2, count * height, tile), bf16)],
        compiler_params=params(16),
        cost_estimate=pl.CostEstimate(
            flops=8 * ops * rows * columns * count * height,
            bytes_accessed=4 * ops * columns * (count * height + 4 * rows),
            transcendentals=0,
        ),
        name="left_products",
    )(place, h_columns, base, *s_parts)


def final_kernel(group, where, base, accumulated, *refs):
    sums, (slope, total) = refs[:group], refs[-2:]
    j = pl.program_id(1)
    tile, width = slope.shape[3], sums[0].shape[3]
    for b in range(group):
        first = (where[0] ^ b) * width - j * tile

        @pl.when(jnp.logical_and(first >= 0, first < tile))
        def _():
            columns = pl.ds(pl.multiple_of(first, 128), width)
            value = base[0, :, :, columns] + sums[b][0].astype(f32)
            slope[0, :, :, columns] = value
            total[0, :, :, columns] = accumulated[0, :, :, columns] + (step_size / 3.0) * value


def make_final(p, split, base, accumulated, sums, place, earlier=()):
    ops, parts, rows, columns = base.shape
    group = len(sums)
    height, width, tile = rows // split, sums[0].shape[3], min(columns, 512)
    block = pl.BlockSpec((1, parts, height, tile), lambda a, j, _: (a, 0, p, j))
    chunk = pl.BlockSpec((1, parts, height, width), lambda a, j, _: (a, 0, 0, 0))
    return pl.pallas_call(
        functools.partial(final_kernel, group),
        grid_spec=pltpu.PrefetchScalarGridSpec(
            num_scalar_prefetch=1,
            grid=(ops, columns // tile),
            in_specs=[block, block] + [chunk] * group + [anywhere()] * len(earlier),
            out_specs=[block, block],
        ),
        out_shape=[jax.ShapeDtypeStruct(base.shape, f32)] * 2,
        input_output_aliases={3 + group + k: k for k in range(len(earlier))},
        compiler_params=params(16),
        cost_estimate=pl.CostEstimate(
            flops=4 * base.size // split,
            bytes_accessed=18 * base.size // split,
            transcendentals=0,
        ),
        name="outputs",
    )(place, base, accumulated, *sums, *earlier)


def shards(
    hier,
    row,
    state,
    prev_slope,
    accumulated,
    hamiltonian,
    couple_v,
    coupling,
    damping,
    occupation,
    parents,
    children,
):
    ops, _, rows, columns = state.shape
    modes = occupation.shape[1]
    group = hier // 2
    width = columns // group
    split = pieces
    height = rows // split
    table = index_rows(hier * ops, modes)
    links, sides = coupled_to(table), smaller_class(table)

    hier_at, row_at = lax.axis_index("hier"), lax.axis_index("row")
    own = hier_at % group
    own_place, row_place = own.reshape(1).astype(jnp.int32), row_at.reshape(1).astype(jnp.int32)

    bits = row_bits(row)
    top, low = bits[0], bits[1:]

    def spread(p):
        return [swap(chunks[p][b], "hier", hier, b) for b in range(1, group)]

    def partial(p):
        return make_partial([owns[p], *got[p]], places, coupling, heres[p], vcols, links, sides)

    def coupled(p):
        return make_coupled([owns[p], *got[p]], received[p], places, coupling, heres[p], vcols, links, sides)

    def gather_back(done):
        return [done[0]] + [swap(done[b], "hier", hier, b) for b in range(1, group)]

    got, sent, received, sums, outs = [], [], [], [], []

    half = [occupation] + [swap(occupation, "hier", hier, b) for b in range(1, group)]
    half_at = (row_at // (row // 2)).reshape(1).astype(jnp.int32)
    half_columns, first, *first_chunks = make_section(
        0, split, state, prev_slope, own_place, half_at, group, hamiltonian
    )
    owns = [first_chunks[0]]
    half_columns, first, first_chunks, half, state, prev_slope, couple_v, hamiltonian = tie(
        (half_columns, first, first_chunks, half, state, prev_slope, couple_v, hamiltonian)
    )

    h_top = [swap(half_columns[x : x + 1], "row", row, top) for x in range(2)]
    second, *second_chunks = make_section(
        1, split, state, prev_slope, own_place, half_at, group
    )
    owns.append(second_chunks[0])
    chunks, sections = [first_chunks, second_chunks], [first, second]
    got.append(spread(0))

    known = jnp.asarray(np.array(table, np.int32))
    found = jnp.concatenate(half, axis=0)
    same = jnp.all(found[None, :, :] == known[:, None, :], axis=2)
    spot = jnp.arange(group * ops, dtype=jnp.int32)[None, :]
    places = jnp.min(jnp.where(same, spot, group * ops), axis=1).astype(jnp.int32)
    vrows = lax.dynamic_slice_in_dim(couple_v, row_at * rows, rows, 1)[:, :, None]
    vcols = lax.dynamic_slice_in_dim(couple_v, own * width, width, 1)
    heres = [vrows[:, p * height : (p + 1) * height] for p in range(split)]
    decay = jnp.sum(half[0].astype(f32) * damping[None, :], axis=1)
    got, chunks, sections, places, heres, vcols, decay, h_top, kept = tie(
        (got, chunks, sections, places, heres, vcols, decay, h_top, hamiltonian)
    )

    sent.append(partial(0))
    received.append(swap(sent[0], "hier", hier, group))
    got.append(spread(1))
    across = swap(sections[0], "row", row, top)
    h_top = jnp.concatenate(h_top)
    near = jnp.concatenate([sections[0].reshape(-1, columns), kept.reshape(-1, columns)])
    blocks = kept.reshape(2, rows, row, split, height)
    h_columns = [blocks[:, :, :, p].reshape(2, rows, row * height) for p in range(split)]
    got, received, across, sections, h_top, near, h_columns = tie(
        (got, received, across, sections, h_top, near, h_columns)
    )

    sent.append(partial(1))
    received.append(swap(sent[1], "hier", hier, group))
    last_across = swap(sections[1], "row", row, top)
    near, s_far, h_far = tree(near, row, low), tree(across, row, low), tree(h_top, row, low)
    done, near, s_far, h_far = tie((coupled(0), near, s_far, h_far))
    sums.append(gather_back(done))
    base = make_right(sections, hamiltonian, near[1:], h_far, row_place, decay)
    base = make_left([sections[0], *near[1:], *s_far], h_columns[0], base, row_place)
    received, last_across, base = tie((received, last_across, base))

    done, sums, last_across, last_own = tie((coupled(1), sums, last_across, sections[1]))
    sums.append(gather_back(done))
    s_parts = tree(last_own, row, low) + tree(last_across, row, low)
    base = make_left(s_parts, h_columns[1], base, row_place)
    for p in range(split):
        outs = make_final(p, split, base, accumulated, sums[p], own_place, outs)
    slope, total = outs
    return slope, total


def solution(mesh):
    return jax.shard_map(
        functools.partial(shards, mesh.shape["hier"], mesh.shape["row"]),
        mesh=mesh,
        in_specs=(
            P("hier", None, "row", None),
            P("hier", None, "row", None),
            P("hier", None, "row", None),
            P(None, "row", None),
            P(),
            P(),
            P(),
            P("hier", None),
            P("hier", None),
            P("hier", None),
        ),
        out_specs=(P("hier", None, "row", None), P("hier", None, "row", None)),
        check_vma=False,
    )
```
